32 devices in a mesh: seq: 16 (over z, x, core), rep: 2 (over y).
Axes of the slice: x: 2, y: 2, z: 4, core: 2. Of those that a mesh axis runs over, the one named last changes fastest.
Arguments:
- acts: bfloat16 [8192, 6144], P(('seq', 'rep')), may hold values from -6 to 6
- grad_logits: bfloat16 [8192, 128], P(('seq', 'rep')), may hold values from -0.017944336 to 0.017944336
- master: float32 [6144, 128], P('seq'), may hold values from -0.078125 to 0.078125
- moment_one: float32 [6144, 128], P('seq'), may hold values from -3 to 3
- moment_two: float32 [6144, 128], P('seq'), may hold values from 0.05 to 2
- step_count: int32 [1], replicated, may hold values from 1 to 40
Outputs:
- master_new: float32 [6144, 128], P('seq')
- moment_one_new: float32 [6144, 128], P('seq')
- moment_two_new: float32 [6144, 128], P('seq')
- logits_new: bfloat16 [8192, 128], P(('seq', 'rep'))
The draws below stay inside these ranges and needn't reach their ends.
All inputs are finite; a program needn't handle non-finite values.
Results may differ from the reference program's by a relative error of at most 0.0024.
The reference program's roundings to bfloat16 on the way count: a program that leaves them out, or rounds other values in their place, can miss the bound.
Values may be sent and summed in bfloat16 or wider, within the bound.
No kernel may reach another device: no remote copies, remote signals or barrier semaphores. Data moves between devices by JAX's collectives and lax.ppermute only.
A program may use at most 64 MiB of HBM per device.

```python
import math
import jax
import jax.numpy as jnp
from jax import lax

D = 6144
E = 128
TOK_DEV = 256
TOKENS = 8192
N_SEQ = 16
N_REP = 2


def raised(result, stream_key, source, target, blocks, factor):
    owner, partner = [(jnp.arange(result.shape[position]) // (result.shape[position] // blocks)).reshape([-1 if axis == position else 1 for axis in range(result.ndim)]) for position in (source, target)]
    chosen = jax.random.permutation(stream_key, blocks)[partner]
    strong = (owner == chosen) | (owner == (partner + blocks // 2) % blocks)
    return jnp.where(strong, factor * result, result)


def levels(key, dims, pieces, least, top_value):
    def one(position, blocks):
        heights = jax.random.uniform(jax.random.fold_in(jax.random.fold_in(key, 6), position), (blocks,), jnp.float32, least / len(pieces), top_value / len(pieces))
        return jnp.repeat(jnp.exp(heights), dims[position] // blocks).reshape((-1,) + (1,) * (len(dims) - position - 1))

    level = one(*pieces[0])
    for cut in pieces[1:]:
        level = level * one(*cut)
    return level


def gaussian(rng, shape, deviation, most, pieces=(), held_as=jnp.bfloat16):
    factor_of = levels(rng, shape, pieces, -0.22, 0.18) if pieces else 1.0
    entries = jax.random.normal(rng, shape, jnp.float32) * deviation * factor_of
    return jnp.minimum(jnp.maximum(entries, -most), most).astype(held_as)


def gaussian_with(own_key, shape, width, reach, pieces, heavy, held_as=jnp.bfloat16):
    drawn = width * jax.random.normal(own_key, shape, jnp.float32)
    if pieces:
        drawn = drawn * levels(own_key, shape, pieces, -0.22, 0.18)
    return jnp.clip(raised(drawn, jax.random.fold_in(own_key, 3), *heavy), -reach, reach).astype(held_as)


def setup_inputs(seed: int = 0) -> dict:
    key_of = jax.random.split(jax.random.key(seed), 7)
    return {
        "acts": gaussian_with(key_of[0], (TOKENS, D), 1.0, 6.0, ((0, 32),), (0, 1, 32, 2.75)),
        "grad_logits": gaussian(key_of[1], (TOKENS, E), 0.003, 0.017944336, ((0, 32),)),
        "master": gaussian(key_of[2], (D, E), D ** -0.5, 0.078125, ((0, 16),), jnp.float32),
        "moment_one": gaussian(key_of[3], (D, E), 0.5, 3.0, ((0, 16),), jnp.float32),
        "moment_two": jnp.clip(jnp.exp(math.log(2.0) - 3.6888794 * jax.random.uniform(key_of[4], (D, E), jnp.float32) ** levels(key_of[4], (D, E), ((0, 16),), -0.2, 0.2)), 0.05, 2.0),
        "step_count": jax.random.randint(key_of[5], (1,), 1, 41).astype(jnp.int32),
    }


def reference(acts, grad_logits, master, moment_one, moment_two, step_count):
    blocks = N_SEQ * N_REP
    act_blocks = acts.reshape(blocks, TOK_DEV, D)
    grad_blocks = grad_logits.reshape(blocks, TOK_DEV, E)

    def accumulate(total, pair):
        piece = lax.dot_general(pair[0], pair[1], (((0,), (0,)), ((), ())), preferred_element_type=jnp.float32)
        rounded = lax.optimization_barrier(piece.astype(jnp.bfloat16))
        return (total + rounded.astype(jnp.float32), None)
    grad, _ = lax.scan(accumulate, jnp.zeros((D, E), jnp.float32), (act_blocks, grad_blocks))
    count = step_count[0].astype(jnp.float32)
    beta_one = 0.9
    beta_two = 0.95
    first = beta_one * moment_one + (1.0 - beta_one) * grad
    second = beta_two * moment_two + (1.0 - beta_two) * grad * grad
    first_hat = first / (1.0 - jnp.power(beta_one, count))
    second_hat = second / (1.0 - jnp.power(beta_two, count))
    updated = master - 0.01 * (first_hat / (jnp.sqrt(second_hat) + 1e-08) + 0.1 * master)
    weight_new = updated.astype(jnp.bfloat16)
    logits = jnp.dot(acts, weight_new, preferred_element_type=jnp.float32).astype(jnp.bfloat16)
    return (updated, first, second, logits)
```

```python
import jax
import jax.numpy as jnp
from jax import lax
from jax.experimental import pallas as pl
from jax.experimental.pallas import tpu as pltpu
from jax.sharding import PartitionSpec as P

AXES = ("seq", "rep")


def adamw(grad, master, moment_one, moment_two, step_count):
    count = step_count[0].astype(jnp.float32)
    beta_one = 0.9
    beta_two = 0.95
    first = beta_one * moment_one + (1.0 - beta_one) * grad
    second = beta_two * moment_two + (1.0 - beta_two) * grad * grad
    first_hat = first / (1.0 - jnp.power(beta_one, count))
    second_hat = second / (1.0 - jnp.power(beta_two, count))
    updated = master - 0.01 * (first_hat / (jnp.sqrt(second_hat) + 1e-08) + 0.1 * master)
    return updated, first, second


def logits_kernel(places, half, acts_ref, *refs):
    me_ref, pieces, out_ref, weight = refs[0], refs[1:-2], refs[-2], refs[-1]
    me = me_ref[0]
    for piece, masks in zip(pieces, places):
        for j, mask in enumerate(masks):
            row = pl.multiple_of(jnp.bitwise_xor(me, mask) * half, half)
            weight[pl.ds(row, half), :] = piece[j]
    out_ref[...] = jnp.dot(
        acts_ref[...], weight[...], preferred_element_type=jnp.float32
    ).astype(out_ref.dtype)


def solution(mesh):
    n_seq, n_rep = mesh.shape["seq"], mesh.shape["rep"]
    devices = n_seq * n_rep
    core = n_rep
    low = [a * 2 * n_rep + b for a in range(4) for b in range(n_rep)]
    high = [8 * n_rep * j for j in range(n_seq // 8)]

    def swap(x, mask):
        return lax.ppermute(x, AXES, [(i, i ^ mask) for i in range(devices)])

    def per_device(acts, grad_logits, master, moment_one, moment_two, step_count):
        rows, experts = master.shape
        half = rows // n_rep
        seq, rep = lax.axis_index("seq"), lax.axis_index("rep")
        me = seq * n_rep + rep
        my_core, my_low = seq % 2, (seq // 2) % 4
        my_high = seq // 8

        product = lax.dot_general(
            acts, grad_logits, (((0,), (0,)), ((), ())), preferred_element_type=jnp.float32
        ).astype(jnp.bfloat16)
        by_core = product.reshape(n_seq // 2, 2, rows, experts)
        away = lax.dynamic_index_in_dim(by_core, 1 - my_core, 1, keepdims=False)
        kept = lax.dynamic_index_in_dim(by_core, my_core, 1, keepdims=False)
        arrived = swap(away, core)
        chip = (kept.astype(jnp.float32) + arrived.astype(jnp.float32)).astype(jnp.bfloat16)
        chip = chip.reshape(len(high), 4, n_rep, half, experts)

        total = None
        for mask in low:
            other_low = jnp.bitwise_xor(my_low, mask // (2 * n_rep))
            other_rep = jnp.bitwise_xor(rep, mask % n_rep)
            part = lax.dynamic_slice(
                chip, (0, other_low, other_rep, 0, 0), (len(high), 1, 1, half, experts)
            ).reshape(len(high), half, experts)
            if mask:
                part = swap(part, mask)
            part = part.astype(jnp.float32)
            total = part if total is None else total + part

        grad = None
        for j, mask in enumerate(high):
            part = lax.dynamic_index_in_dim(total, jnp.bitwise_xor(my_high, j), 0, keepdims=False)
            if mask:
                part = swap(part, mask)
            grad = part if grad is None else grad + part

        mine = [
            lax.dynamic_slice_in_dim(a, rep * half, half, 0)
            for a in (master, moment_one, moment_two)
        ]
        weight = adamw(grad, *mine, step_count)[0].astype(jnp.bfloat16)

        other = swap(grad, 1)
        whole = jnp.where(
            rep == 0,
            jnp.concatenate([grad, other], 0),
            jnp.concatenate([other, grad], 0),
        )
        updated, first, second = adamw(whole, master, moment_one, moment_two, step_count)

        column = jnp.stack([swap(weight, mask) if mask else weight for mask in high])
        cube = [swap(column, mask) if mask else column for mask in low]
        pair = [swap(piece, core) for piece in cube]
        pieces = cube + pair
        places = [[m ^ h for h in high] for m in low] + [[m ^ core ^ h for h in high] for m in low]
        if half % 16 == 0:
            vmem = pl.BlockSpec(memory_space=pltpu.VMEM)
            logits = pl.pallas_call(
                lambda *refs: logits_kernel(places, half, *refs),
                out_shape=jax.ShapeDtypeStruct((acts.shape[0], experts), jnp.bfloat16),
                in_specs=[vmem, pl.BlockSpec(memory_space=pltpu.SMEM)] + [vmem] * len(pieces),
                out_specs=vmem,
                scratch_shapes=[pltpu.VMEM((n_seq * rows, experts), jnp.bfloat16)],
                compiler_params=pltpu.CompilerParams(vmem_limit_bytes=32 * 2**20),
            )(acts, me.reshape(1), *pieces)
        else:
            order = jnp.argsort(jnp.bitwise_xor(me, jnp.array(places).reshape(-1)))
            full = jnp.concatenate(pieces)[order].reshape(n_seq * rows, experts)
            logits = jnp.dot(acts, full, preferred_element_type=jnp.float32).astype(jnp.bfloat16)
        return updated, first, second, logits

    rows_of, tokens = P("seq", None), P(AXES, None)
    return jax.shard_map(
        per_device,
        mesh=mesh,
        in_specs=(tokens, tokens, rows_of, rows_of, rows_of, P()),
        out_specs=(rows_of, rows_of, rows_of, tokens),
        check_vma=False,
    )
```

```python
import jax
import jax.numpy as jnp
from jax import lax
from jax.experimental import pallas as pl
from jax.experimental.pallas import tpu as pltpu
from jax.sharding import Mesh
from jax.sharding import PartitionSpec as P

CUBE = ("low", "rep")


def adamw(grad, master, moment_one, moment_two, step_count):
    count = step_count[0].astype(jnp.float32)
    beta_one = 0.9
    beta_two = 0.95
    first = beta_one * moment_one + (1.0 - beta_one) * grad
    second = beta_two * moment_two + (1.0 - beta_two) * grad * grad
    first_hat = first / (1.0 - jnp.power(beta_one, count))
    second_hat = second / (1.0 - jnp.power(beta_two, count))
    updated = master - 0.01 * (first_hat / (jnp.sqrt(second_hat) + 1e-08) + 0.1 * master)
    return updated, first, second


def logits_kernel(n_rep, half, where_ref, acts_ref, own_ref, other_ref, out_ref, weight):
    my_high, my_core = where_ref[0], where_ref[1]
    cube, highs = own_ref.shape[:2]
    for piece, core in ((own_ref, my_core), (other_ref, 1 - my_core)):
        for k in range(cube):
            for j in range(highs):
                owner = (jnp.bitwise_xor(my_high, j) * (cube // n_rep) + k // n_rep) * 2 + core
                row = pl.multiple_of((owner * n_rep + k % n_rep) * half, half)
                weight[pl.ds(row, half), :] = piece[k, j]
    out_ref[...] = jnp.dot(
        acts_ref[...], weight[...], preferred_element_type=jnp.float32
    ).astype(out_ref.dtype)


def solution(mesh):
    n_seq, n_rep = mesh.shape["seq"], mesh.shape["rep"]
    n_low = 4
    n_high = n_seq // (2 * n_low)
    cube = n_low * n_rep
    fine = Mesh(
        mesh.devices.reshape(n_high, n_low, 2, n_rep), ("high", "low", "core", "rep")
    )

    def swap(x, axis, mask=1):
        return lax.ppermute(x, axis, [(i, i ^ mask) for i in range(fine.shape[axis])])

    def per_device(acts, grad_logits, master, moment_one, moment_two, step_count):
        rows, experts = master.shape
        half = rows // n_rep
        rep = lax.axis_index("rep")
        my_core, my_high = lax.axis_index("core"), lax.axis_index("high")

        product = lax.dot_general(
            acts, grad_logits, (((0,), (0,)), ((), ())), preferred_element_type=jnp.float32
        ).astype(jnp.bfloat16)
        by_core = product.reshape(n_seq // 2, 2, rows, experts)
        away = lax.dynamic_index_in_dim(by_core, 1 - my_core, 1, keepdims=False)
        kept = lax.dynamic_index_in_dim(by_core, my_core, 1, keepdims=False)
        arrived = swap(away, "core")
        chip = (kept.astype(jnp.float32) + arrived.astype(jnp.float32)).astype(jnp.bfloat16)
        chip = chip.reshape(n_high, cube, half, experts).transpose(1, 0, 2, 3)
        parts = lax.all_to_all(chip, CUBE, 0, 0, tiled=True)
        total = jnp.sum(parts.astype(jnp.float32), axis=0)

        grad = None
        for j in range(n_high):
            part = lax.dynamic_index_in_dim(total, jnp.bitwise_xor(my_high, j), 0, keepdims=False)
            if j:
                part = swap(part, "high", j)
            grad = part if grad is None else grad + part

        mine = [
            lax.dynamic_slice_in_dim(a, rep * half, half, 0)
            for a in (master, moment_one, moment_two)
        ]
        weight = adamw(grad, *mine, step_count)[0].astype(jnp.bfloat16)

        other = swap(grad, "rep")
        whole = jnp.where(
            rep == 0,
            jnp.concatenate([grad, other], 0),
            jnp.concatenate([other, grad], 0),
        )
        updated, first, second = adamw(whole, master, moment_one, moment_two, step_count)

        column = jnp.stack([swap(weight, "high", j) if j else weight for j in range(n_high)])
        column = jnp.broadcast_to(column, (cube, n_high, half, experts))
        own = lax.all_to_all(column, CUBE, 0, 0, tiled=True)
        across = swap(own, "core")
        if half % 16 == 0:
            vmem = pl.BlockSpec(memory_space=pltpu.VMEM)
            logits = pl.pallas_call(
                lambda *refs: logits_kernel(n_rep, half, *refs),
                out_shape=jax.ShapeDtypeStruct((acts.shape[0], experts), jnp.bfloat16),
                in_specs=[pl.BlockSpec(memory_space=pltpu.SMEM)] + [vmem] * 3,
                out_specs=vmem,
                scratch_shapes=[pltpu.VMEM((n_seq * rows, experts), jnp.bfloat16)],
                compiler_params=pltpu.CompilerParams(vmem_limit_bytes=32 * 2**20),
            )(jnp.stack([my_high, my_core]), acts, own, across)
        else:
            both = jnp.where(my_core == 0, jnp.stack([own, across]), jnp.stack([across, own]))
            both = both[:, :, jnp.bitwise_xor(my_high, jnp.arange(n_high))]
            full = both.reshape(2, n_low, n_rep, n_high, half, experts).transpose(3, 1, 0, 2, 4, 5)
            full = full.reshape(n_seq * rows, experts)
            logits = jnp.dot(acts, full, preferred_element_type=jnp.float32).astype(jnp.bfloat16)
        return updated, first, second, logits

    rows_of, tokens = P(("high", "low", "core"), None), P(("high", "low", "core", "rep"), None)
    return jax.shard_map(
        per_device,
        mesh=fine,
        in_specs=(tokens, tokens, rows_of, rows_of, rows_of, P()),
        out_specs=(rows_of, rows_of, rows_of, tokens),
        check_vma=False,
    )
```

```python
import jax
import jax.numpy as jnp
from jax import lax
from jax.experimental import pallas as pl
from jax.experimental.pallas import tpu as pltpu
from jax.sharding import Mesh
from jax.sharding import PartitionSpec as P

AXES = ("high", "low", "core", "rep")
N_LOW = 4


def parity(n):
    return (n ^ (n >> 1)) & 1


def adamw(grad, master, moment_one, moment_two, step_count):
    count = step_count[0].astype(jnp.float32)
    beta_one = 0.9
    beta_two = 0.95
    first = beta_one * moment_one + (1.0 - beta_one) * grad
    second = beta_two * moment_two + (1.0 - beta_two) * grad * grad
    first_hat = first / (1.0 - jnp.power(beta_one, count))
    second_hat = second / (1.0 - jnp.power(beta_two, count))
    updated = master - 0.01 * (first_hat / (jnp.sqrt(second_hat) + 1e-08) + 0.1 * master)
    return updated, first, second


def block_row(where, chip, c, j):
    high, low, core, rep = where
    k, flip, by_core = chip
    rep = rep ^ flip ^ core if by_core else rep ^ flip
    return (((high ^ j) * N_LOW + (low ^ k)) * 2 + c) * 2 + rep


def logits_kernel(half, chips, where_ref, acts_ref, *refs):
    pieces, out_ref, weight = refs[:-2], refs[-2], refs[-1]
    where = [where_ref[i] for i in range(4)]
    for piece, chip in zip(pieces, chips):
        for c in range(piece.shape[0]):
            for j in range(piece.shape[1]):
                row = pl.multiple_of(block_row(where, chip, c, j) * half, half)
                weight[pl.ds(row, half), :] = piece[c, j]
    out_ref[...] = jnp.dot(
        acts_ref[...], weight[...], preferred_element_type=jnp.float32
    ).astype(out_ref.dtype)


def solution(mesh):
    n_seq, n_rep = mesh.shape["seq"], mesh.shape["rep"]
    n_high = n_seq // (2 * N_LOW)
    fine = Mesh(mesh.devices.reshape(n_high, N_LOW, 2, n_rep), AXES)

    def swap(x, axis, mask=1):
        return lax.ppermute(x, axis, [(i, i ^ mask) for i in range(fine.shape[axis])])

    def to_partner(x, k):
        axes = ("low", "core", "rep")
        pairs = []
        for low in range(N_LOW):
            for c in range(2):
                for r in range(n_rep):
                    flip = parity(k) ^ c
                    if k or flip:
                        there = ((low ^ k) * 2 + c) * n_rep + (r ^ flip)
                        pairs.append(((low * 2 + c) * n_rep + r, there))
        return lax.ppermute(x, axes, pairs)

    def per_device(acts, grad_logits, master, moment_one, moment_two, step_count):
        rows, experts = master.shape
        half = rows // n_rep
        high, low, core, rep = (lax.axis_index(a) for a in AXES)
        first_core = core == 0

        product = lax.dot_general(
            acts, grad_logits, (((0,), (0,)), ((), ())), preferred_element_type=jnp.float32
        ).astype(jnp.bfloat16)
        product = product.reshape(n_high, N_LOW, 2, n_rep, half, experts)

        def for_partner(k, of_core):
            chip = (0, low ^ k, 0, rep ^ parity(k) ^ of_core, 0, 0)
            block = lax.dynamic_slice(product, chip, (n_high, 1, 2, 1, half, experts))
            return block.reshape(n_high, 2, half, experts)

        away = jnp.stack([for_partner(k, 1 - core) for k in range(N_LOW)])
        arrived = swap(away, "core").astype(jnp.float32)
        total = None
        for k in range(N_LOW):
            chip = (for_partner(k, core).astype(jnp.float32) + arrived[k]).astype(jnp.bfloat16)
            part = to_partner(chip, k)
            if k == 0:
                part = jnp.where(first_core, chip, part)
            part = part.astype(jnp.float32)
            total = part if total is None else total + part

        def of_core(x, c):
            return lax.dynamic_index_in_dim(x, c, 1, keepdims=False)

        total = of_core(total, core) + swap(of_core(total, 1 - core), "core")

        grad = None
        for j in range(n_high):
            part = lax.dynamic_index_in_dim(total, high ^ j, 0, keepdims=False)
            if j:
                part = swap(part, "high", j)
            grad = part if grad is None else grad + part

        mine = [
            lax.dynamic_slice_in_dim(a, rep * half, half, 0)
            for a in (master, moment_one, moment_two)
        ]
        weight = adamw(grad, *mine, step_count)[0].astype(jnp.bfloat16)

        column = jnp.stack([swap(weight, "high", j) if j else weight for j in range(n_high)])
        other = swap(grad, "rep")
        whole = jnp.where(
            rep == 0,
            jnp.concatenate([grad, other], 0),
            jnp.concatenate([other, grad], 0),
        )
        updated, first, second = adamw(whole, master, moment_one, moment_two, step_count)

        across = swap(column, "core")
        own = jnp.where(first_core, jnp.stack([column, across]), jnp.stack([across, column]))
        got = [to_partner(own, k) for k in range(N_LOW)]
        over = [swap(piece, "core") for piece in got]
        pieces = [own, jnp.where(first_core, over[0], got[0])] + got[1:] + over[1:]
        chips = [(0, 0, False), (0, 1, False)]
        chips += [(k, parity(k), True) for k in range(1, N_LOW)]
        chips += [(k, parity(k) ^ 1, True) for k in range(1, N_LOW)]
        where = (high, low, core, rep)
        if half % 16 == 0:
            vmem = pl.BlockSpec(memory_space=pltpu.VMEM)
            logits = pl.pallas_call(
                lambda *refs: logits_kernel(half, chips, *refs),
                out_shape=jax.ShapeDtypeStruct((acts.shape[0], experts), jnp.bfloat16),
                in_specs=[pl.BlockSpec(memory_space=pltpu.SMEM)] + [vmem] * (1 + len(pieces)),
                out_specs=vmem,
                scratch_shapes=[pltpu.VMEM((n_seq * rows, experts), jnp.bfloat16)],
                compiler_params=pltpu.CompilerParams(vmem_limit_bytes=32 * 2**20),
            )(jnp.stack(where), acts, *pieces)
        else:
            blocks = jnp.stack(pieces).reshape(-1, half, experts)
            places = [
                block_row(where, chip, c, j)
                for chip in chips
                for c in range(2)
                for j in range(n_high)
            ]
            full = jnp.zeros_like(blocks).at[jnp.stack(places)].set(blocks)
            full = full.reshape(n_seq * rows, experts)
            logits = jnp.dot(acts, full, preferred_element_type=jnp.float32).astype(jnp.bfloat16)
        return updated, first, second, logits

    rows_of, tokens = P(AXES[:3], None), P(AXES, None)
    return jax.shard_map(
        per_device,
        mesh=fine,
        in_specs=(tokens, tokens, rows_of, rows_of, rows_of, P()),
        out_specs=(rows_of, rows_of, rows_of, tokens),
        check_vma=False,
    )
```

```python
import jax
import jax.numpy as jnp
from jax import lax
from jax.experimental import pallas as pl
from jax.experimental.pallas import tpu as pltpu
from jax.sharding import Mesh
from jax.sharding import PartitionSpec as P

AXES = ("high", "low", "core", "rep")
N_LOW = 4
ORDER = (((0, 1), (1, 0), (2, 0)), ((1, 0), (2, 0), (0, 1)))
STEPS = [(a, b, c) for a in range(2) for b in range(2) for c in range(2)]


def change(core, taken):
    low = rep = 0
    for step, one in zip(ORDER[core], taken):
        if one:
            low, rep = low ^ step[0], rep ^ step[1]
    return low, rep


def change_here(core, taken):
    (low0, rep0), (low1, rep1) = change(0, taken), change(1, taken)
    return low0 + core * (low1 - low0), rep0 + core * (rep1 - rep0)


def adamw(grad, master, moment_one, moment_two, step_count):
    count = step_count[0].astype(jnp.float32)
    beta_one = 0.9
    beta_two = 0.95
    first = beta_one * moment_one + (1.0 - beta_one) * grad
    second = beta_two * moment_two + (1.0 - beta_two) * grad * grad
    first_hat = first / (1.0 - jnp.power(beta_one, count))
    second_hat = second / (1.0 - jnp.power(beta_two, count))
    updated = master - 0.01 * (first_hat / (jnp.sqrt(second_hat) + 1e-08) + 0.1 * master)
    return updated, first, second


def block_row(where, taken, of_core, j):
    high, low, core, rep = where
    owner = core ^ of_core
    d_low, d_rep = change_here(owner, taken)
    return (((high ^ j) * N_LOW + (low ^ d_low)) * 2 + owner) * 2 + (rep ^ d_rep)


def logits_kernel(half, chips, where_ref, acts_ref, *refs):
    pieces, out_ref, weight = refs[:-2], refs[-2], refs[-1]
    where = [where_ref[i] for i in range(4)]
    for piece, (of_core, reached) in zip(pieces, chips):
        for i, taken in enumerate(reached):
            for j in range(piece.shape[1]):
                row = pl.multiple_of(block_row(where, taken, of_core, j) * half, half)
                weight[pl.ds(row, half), :] = piece[i, j]
    out_ref[...] = jnp.dot(
        acts_ref[...], weight[...], preferred_element_type=jnp.float32
    ).astype(out_ref.dtype)


def solution(mesh):
    n_seq, n_rep = mesh.shape["seq"], mesh.shape["rep"]
    n_high = n_seq // (2 * N_LOW)
    fine = Mesh(mesh.devices.reshape(n_high, N_LOW, 2, n_rep), AXES)

    def swap(x, axis, mask=1):
        return lax.ppermute(x, axis, [(i, i ^ mask) for i in range(fine.shape[axis])])

    def step_swap(x, step):
        pairs = []
        for low in range(N_LOW):
            for core in range(2):
                d_low, d_rep = ORDER[core][step]
                for rep in range(n_rep):
                    there = ((low ^ d_low) * 2 + core) * n_rep + (rep ^ d_rep)
                    pairs.append(((low * 2 + core) * n_rep + rep, there))
        return lax.ppermute(x, AXES[1:], pairs)

    def per_device(acts, grad_logits, master, moment_one, moment_two, step_count):
        rows, experts = master.shape
        half = rows // n_rep
        where = high, low, core, rep = tuple(lax.axis_index(a) for a in AXES)
        f32, bf16 = jnp.float32, jnp.bfloat16

        product = lax.dot_general(
            acts, grad_logits, (((0,), (0,)), ((), ())), preferred_element_type=f32
        ).astype(bf16)
        product = product.reshape(n_high, N_LOW, 2, n_rep, half, experts)

        def blocks(owner, taken):
            d_low, d_rep = change_here(owner, taken)
            at = (0, low ^ d_low, owner, rep ^ d_rep, 0, 0)
            block = lax.dynamic_slice(product, at, (n_high, 1, 1, 1, half, experts))
            return block.reshape(n_high, half, experts)

        parts = []
        for a in (1, 0):
            away = jnp.stack([blocks(1 - core, taken) for taken in STEPS if taken[0] == a])
            kept = jnp.stack([blocks(core, taken) for taken in STEPS if taken[0] == a])
            parts.append(kept.astype(f32) + swap(away, "core").astype(f32))
        total = parts[1] + step_swap(parts[0].astype(bf16), 0).astype(f32)
        total = total[:2] + step_swap(total[2:].astype(bf16), 1).astype(f32)
        total = total[0] + step_swap(total[1], 2)

        grad = None
        for j in range(n_high):
            part = lax.dynamic_index_in_dim(total, high ^ j, 0, keepdims=False)
            if j:
                part = swap(part, "high", j)
            grad = part if grad is None else grad + part

        mine = [
            lax.dynamic_slice_in_dim(a, rep * half, half, 0)
            for a in (master, moment_one, moment_two)
        ]
        weight = adamw(grad, *mine, step_count)[0].astype(bf16)

        column = jnp.stack([swap(weight, "high", j) if j else weight for j in range(n_high)])
        other = swap(grad, "rep")
        column, other = lax.optimization_barrier((column, other))
        whole = jnp.where(
            rep == 0,
            jnp.concatenate([grad, other], 0),
            jnp.concatenate([other, grad], 0),
        )
        state = adamw(whole, master, moment_one, moment_two, step_count)

        near = column[None]
        near = jnp.concatenate([near, step_swap(near, 2)])
        near = jnp.concatenate([near, step_swap(near, 1)])
        far = step_swap(near, 0)
        near_over = swap(near, "core")
        far, state = lax.optimization_barrier((far, state))
        far_over = swap(far, "core")
        pieces = [near, far, near_over, far_over]
        near_taken, far_taken = STEPS[:4], STEPS[4:]
        chips = [(0, near_taken), (0, far_taken), (1, near_taken), (1, far_taken)]
        if half % 16 == 0:
            vmem = pl.BlockSpec(memory_space=pltpu.VMEM)
            logits = pl.pallas_call(
                lambda *refs: logits_kernel(half, chips, *refs),
                out_shape=jax.ShapeDtypeStruct((acts.shape[0], experts), bf16),
                in_specs=[pl.BlockSpec(memory_space=pltpu.SMEM)] + [vmem] * (1 + len(pieces)),
                out_specs=vmem,
                scratch_shapes=[pltpu.VMEM((n_seq * rows, experts), bf16)],
                compiler_params=pltpu.CompilerParams(vmem_limit_bytes=32 * 2**20),
            )(jnp.stack(where), acts, *pieces)
        else:
            places = [
                block_row(where, taken, of_core, j)
                for of_core, reached in chips
                for taken in reached
                for j in range(n_high)
            ]
            received = jnp.concatenate(pieces).reshape(-1, half, experts)
            full = jnp.zeros_like(received).at[jnp.stack(places)].set(received)
            full = full.reshape(n_seq * rows, experts)
            logits = jnp.dot(acts, full, preferred_element_type=f32).astype(bf16)
        return *state, logits

    rows_of, tokens = P(AXES[:3], None), P(AXES, None)
    return jax.shard_map(
        per_device,
        mesh=fine,
        in_specs=(tokens, tokens, rows_of, rows_of, rows_of, P()),
        out_specs=(rows_of, rows_of, rows_of, tokens),
        check_vma=False,
    )
```

```python
import jax
import jax.numpy as jnp
from jax import lax
from jax.experimental import pallas as pl
from jax.experimental.pallas import tpu as pltpu
from jax.sharding import Mesh
from jax.sharding import PartitionSpec as P

AXES = ("high", "low", "core", "rep")
N_LOW = 4
SLOTS = (0, 3, 1, 2)


def parity(n):
    return (n ^ (n >> 1)) & 1


def adamw(grad, master, moment_one, moment_two, step_count):
    count = step_count[0].astype(jnp.float32)
    beta_one = 0.9
    beta_two = 0.95
    first = beta_one * moment_one + (1.0 - beta_one) * grad
    second = beta_two * moment_two + (1.0 - beta_two) * grad * grad
    first_hat = first / (1.0 - jnp.power(beta_one, count))
    second_hat = second / (1.0 - jnp.power(beta_two, count))
    updated = master - 0.01 * (first_hat / (jnp.sqrt(second_hat) + 1e-08) + 0.1 * master)
    return updated, first, second


def logits_kernel(half, chips, n_high, where_ref, acts_ref, *refs):
    pieces, before, out_ref, weight = refs[: len(chips)], refs[len(chips) : -2], refs[-2], refs[-1]
    high, low, _, rep = [where_ref[i] for i in range(4)]
    total = before[0][...] if before else None
    for piece, (_, flip, slot) in zip(pieces, chips):
        row = pl.multiple_of((rep ^ flip) * half, half)
        for c in range(2):
            for j in range(n_high):
                weight[slot, j, c, pl.ds(row, half), :] = piece[c, j]
    wide = 4 * half
    experts = weight.shape[-1]
    for slot, k in dict.fromkeys((slot, k) for k, _, slot in chips):
        for j in range(n_high):
            column = pl.multiple_of(((high ^ j) * N_LOW + (low ^ k)) * wide, wide)
            part = jnp.dot(
                acts_ref[:, pl.ds(column, wide)],
                weight[slot, j].reshape(wide, experts),
                preferred_element_type=jnp.float32,
            )
            total = part if total is None else total + part
    out_ref[...] = total.astype(out_ref.dtype)


def solution(mesh):
    n_seq, n_rep = mesh.shape["seq"], mesh.shape["rep"]
    n_high = n_seq // (2 * N_LOW)
    fine = Mesh(mesh.devices.reshape(n_high, N_LOW, 2, n_rep), AXES)

    def swap(x, axis, mask=1):
        return lax.ppermute(x, axis, [(i, i ^ mask) for i in range(fine.shape[axis])])

    def to_partner(x, k):
        pairs = []
        for low in range(N_LOW):
            for core in range(2):
                d_low, d_rep = k ^ (3 * core), parity(k) ^ core
                for rep in range(n_rep):
                    if d_low or d_rep:
                        there = ((low ^ d_low) * 2 + core) * n_rep + (rep ^ d_rep)
                        pairs.append(((low * 2 + core) * n_rep + rep, there))
        return lax.ppermute(x, AXES[1:], pairs)

    def per_device(acts, grad_logits, master, moment_one, moment_two, step_count):
        rows, experts = master.shape
        half = rows // n_rep
        where = high, low, core, rep = tuple(lax.axis_index(a) for a in AXES)
        first_core = core == 0
        f32, bf16 = jnp.float32, jnp.bfloat16

        product = lax.dot_general(
            acts, grad_logits, (((0,), (0,)), ((), ())), preferred_element_type=f32
        ).astype(bf16)
        product = product.reshape(n_high, N_LOW, 2, n_rep, half, experts)

        def for_partner(k, of_core):
            chip = (0, low ^ k ^ (3 * of_core), 0, rep ^ parity(k) ^ of_core, 0, 0)
            block = lax.dynamic_slice(product, chip, (n_high, 1, 2, 1, half, experts))
            return block.reshape(n_high, 2, half, experts)

        total = None
        for slots in (SLOTS[:2], SLOTS[2:]):
            away = jnp.stack([for_partner(k, 1 - core) for k in slots])
            arrived = swap(away, "core").astype(f32)
            for i, k in enumerate(slots):
                chip = (for_partner(k, core).astype(f32) + arrived[i]).astype(bf16)
                part = to_partner(chip, k)
                if k == 0:
                    part = jnp.where(first_core, chip, part)
                part = part.astype(f32)
                total = part if total is None else total + part

        def of_core(x, c):
            return lax.dynamic_index_in_dim(x, c, 1, keepdims=False)

        total = of_core(total, core) + swap(of_core(total, 1 - core), "core")

        grad = None
        for j in range(n_high):
            part = lax.dynamic_index_in_dim(total, high ^ j, 0, keepdims=False)
            if j:
                part = swap(part, "high", j)
            grad = part if grad is None else grad + part

        mine = [
            lax.dynamic_slice_in_dim(a, rep * half, half, 0)
            for a in (master, moment_one, moment_two)
        ]
        weight = adamw(grad, *mine, step_count)[0].astype(bf16)

        column = jnp.stack([swap(weight, "high", j) if j else weight for j in range(n_high)])
        other = swap(grad, "rep")
        across = swap(column, "core")
        across, other = lax.optimization_barrier((across, other))
        own = jnp.where(first_core, jnp.stack([column, across]), jnp.stack([across, column]))

        whole = jnp.where(
            rep == 0,
            jnp.concatenate([grad, other], 0),
            jnp.concatenate([other, grad], 0),
        )
        state = adamw(whole, master, moment_one, moment_two, step_count)

        got = {k: to_partner(own, k) for k in SLOTS}
        got[SLOTS[1]], state = lax.optimization_barrier((got[SLOTS[1]], state))
        over = {k: swap(got[k], "core") for k in SLOTS}

        logits = None
        for pair in (SLOTS[:2], SLOTS[2:]):
            pieces, chips = [], []
            for k in pair:
                by_core = [jnp.where(first_core, got[k], over[k]), jnp.where(first_core, over[k], got[k])]
                if k == 0:
                    by_core[0] = own
                for c in range(2):
                    d_low, d_rep = k ^ (3 * c), parity(k) ^ c
                    pieces.append(by_core[c])
                    chips.append((d_low, d_rep, 0 if d_low == pair[0] else 1))
            last = pair == SLOTS[2:]
            if half % 16 == 0:
                vmem = pl.BlockSpec(memory_space=pltpu.VMEM)
                before = [] if logits is None else [logits]
                logits = pl.pallas_call(
                    lambda *refs, chips=chips: logits_kernel(half, chips, n_high, *refs),
                    out_shape=jax.ShapeDtypeStruct((acts.shape[0], experts), bf16 if last else f32),
                    in_specs=[pl.BlockSpec(memory_space=pltpu.SMEM)]
                    + [vmem] * (1 + len(pieces) + len(before)),
                    out_specs=vmem,
                    scratch_shapes=[pltpu.VMEM((2, n_high, 2, rows, experts), bf16)],
                    compiler_params=pltpu.CompilerParams(vmem_limit_bytes=32 * 2**20),
                )(jnp.stack(where), acts, *pieces, *before)
            else:
                places = [
                    (((high ^ j) * N_LOW + (low ^ d_low)) * 2 + c) * n_rep + (rep ^ d_rep)
                    for d_low, d_rep, _ in chips
                    for c in range(2)
                    for j in range(n_high)
                ]
                received = jnp.concatenate(pieces).reshape(-1, half, experts)
                full = jnp.zeros((2 * received.shape[0], half, experts), bf16)
                full = full.at[jnp.stack(places)].set(received).reshape(n_seq * rows, experts)
                part = jnp.dot(acts, full, preferred_element_type=f32)
                logits = part if logits is None else (logits + part).astype(bf16)
        return *state, logits

    rows_of, tokens = P(AXES[:3], None), P(AXES, None)
    return jax.shard_map(
        per_device,
        mesh=fine,
        in_specs=(tokens, tokens, rows_of, rows_of, rows_of, P()),
        out_specs=(rows_of, rows_of, rows_of, tokens),
        check_vma=False,
    )
```

```python
import jax
import jax.numpy as jnp
from jax import lax
from jax.experimental import pallas as pl
from jax.experimental.pallas import tpu as pltpu
from jax.sharding import Mesh
from jax.sharding import PartitionSpec as P

AXES = ("high", "low", "core", "rep")
N_LOW = 4
SLOTS = (1, 2, 3, 0)


def parity(n):
    return (n ^ (n >> 1)) & 1


def adamw(grad, master, moment_one, moment_two, step_count):
    count = step_count[0].astype(jnp.float32)
    beta_one = 0.9
    beta_two = 0.95
    first = beta_one * moment_one + (1.0 - beta_one) * grad
    second = beta_two * moment_two + (1.0 - beta_two) * grad * grad
    first_hat = first / (1.0 - jnp.power(beta_one, count))
    second_hat = second / (1.0 - jnp.power(beta_two, count))
    updated = master - 0.01 * (first_hat / (jnp.sqrt(second_hat) + 1e-08) + 0.1 * master)
    return updated, first, second


def logits_kernel(half, pair, n_high, where_ref, acts_ref, *refs):
    pieces, before, out_ref, weight = refs[:4], refs[4:-2], refs[-2], refs[-1]
    high, low, core, rep = [where_ref[i] for i in range(4)]
    total = before[0][...] if before else None
    for i, piece in enumerate(pieces):
        k, of_core = pair[i // 2], core ^ (i % 2)
        slot = of_core ^ (i // 2)
        row = pl.multiple_of((rep ^ parity(k) ^ of_core) * half, half)
        for c in range(2):
            for j in range(n_high):
                weight[slot, j, c, pl.ds(row, half), :] = piece[c, j]
    wide = 4 * half
    experts = weight.shape[-1]
    for slot in range(2):
        for j in range(n_high):
            column = pl.multiple_of(((high ^ j) * N_LOW + (low ^ pair[slot])) * wide, wide)
            part = jnp.dot(
                acts_ref[:, pl.ds(column, wide)],
                weight[slot, j].reshape(wide, experts),
                preferred_element_type=jnp.float32,
            )
            total = part if total is None else total + part
    out_ref[...] = total.astype(out_ref.dtype)


def solution(mesh):
    n_seq, n_rep = mesh.shape["seq"], mesh.shape["rep"]
    n_high = n_seq // (2 * N_LOW)
    fine = Mesh(mesh.devices.reshape(n_high, N_LOW, 2, n_rep), AXES)

    def swap(x, axis, mask=1):
        return lax.ppermute(x, axis, [(i, i ^ mask) for i in range(fine.shape[axis])])

    def to_partner(x, k):
        pairs = []
        for low in range(N_LOW):
            for core in range(2):
                d_low, d_rep = k ^ (3 * core), parity(k) ^ core
                for rep in range(n_rep):
                    there = ((low ^ d_low) * 2 + core) * n_rep + (rep ^ d_rep)
                    pairs.append(((low * 2 + core) * n_rep + rep, there))
        return lax.ppermute(x, AXES[1:], pairs)

    def per_device(acts, grad_logits, master, moment_one, moment_two, step_count):
        rows, experts = master.shape
        half = rows // n_rep
        where = high, low, core, rep = tuple(lax.axis_index(a) for a in AXES)
        first_core = core == 0
        f32, bf16 = jnp.float32, jnp.bfloat16

        product = lax.dot_general(
            acts, grad_logits, (((0,), (0,)), ((), ())), preferred_element_type=f32
        ).astype(bf16)
        product = product.reshape(n_high, N_LOW, 2, n_rep, half, experts)

        def for_partner(k, of_core):
            chip = (0, low ^ k ^ (3 * of_core), 0, rep ^ parity(k) ^ of_core, 0, 0)
            block = lax.dynamic_slice(product, chip, (n_high, 1, 2, 1, half, experts))
            return block.reshape(n_high, 2, half, experts)

        total = None
        for slots in (SLOTS[:2], SLOTS[2:]):
            away = jnp.stack([for_partner(k, 1 - core) for k in slots])
            arrived = swap(away, "core").astype(f32)
            for i, k in enumerate(slots):
                chip = (for_partner(k, core).astype(f32) + arrived[i]).astype(bf16)
                part = to_partner(chip, k)
                part = part.astype(f32)
                total = part if total is None else total + part

        def of_core(x, c):
            return lax.dynamic_index_in_dim(x, c, 1, keepdims=False)

        total = of_core(total, core) + swap(of_core(total, 1 - core), "core")

        grad = None
        for j in range(n_high):
            part = lax.dynamic_index_in_dim(total, high ^ j, 0, keepdims=False)
            if j:
                part = swap(part, "high", j)
            grad = part if grad is None else grad + part

        mine = [
            lax.dynamic_slice_in_dim(a, rep * half, half, 0)
            for a in (master, moment_one, moment_two)
        ]
        weight = adamw(grad, *mine, step_count)[0].astype(bf16)

        column = jnp.stack([swap(weight, "high", j) if j else weight for j in range(n_high)])
        other = swap(grad, "rep")
        across = swap(column, "core")
        across, other = lax.optimization_barrier((across, other))
        own = jnp.where(first_core, jnp.stack([column, across]), jnp.stack([across, column]))

        whole = jnp.where(
            rep == 0,
            jnp.concatenate([grad, other], 0),
            jnp.concatenate([other, grad], 0),
        )
        state = adamw(whole, master, moment_one, moment_two, step_count)

        got = {k: to_partner(own, k) for k in SLOTS}
        got[SLOTS[1]], state = lax.optimization_barrier((got[SLOTS[1]], state))
        over = {k: swap(got[k], "core") for k in SLOTS}

        logits = None
        for pair in (SLOTS[:2], SLOTS[2:]):
            pieces = [x[k] for k in pair for x in (got, over)]
            last = pair == SLOTS[2:]
            if half % 16 == 0:
                vmem = pl.BlockSpec(memory_space=pltpu.VMEM)
                before = [] if logits is None else [logits]
                logits = pl.pallas_call(
                    lambda *refs, pair=pair: logits_kernel(half, pair, n_high, *refs),
                    out_shape=jax.ShapeDtypeStruct((acts.shape[0], experts), bf16 if last else f32),
                    in_specs=[pl.BlockSpec(memory_space=pltpu.SMEM)]
                    + [vmem] * (1 + len(pieces) + len(before)),
                    out_specs=vmem,
                    scratch_shapes=[pltpu.VMEM((2, n_high, 2, rows, experts), bf16)],
                    compiler_params=pltpu.CompilerParams(vmem_limit_bytes=10 * 2**20),
                )(jnp.stack(where), acts, *pieces, *before)
            else:
                places = [
                    (((high ^ j) * N_LOW + (low ^ k ^ (3 * of_core))) * 2 + c) * n_rep
                    + (rep ^ parity(k) ^ of_core)
                    for k in pair
                    for of_core in (core, 1 - core)
                    for c in range(2)
                    for j in range(n_high)
                ]
                received = jnp.concatenate(pieces).reshape(-1, half, experts)
                full = jnp.zeros((2 * received.shape[0], half, experts), bf16)
                full = full.at[jnp.stack(places)].set(received).reshape(n_seq * rows, experts)
                part = jnp.dot(acts, full, preferred_element_type=f32)
                logits = part if logits is None else (logits + part).astype(bf16)
        return *state, logits

    rows_of, tokens = P(AXES[:3], None), P(AXES, None)
    return jax.shard_map(
        per_device,
        mesh=fine,
        in_specs=(tokens, tokens, rows_of, rows_of, rows_of, P()),
        out_specs=(rows_of, rows_of, rows_of, tokens),
        check_vma=False,
    )
```

```python
import functools

import jax
import jax.numpy as jnp
from jax import lax
from jax.experimental import pallas as pl
from jax.experimental.pallas import tpu as pltpu
from jax.sharding import Mesh
from jax.sharding import PartitionSpec as P

AXES = ("high", "low", "core", "rep")
N_LOW = 4
FIRST = (1, 2)
VMEM_LIMIT = 8 * 2**20


def parity(n):
    return (n ^ (n >> 1)) & 1


def adamw(grad, master, moment_one, moment_two, step_count):
    count = step_count[0].astype(jnp.float32)
    beta_one = 0.9
    beta_two = 0.95
    first = beta_one * moment_one + (1.0 - beta_one) * grad
    second = beta_two * moment_two + (1.0 - beta_two) * grad * grad
    first_hat = first / (1.0 - jnp.power(beta_one, count))
    second_hat = second / (1.0 - jnp.power(beta_two, count))
    updated = master - 0.01 * (first_hat / (jnp.sqrt(second_hat) + 1e-08) + 0.1 * master)
    return updated, first, second


def load_columns(acts_ref, chunks, sems, high, low, n_high):
    wide = chunks.shape[-1]
    copies = []
    for p, at in enumerate(low):
        for j in range(n_high):
            column = pl.multiple_of(((high ^ j) * N_LOW + at) * wide, wide)
            n = p * n_high + j
            copy = pltpu.make_async_copy(acts_ref.at[:, pl.ds(column, wide)], chunks.at[n], sems.at[n])
            copy.start()
            copies.append(copy)
    return copies


def partial_products(copies, chunks, grad_ref, blocks):
    for n, copy in enumerate(copies):
        copy.wait()
        product = lax.dot_general(
            chunks[n], grad_ref[...], (((0,), (0,)), ((), ())), preferred_element_type=jnp.float32
        )
        blocks[...] = product.astype(blocks.dtype).reshape(blocks.shape)
        yield n


def first_grad_kernel(n_high, where_ref, acts_ref, grad_ref, away_ref, kept_ref, chunks, blocks, sems):
    _, low, core, rep = [where_ref[i] for i in range(4)]
    copies = load_columns(acts_ref, chunks, sems, 0, [low ^ k for k in FIRST], n_high)
    for n in partial_products(copies, chunks, grad_ref, blocks):
        p, j = divmod(n, n_high)
        flip = rep ^ core ^ parity(FIRST[p])
        for c in range(2):
            kept_ref[p ^ core, c, j] = blocks[c, flip]
            away_ref[p ^ core ^ 1, c, j] = blocks[c, flip ^ 1]


def second_grad_kernel(n_high, where_ref, acts_ref, grad_ref, away_ref, kept_ref, chunks, blocks, sems):
    _, low, core, rep = [where_ref[i] for i in range(4)]
    at = [low ^ (3 * (1 - core)), low ^ (3 * core)]
    copies = load_columns(acts_ref, chunks, sems, 0, at, n_high)
    for n in partial_products(copies, chunks, grad_ref, blocks):
        p, j = divmod(n, n_high)
        slot_ref = kept_ref if p == 0 else away_ref
        flip = rep ^ core ^ p
        for c in range(2):
            slot_ref[c, j] = blocks[c, flip]
        kept_ref[2 + (core ^ p), j] = blocks[core, flip ^ 1]
        away_ref[2 + (core ^ p), j] = blocks[core ^ 1, flip ^ 1]


def logits_kernel(n_high, lows, place, where_ref, acts_ref, *refs):
    *pieces, out_ref, chunks, weight, sems = refs
    before = None
    if len(pieces[-1].shape) == 2:
        *pieces, before = pieces
    high, low, core, rep = [where_ref[i] for i in range(4)]
    copies = load_columns(acts_ref, chunks, sems, high, [low ^ k for k in lows], n_high)
    half, experts = weight.shape[-2:]
    for i, piece in enumerate(pieces):
        for b, (slot, owner, of_rep) in enumerate(place(core, rep, i)):
            for j in range(n_high):
                weight[slot, j, owner, of_rep] = piece[b, j]
    total = None if before is None else before[...]
    for n, copy in enumerate(copies):
        slot, j = divmod(n, n_high)
        copy.wait()
        part = jnp.dot(
            chunks[n],
            weight[slot, j].reshape(4 * half, experts),
            preferred_element_type=jnp.float32,
        )
        total = part if total is None else total + part
    out_ref[...] = total.astype(out_ref.dtype)


def first_place(core, rep, i):
    k, of_core = FIRST[i // 2], core ^ (i % 2)
    return [(of_core ^ (i // 2), c, rep ^ parity(k) ^ of_core) for c in range(2)]


def second_place(core, rep, i):
    if i < 2:
        of_core = core ^ i
        return [(of_core, c, rep ^ of_core) for c in range(2)]
    owner = core ^ (i % 2)
    return [(0, owner, rep ^ 1)] if i < 4 else [(1, owner, rep)]


def solution(mesh):
    n_seq, n_rep = mesh.shape["seq"], mesh.shape["rep"]
    n_high = n_seq // (2 * N_LOW)
    fine = Mesh(mesh.devices.reshape(n_high, N_LOW, 2, n_rep), AXES)

    def swap(x, axis, mask=1):
        return lax.ppermute(x, axis, [(i, i ^ mask) for i in range(fine.shape[axis])])

    def cube_swap(x, change):
        pairs = []
        for low in range(N_LOW):
            for core in range(2):
                d_low, d_rep = change(core)
                for rep in range(n_rep):
                    there = ((low ^ d_low) * 2 + core) * n_rep + (rep ^ d_rep)
                    pairs.append(((low * 2 + core) * n_rep + rep, there))
        return lax.ppermute(x, AXES[1:], pairs)

    def to_partner(x, k):
        return cube_swap(x, lambda core: (k ^ (3 * core), parity(k) ^ core))

    def to_corner(x):
        return cube_swap(x, lambda core: (3, 1))

    def per_device(acts, grad_logits, master, moment_one, moment_two, step_count):
        tokens, experts = grad_logits.shape
        rows = master.shape[0]
        half = rows // n_rep
        high, low, core, rep = (lax.axis_index(a) for a in AXES)
        where = jnp.stack([high, low, core, rep])
        first_core = core == 0
        f32, bf16 = jnp.float32, jnp.bfloat16
        in_kernels = half % 16 == 0 and (4 * half) % 128 == 0

        smem = pl.BlockSpec(memory_space=pltpu.SMEM)
        vmem = pl.BlockSpec(memory_space=pltpu.VMEM)
        anywhere = pl.BlockSpec(memory_space=pl.ANY)
        chunks = [
            pltpu.VMEM((2 * n_high, tokens, 4 * half), bf16),
            pltpu.VMEM((2, 2, half, experts), bf16),
            pltpu.SemaphoreType.DMA((2 * n_high,)),
        ]
        params = pltpu.CompilerParams(vmem_limit_bytes=VMEM_LIMIT)

        if in_kernels:
            acts = pltpu.with_memory_space_constraint(acts, pltpu.HBM)

            def products(kernel, blocks, grad_logits):
                shape = pltpu.VMEM((*blocks, n_high, half, experts), bf16)
                return pl.pallas_call(
                    functools.partial(kernel, n_high),
                    out_shape=(shape, shape),
                    in_specs=[smem, anywhere, vmem],
                    out_specs=(vmem, vmem),
                    scratch_shapes=chunks,
                    compiler_params=params,
                )(where, acts, grad_logits)

            away_first, kept_first = products(first_grad_kernel, (2, 2), grad_logits)
            away_first, later = lax.optimization_barrier((away_first, grad_logits))
            away_second, kept_second = products(second_grad_kernel, (4,), later)
        else:
            product = lax.dot_general(
                acts, grad_logits, (((0,), (0,)), ((), ())), preferred_element_type=f32
            ).astype(bf16)
            product = product.reshape(n_high, N_LOW, 2, n_rep, half, experts)

            def block(d_low, owner, d_rep):
                at = (0, low ^ d_low, owner, rep ^ d_rep, 0, 0)
                part = lax.dynamic_slice(product, at, (n_high, 1, 1, 1, half, experts))
                return part.reshape(n_high, half, experts)

            def slot(k, of_core):
                change = k ^ (3 * of_core), parity(k) ^ of_core
                return [block(change[0], c, change[1]) for c in range(2)]

            def both(of_core):
                first = jnp.stack([jnp.stack(slot(k, of_core)) for k in FIRST])
                rest = [block(3, of_core, 1), block(0, of_core, 0)]
                return first, jnp.stack(slot(3, of_core) + rest)

            away_first, away_second = both(1 - core)
            kept_first, kept_second = both(core)

        summed = kept_first.astype(f32) + swap(away_first, "core").astype(f32)
        parts = [to_partner(summed[i].astype(bf16), k) for i, k in enumerate(FIRST)]
        summed = kept_second.astype(f32) + swap(away_second, "core").astype(f32)
        parts.append(to_partner(summed[:2].astype(bf16), 3))
        parts.append(to_corner(summed[2].astype(bf16)))
        *parts, corner = [x.astype(f32) for x in lax.optimization_barrier(parts)]
        total = sum(parts)

        def of_core(x, c):
            return lax.dynamic_index_in_dim(x, c, 0, keepdims=False)

        total = of_core(total, core) + swap(of_core(total, 1 - core), "core") + summed[3] + corner

        grad = None
        for j in range(n_high):
            part = lax.dynamic_index_in_dim(total, high ^ j, 0, keepdims=False)
            if j:
                part = swap(part, "high", j)
            grad = part if grad is None else grad + part

        mine = [
            lax.dynamic_slice_in_dim(a, rep * half, half, 0)
            for a in (master, moment_one, moment_two)
        ]
        weight = adamw(grad, *mine, step_count)[0].astype(bf16)

        column = jnp.stack([swap(weight, "high", j) if j else weight for j in range(n_high)])
        other = swap(grad, "rep")
        across = swap(column, "core")
        across, other = lax.optimization_barrier((across, other))
        chip = jnp.where(first_core, jnp.stack([column, across]), jnp.stack([across, column]))

        whole = jnp.where(
            rep == 0,
            jnp.concatenate([grad, other], 0),
            jnp.concatenate([other, grad], 0),
        )
        state = adamw(whole, master, moment_one, moment_two, step_count)

        got = [to_partner(chip, k) for k in (*FIRST, 3)]
        corner = to_corner(column)
        got[0], state = lax.optimization_barrier((got[0], state))
        got[2], corner = lax.optimization_barrier((got[2], corner))
        over = [swap(x, "core") for x in got]
        corner_over = swap(corner, "core")

        first = [x[i] for i in range(2) for x in (got, over)]
        second = [got[2], over[2], corner[None], corner_over[None], column[None], across[None]]
        stages = ((FIRST, first_place, first), ((3, 0), second_place, second))
        logits = None
        for lows, place, pieces in stages:
            if in_kernels:
                before = [] if logits is None else [logits]
                operands = [
                    pltpu.with_memory_space_constraint(x, pltpu.VMEM) for x in pieces + before
                ]
                logits = pl.pallas_call(
                    functools.partial(logits_kernel, n_high, lows, place),
                    out_shape=jax.ShapeDtypeStruct((tokens, experts), bf16 if before else f32),
                    in_specs=[smem, anywhere] + [vmem] * len(operands),
                    out_specs=vmem,
                    scratch_shapes=[
                        chunks[0],
                        pltpu.VMEM((2, n_high, 2, 2, half, experts), bf16),
                        chunks[2],
                    ],
                    compiler_params=params,
                )(where, acts, *operands)
            else:
                at = jnp.array(lows)
                places = jnp.stack(
                    [
                        (((high ^ j) * N_LOW + (low ^ at[which])) * 2 + owner) * n_rep + of_rep
                        for i in range(len(pieces))
                        for which, owner, of_rep in place(core, rep, i)
                        for j in range(n_high)
                    ]
                )
                received = jnp.concatenate(pieces).reshape(-1, half, experts)
                full = jnp.zeros((2 * received.shape[0], half, experts), bf16)
                full = full.at[places].set(received).reshape(n_seq * rows, experts)
                part = jnp.dot(acts, full, preferred_element_type=f32)
                logits = part if logits is None else (logits + part).astype(bf16)
        return *state, logits

    rows_of, tokens_of = P(AXES[:3], None), P(AXES, None)
    return jax.shard_map(
        per_device,
        mesh=fine,
        in_specs=(tokens_of, tokens_of, rows_of, rows_of, rows_of, P()),
        out_specs=(rows_of, rows_of, rows_of, tokens_of),
        check_vma=False,
    )
```

```python
import functools

import jax
import jax.numpy as jnp
from jax import lax
from jax.experimental import pallas as pl
from jax.experimental.pallas import tpu as pltpu
from jax.sharding import Mesh
from jax.sharding import PartitionSpec as P

AXES = ("high", "low", "core", "rep")
N_LOW = 4
FIRST = (1, 2)
VMEM_LIMIT = 8 * 2**20


def parity(n):
    return (n ^ (n >> 1)) & 1


def adamw(grad, master, moment_one, moment_two, step_count):
    count = step_count[0].astype(jnp.float32)
    beta_one = 0.9
    beta_two = 0.95
    first = beta_one * moment_one + (1.0 - beta_one) * grad
    second = beta_two * moment_two + (1.0 - beta_two) * grad * grad
    first_hat = first / (1.0 - jnp.power(beta_one, count))
    second_hat = second / (1.0 - jnp.power(beta_two, count))
    updated = master - 0.01 * (first_hat / (jnp.sqrt(second_hat) + 1e-08) + 0.1 * master)
    return updated, first, second


def load_columns(acts_ref, chunks, sems, high, low, n_high):
    wide = chunks.shape[-1]
    copies = []
    for p, at in enumerate(low):
        for j in range(n_high):
            column = pl.multiple_of(((high ^ j) * N_LOW + at) * wide, wide)
            n = p * n_high + j
            copy = pltpu.make_async_copy(acts_ref.at[:, pl.ds(column, wide)], chunks.at[n], sems.at[n])
            copy.start()
            copies.append(copy)
    return copies


def grad_kernel(n_high, where_ref, acts_ref, grad_ref, *refs):
    state_refs, refs = refs[:3], refs[3:]
    away_first, kept_first, away_second, kept_second, mine_ref, chunks, logit_grads, blocks, sems = refs
    _, low, core, rep = [where_ref[i] for i in range(4)]
    half = blocks.shape[2]
    last = sems.shape[0]
    loads = pltpu.make_async_copy(grad_ref, logit_grads, sems.at[last - 1])
    loads.start()
    at = [low ^ k for k in FIRST] + [low ^ (3 * (1 - core)), low ^ (3 * core)]
    copies = load_columns(acts_ref, chunks, sems, 0, at, n_high)
    rows = pl.ds(pl.multiple_of(rep * half, half), half)
    state = [
        pltpu.make_async_copy(ref.at[rows], mine_ref.at[i], sems.at[last - 4 + i])
        for i, ref in enumerate(state_refs)
    ]
    for copy in state:
        copy.start()
    loads.wait()
    for n, copy in enumerate(copies):
        copy.wait()
        product = lax.dot_general(
            chunks[n], logit_grads[...], (((0,), (0,)), ((), ())), preferred_element_type=jnp.float32
        )
        blocks[...] = product.astype(blocks.dtype).reshape(blocks.shape)
        p, j = divmod(n, n_high)
        if p < 2:
            flip = rep ^ core ^ parity(FIRST[p])
            for c in range(2):
                kept_first[p ^ core, c, j] = blocks[c, flip]
                away_first[p ^ core ^ 1, c, j] = blocks[c, flip ^ 1]
        else:
            p = p - 2
            slot = kept_second if p == 0 else away_second
            flip = rep ^ core ^ p
            for c in range(2):
                slot[c, j] = blocks[c, flip]
            kept_second[2 + (core ^ p), j] = blocks[core, flip ^ 1]
            away_second[2 + (core ^ p), j] = blocks[core ^ 1, flip ^ 1]
    for copy in state:
        copy.wait()


def columns_kernel(n_high, where_ref, acts_ref, first_ref, second_ref, sems):
    high, low = where_ref[0], where_ref[1]
    copies = []
    for i, (lows, out) in enumerate(((FIRST, first_ref), ((3, 0), second_ref))):
        copies += load_columns(acts_ref, out, sems.at[i], high, [low ^ k for k in lows], n_high)
    for copy in copies:
        copy.wait()


def logits_kernel(n_high, place, where_ref, columns_ref, *refs):
    *pieces, out_ref, weight = refs
    before = None
    if len(pieces[-1].shape) == 2:
        *pieces, before = pieces
    core, rep = where_ref[2], where_ref[3]
    half, experts = weight.shape[-2:]
    for i, piece in enumerate(pieces):
        for b, (chip, owner, of_rep) in enumerate(place(core, rep, i)):
            for j in range(n_high):
                weight[chip, j, owner, of_rep] = piece[b, j]
    total = None if before is None else before[...]
    for n in range(2 * n_high):
        part = jnp.dot(
            columns_ref[n],
            weight[n // n_high, n % n_high].reshape(4 * half, experts),
            preferred_element_type=jnp.float32,
        )
        total = part if total is None else total + part
    out_ref[...] = total.astype(out_ref.dtype)


def first_place(core, rep, i):
    k, of_core = FIRST[i // 2], core ^ (i % 2)
    return [(of_core ^ (i // 2), c, rep ^ parity(k) ^ of_core) for c in range(2)]


def second_place(core, rep, i):
    if i < 2:
        of_core = core ^ i
        return [(of_core, c, rep ^ of_core) for c in range(2)]
    owner = core ^ (i % 2)
    return [(0, owner, rep ^ 1)] if i < 4 else [(1, owner, rep)]


def solution(mesh):
    n_seq, n_rep = mesh.shape["seq"], mesh.shape["rep"]
    n_high = n_seq // (2 * N_LOW)
    fine = Mesh(mesh.devices.reshape(n_high, N_LOW, 2, n_rep), AXES)

    def swap(x, axis, mask=1):
        return lax.ppermute(x, axis, [(i, i ^ mask) for i in range(fine.shape[axis])])

    def cube_swap(x, change):
        pairs = []
        for low in range(N_LOW):
            for core in range(2):
                d_low, d_rep = change(core)
                for rep in range(n_rep):
                    there = ((low ^ d_low) * 2 + core) * n_rep + (rep ^ d_rep)
                    pairs.append(((low * 2 + core) * n_rep + rep, there))
        return lax.ppermute(x, AXES[1:], pairs)

    def to_partner(x, k):
        return cube_swap(x, lambda core: (k ^ (3 * core), parity(k) ^ core))

    def to_corner(x):
        return cube_swap(x, lambda core: (3, 1))

    def per_device(acts, grad_logits, master, moment_one, moment_two, step_count):
        tokens, experts = grad_logits.shape
        rows = master.shape[0]
        half = rows // n_rep
        high, low, core, rep = (lax.axis_index(a) for a in AXES)
        where = jnp.stack([high, low, core, rep])
        first_core = core == 0
        f32, bf16 = jnp.float32, jnp.bfloat16
        in_kernels = half % 16 == 0 and (4 * half) % 128 == 0

        smem = pl.BlockSpec(memory_space=pltpu.SMEM)
        vmem = pl.BlockSpec(memory_space=pltpu.VMEM)
        anywhere = pl.BlockSpec(memory_space=pl.ANY)
        params = pltpu.CompilerParams(vmem_limit_bytes=VMEM_LIMIT)
        state_in = (master, moment_one, moment_two)

        if in_kernels:
            acts = pltpu.with_memory_space_constraint(acts, pltpu.HBM)
            first_shape = pltpu.VMEM((2, 2, n_high, half, experts), bf16)
            second_shape = pltpu.VMEM((4, n_high, half, experts), bf16)
            away_first, kept_first, away_second, kept_second, mine = pl.pallas_call(
                functools.partial(grad_kernel, n_high),
                out_shape=(first_shape, first_shape, second_shape, second_shape)
                + (pltpu.VMEM((3, half, experts), f32),),
                in_specs=[smem] + [anywhere] * 5,
                out_specs=(vmem,) * 5,
                scratch_shapes=[
                    pltpu.VMEM((4 * n_high, tokens, 4 * half), bf16),
                    pltpu.VMEM((tokens, experts), bf16),
                    pltpu.VMEM((2, 2, half, experts), bf16),
                    pltpu.SemaphoreType.DMA((4 * n_high + 4,)),
                ],
                compiler_params=params,
            )(
                where,
                acts,
                *(pltpu.with_memory_space_constraint(x, pltpu.HBM) for x in (grad_logits, *state_in)),
            )
        else:
            product = lax.dot_general(
                acts, grad_logits, (((0,), (0,)), ((), ())), preferred_element_type=f32
            ).astype(bf16)
            product = product.reshape(n_high, N_LOW, 2, n_rep, half, experts)

            def block(d_low, owner, d_rep):
                at = (0, low ^ d_low, owner, rep ^ d_rep, 0, 0)
                part = lax.dynamic_slice(product, at, (n_high, 1, 1, 1, half, experts))
                return part.reshape(n_high, half, experts)

            def slot(k, of_core):
                change = k ^ (3 * of_core), parity(k) ^ of_core
                return [block(change[0], c, change[1]) for c in range(2)]

            def both(of_core):
                first = jnp.stack([jnp.stack(slot(k, of_core)) for k in FIRST])
                rest = [block(3, of_core, 1), block(0, of_core, 0)]
                return first, jnp.stack(slot(3, of_core) + rest)

            away_first, away_second = both(1 - core)
            kept_first, kept_second = both(core)
            mine = jnp.stack([lax.dynamic_slice_in_dim(x, rep * half, half, 0) for x in state_in])

        summed = kept_first.astype(f32) + swap(away_first, "core").astype(f32)
        parts = [to_partner(summed[i].astype(bf16), k) for i, k in enumerate(FIRST)]
        summed = kept_second.astype(f32) + swap(away_second, "core").astype(f32)
        parts.append(to_partner(summed[:2].astype(bf16), 3))
        parts.append(to_corner(summed[2].astype(bf16)))
        *parts, corner = [x.astype(f32) for x in lax.optimization_barrier(parts)]
        total = sum(parts)

        def of_core(x, c):
            return lax.dynamic_index_in_dim(x, c, 0, keepdims=False)

        total = of_core(total, core) + swap(of_core(total, 1 - core), "core") + summed[3] + corner

        grad = None
        for j in range(n_high):
            part = lax.dynamic_index_in_dim(total, high ^ j, 0, keepdims=False)
            if j:
                part = swap(part.astype(bf16), "high", j).astype(f32)
            grad = part if grad is None else grad + part
        weight = adamw(grad, *mine, step_count)[0].astype(bf16)

        column = jnp.stack([swap(weight, "high", j) if j else weight for j in range(n_high)])
        other = swap(grad, "rep")
        across = swap(column, "core")
        across, other = lax.optimization_barrier((across, other))
        chip = jnp.where(first_core, jnp.stack([column, across]), jnp.stack([across, column]))

        whole = jnp.where(
            rep == 0,
            jnp.concatenate([grad, other], 0),
            jnp.concatenate([other, grad], 0),
        )
        state = adamw(whole, *state_in, step_count)

        got = [to_partner(chip, k) for k in (*FIRST, 3)]
        corner = to_corner(column)
        columns = [None, None]
        if in_kernels:
            state, late_acts = lax.optimization_barrier((state, acts))
            columns = pl.pallas_call(
                functools.partial(columns_kernel, n_high),
                out_shape=(pltpu.VMEM((2 * n_high, tokens, 4 * half), bf16),) * 2,
                in_specs=[smem, anywhere],
                out_specs=(vmem, vmem),
                scratch_shapes=[pltpu.SemaphoreType.DMA((2, 2 * n_high))],
                compiler_params=params,
            )(where, pltpu.with_memory_space_constraint(late_acts, pltpu.HBM))
        got[0], state, columns = lax.optimization_barrier((got[0], state, columns))
        got[2], corner = lax.optimization_barrier((got[2], corner))
        over = [swap(x, "core") for x in got]
        corner_over = swap(corner, "core")

        first = [x[i] for i in range(2) for x in (got, over)]
        second = [got[2], over[2], corner[None], corner_over[None], column[None], across[None]]
        stages = ((FIRST, first_place, first), ((3, 0), second_place, second))
        logits = None
        for (lows, place, pieces), acts_columns in zip(stages, columns):
            if in_kernels:
                before = [] if logits is None else [logits]
                operands = [
                    pltpu.with_memory_space_constraint(x, pltpu.VMEM) for x in [acts_columns] + pieces + before
                ]
                logits = pl.pallas_call(
                    functools.partial(logits_kernel, n_high, place),
                    out_shape=jax.ShapeDtypeStruct((tokens, experts), bf16 if before else f32),
                    in_specs=[smem] + [vmem] * len(operands),
                    out_specs=vmem,
                    scratch_shapes=[pltpu.VMEM((2, n_high, 2, 2, half, experts), bf16)],
                    compiler_params=params,
                )(where, *operands)
            else:
                at = jnp.array(lows)
                places = jnp.stack(
                    [
                        (((high ^ j) * N_LOW + (low ^ at[which])) * 2 + owner) * n_rep + of_rep
                        for i in range(len(pieces))
                        for which, owner, of_rep in place(core, rep, i)
                        for j in range(n_high)
                    ]
                )
                received = jnp.concatenate(pieces).reshape(-1, half, experts)
                full = jnp.zeros((2 * received.shape[0], half, experts), bf16)
                full = full.at[places].set(received).reshape(n_seq * rows, experts)
                part = jnp.dot(acts, full, preferred_element_type=f32)
                logits = part if logits is None else (logits + part).astype(bf16)
        return *state, logits

    rows_of, tokens_of = P(AXES[:3], None), P(AXES, None)
    return jax.shard_map(
        per_device,
        mesh=fine,
        in_specs=(tokens_of, tokens_of, rows_of, rows_of, rows_of, P()),
        out_specs=(rows_of, rows_of, rows_of, tokens_of),
        check_vma=False,
    )
```

```python
import functools

import jax
import jax.numpy as jnp
from jax import lax
from jax.experimental import pallas as pl
from jax.experimental.pallas import tpu as pltpu
from jax.sharding import Mesh
from jax.sharding import PartitionSpec as P

AXES = ("high", "low", "core", "rep")
N_LOW = 4
FIRST = (1, 2)
VMEM_LIMIT = 8 * 2**20


def parity(n):
    return (n ^ (n >> 1)) & 1


def adamw(grad, master, moment_one, moment_two, step_count):
    count = step_count[0].astype(jnp.float32)
    beta_one = 0.9
    beta_two = 0.95
    first = beta_one * moment_one + (1.0 - beta_one) * grad
    second = beta_two * moment_two + (1.0 - beta_two) * grad * grad
    first_hat = first / (1.0 - jnp.power(beta_one, count))
    second_hat = second / (1.0 - jnp.power(beta_two, count))
    updated = master - 0.01 * (first_hat / (jnp.sqrt(second_hat) + 1e-08) + 0.1 * master)
    return updated, first, second


def near_places(core, n_high):
    return [(k, 0) for k in FIRST] + [(k, j) for k in (3 * (1 - core), 3 * core) for j in range(n_high)]


def far_places(n_high):
    return [(k, j) for k in FIRST for j in range(1, n_high)]


def load_columns(acts_ref, columns, sems, first_sem, high, low, places):
    wide = columns.shape[-1]
    copies = []
    for n, (k, j) in enumerate(places):
        column = pl.multiple_of(((high ^ j) * N_LOW + (low ^ k)) * wide, wide)
        copy = pltpu.make_async_copy(
            acts_ref.at[:, pl.ds(column, wide)], columns.at[n], sems.at[first_sem + n]
        )
        copy.start()
        copies.append(copy)
    return copies


def grad_kernel(n_high, where_ref, acts_ref, grad_ref, *refs):
    state_refs, refs = refs[:3], refs[3:]
    away_far, away_near, away_rest, kept_far, kept_near, kept_rest = refs[:6]
    mine_ref, near_columns, far_columns, logit_grads, blocks, sems = refs[6:]
    high, low, core, rep = [where_ref[i] for i in range(4)]
    half = blocks.shape[2]
    last = sems.shape[0]
    loads = pltpu.make_async_copy(grad_ref, logit_grads, sems.at[last - 1])
    loads.start()
    places = near_places(core, n_high), far_places(n_high)
    loaded = []
    for at, columns in zip(places, (near_columns, far_columns)):
        copies = load_columns(acts_ref, columns, sems, len(loaded), high, low, at)
        loaded += [(copy, columns, n) for n, copy in enumerate(copies)]
    rows = pl.ds(pl.multiple_of(rep * half, half), half)
    state = [
        pltpu.make_async_copy(ref.at[rows], mine_ref.at[i], sems.at[last - 4 + i])
        for i, ref in enumerate(state_refs)
    ]
    for copy in state:
        copy.start()
    loads.wait()
    for copy, columns, m in loaded:
        copy.wait()
        product = lax.dot_general(
            columns[m], logit_grads[...], (((0,), (0,)), ((), ())), preferred_element_type=jnp.float32
        )
        blocks[...] = product.astype(blocks.dtype).reshape(blocks.shape)
        if columns is far_columns:
            p, j = divmod(m, n_high - 1)
            j = j + 1
        else:
            p, j = (m, 0) if m < 2 else divmod(m - 2, n_high)
        if columns is far_columns or m < 2:
            flip = rep ^ core ^ parity(FIRST[p])
            for c in range(2):
                if j:
                    kept_far[p ^ core, c, j - 1] = blocks[c, flip]
                    away_far[p ^ core ^ 1, c, j - 1] = blocks[c, flip ^ 1]
                else:
                    kept_near[p ^ core, c] = blocks[c, flip]
                    away_near[p ^ core ^ 1, c] = blocks[c, flip ^ 1]
        else:
            slot = kept_rest if p == 0 else away_rest
            flip = rep ^ core ^ p
            for c in range(2):
                slot[c, j] = blocks[c, flip]
            kept_rest[2 + (core ^ p), j] = blocks[core, flip ^ 1]
            away_rest[2 + (core ^ p), j] = blocks[core ^ 1, flip ^ 1]
    for copy in state:
        copy.wait()


def logits_kernel(place, where_ref, columns_ref, *refs):
    *pieces, out_ref, weight = refs
    before = None
    if len(pieces[-1].shape) == 2:
        *pieces, before = pieces
    half, experts = weight.shape[-2:]
    for piece, blocks in zip(pieces, place(where_ref[2], where_ref[3])):
        for index, n, owner, of_rep in blocks:
            weight[n, owner, of_rep] = piece[index]
    total = None if before is None else before[...]
    for n in range(weight.shape[0]):
        part = jnp.dot(
            columns_ref[n],
            weight[n].reshape(4 * half, experts),
            preferred_element_type=jnp.float32,
        )
        total = part if total is None else total + part
    out_ref[...] = total.astype(out_ref.dtype)


def slot_owner(core, rep, i, slot, c):
    of_core = core ^ i
    return of_core ^ slot, c, rep ^ parity(FIRST[slot]) ^ of_core


def near_place(core, rep, n_high):
    pieces = []
    for i in range(2):
        at = [(slot, c, *slot_owner(core, rep, i, slot, c)) for slot in range(2) for c in range(2)]
        pieces.append([((slot, c), n, owner, of_rep) for slot, c, n, owner, of_rep in at])
    low_3, low_0 = 2 + n_high * core, 2 + n_high * (1 - core)
    for i in range(2):
        of_core = core ^ i
        blocks = []
        for j in range(n_high):
            blocks += [((c, j), 2 + n_high * i + j, c, rep ^ of_core) for c in range(2)]
            blocks.append(((2, j), low_3 + j, of_core, rep ^ 1))
        pieces.append(blocks)
    pieces.append([((c, j), low_0 + j, c, rep) for c in range(2) for j in range(n_high)])
    return pieces


def far_place(core, rep, n_high):
    pieces = []
    for i in range(2):
        blocks = []
        for slot in range(2):
            for c in range(2):
                which, owner, of_rep = slot_owner(core, rep, i, slot, c)
                for j in range(n_high - 1):
                    blocks.append(((slot, c, j), which * (n_high - 1) + j, owner, of_rep))
        pieces.append(blocks)
    return pieces


def solution(mesh):
    n_seq, n_rep = mesh.shape["seq"], mesh.shape["rep"]
    n_high = n_seq // (2 * N_LOW)
    fine = Mesh(mesh.devices.reshape(n_high, N_LOW, 2, n_rep), AXES)

    def swap(x, axis, mask=1):
        return lax.ppermute(x, axis, [(i, i ^ mask) for i in range(fine.shape[axis])])

    def cube_swap(x, change):
        pairs = []
        for low in range(N_LOW):
            for core in range(2):
                d_low, d_rep = change(core)
                for rep in range(n_rep):
                    there = ((low ^ d_low) * 2 + core) * n_rep + (rep ^ d_rep)
                    pairs.append(((low * 2 + core) * n_rep + rep, there))
        return lax.ppermute(x, AXES[1:], pairs)

    def to_partner(x, k):
        return cube_swap(x, lambda core: (k ^ (3 * core), parity(k) ^ core))

    def to_corner(x):
        return cube_swap(x, lambda core: (3, 1))

    def per_device(acts, grad_logits, master, moment_one, moment_two, step_count):
        tokens, experts = grad_logits.shape
        rows = master.shape[0]
        half = rows // n_rep
        high, low, core, rep = (lax.axis_index(a) for a in AXES)
        where = jnp.stack([high, low, core, rep])
        first_core = core == 0
        f32, bf16 = jnp.float32, jnp.bfloat16
        in_kernels = half % 16 == 0 and (4 * half) % 128 == 0

        smem = pl.BlockSpec(memory_space=pltpu.SMEM)
        vmem = pl.BlockSpec(memory_space=pltpu.VMEM)
        anywhere = pl.BlockSpec(memory_space=pl.ANY)
        params = pltpu.CompilerParams(vmem_limit_bytes=VMEM_LIMIT)
        state_in = (master, moment_one, moment_two)

        if in_kernels:
            acts = pltpu.with_memory_space_constraint(acts, pltpu.HBM)
            shapes = [(2, 2, n_high - 1), (2, 2), (4, n_high)] * 2
            outs = [pltpu.VMEM((*shape, half, experts), bf16) for shape in shapes]
            outs.append(pltpu.VMEM((3, half, experts), f32))
            counts = 2 + 2 * n_high, 2 * (n_high - 1)
            outs += [pltpu.VMEM((n, tokens, 4 * half), bf16) for n in counts]
            *sorted_rows, mine, near_columns, far_columns = pl.pallas_call(
                functools.partial(grad_kernel, n_high),
                out_shape=outs,
                in_specs=[smem] + [anywhere] * 5,
                out_specs=[vmem] * len(outs),
                scratch_shapes=[
                    pltpu.VMEM((tokens, experts), bf16),
                    pltpu.VMEM((2, 2, half, experts), bf16),
                    pltpu.SemaphoreType.DMA((4 * n_high + 4,)),
                ],
                compiler_params=params,
            )(
                where,
                acts,
                *(pltpu.with_memory_space_constraint(x, pltpu.HBM) for x in (grad_logits, *state_in)),
            )
            away, kept = sorted_rows[:3], sorted_rows[3:]
            columns = (near_columns, far_columns)
        else:
            columns = (None, None)
            product = lax.dot_general(
                acts, grad_logits, (((0,), (0,)), ((), ())), preferred_element_type=f32
            ).astype(bf16)
            product = product.reshape(n_high, N_LOW, 2, n_rep, half, experts)
            product = product[high ^ jnp.arange(n_high)]

            def block(d_low, owner, d_rep):
                at = (0, low ^ d_low, owner, rep ^ d_rep, 0, 0)
                part = lax.dynamic_slice(product, at, (n_high, 1, 1, 1, half, experts))
                return part.reshape(n_high, half, experts)

            def slot(k, of_core):
                change = k ^ (3 * of_core), parity(k) ^ of_core
                return jnp.stack([block(change[0], c, change[1]) for c in range(2)])

            def sort_rows(of_core):
                first = jnp.stack([slot(k, of_core) for k in FIRST])
                rest = [slot(3, of_core), block(3, of_core, 1)[None], block(0, of_core, 0)[None]]
                return first[:, :, 1:], first[:, :, 0], jnp.concatenate(rest)

            away, kept = sort_rows(1 - core), sort_rows(core)
            mine = jnp.stack([lax.dynamic_slice_in_dim(x, rep * half, half, 0) for x in state_in])

        far, near, rest = [
            mine_too.astype(f32) + swap(theirs, "core").astype(f32)
            for mine_too, theirs in zip(kept, away)
        ]
        far = [to_partner(far[i].astype(bf16), k) for i, k in enumerate(FIRST)]
        slot_3 = to_partner(rest[:2].astype(bf16), 3)
        corner = to_corner(rest[2].astype(bf16))
        home = rest[3]
        near = [to_partner(near[i].astype(bf16), k) for i, k in enumerate(FIRST)]

        *far, slot_3, corner = [x.astype(f32) for x in lax.optimization_barrier((*far, slot_3, corner))]
        mine_only = corner + home
        far = far[0] + far[1] + slot_3[:, 1:]
        far = [far[c] + jnp.where(core == c, mine_only[1:], 0.0) for c in range(2)]
        far = jnp.stack(far, 1).astype(bf16)
        total = near[0].astype(f32) + near[1].astype(f32) + slot_3[:, 0]
        for j in range(1, n_high):
            total = total + swap(far[j - 1], "high", j).astype(f32)
        theirs = swap(lax.dynamic_index_in_dim(total, 1 - core, 0, keepdims=False), "core")
        grad = lax.dynamic_index_in_dim(total, core, 0, keepdims=False) + theirs + mine_only[0]

        weight = adamw(grad, *mine, step_count)[0].astype(bf16)
        across = swap(weight, "core")
        near = jnp.where(core == 0, jnp.stack([weight, across]), jnp.stack([across, weight]))
        far = [swap(near, "high", j) for j in range(1, n_high)]
        got_near = [to_partner(near, k) for k in FIRST]
        other = swap(grad, "rep")
        got_near, far = lax.optimization_barrier((got_near, far))
        chip = jnp.stack([near, *far], 1)
        far = chip[:, 1:]
        slot_3 = to_partner(chip, 3)
        corner = to_corner(lax.dynamic_index_in_dim(chip, core, 0, keepdims=False))
        got_far = [to_partner(far, k) for k in FIRST]

        whole = jnp.where(
            rep == 0,
            jnp.concatenate([grad, other], 0),
            jnp.concatenate([other, grad], 0),
        )
        state = adamw(whole, *state_in, step_count)
        got_far, slot_3, corner, state = lax.optimization_barrier((got_far, slot_3, corner, state))
        near = jnp.stack(got_near)
        near_over = swap(near, "core")
        rest = jnp.concatenate([slot_3, corner[None]])
        rest_over = swap(rest, "core")
        far = jnp.stack(got_far)
        far_over = swap(far, "core")

        pieces = ([near, near_over, rest, rest_over, chip], [far, far_over])
        stages = (near_places(core, n_high), far_places(n_high))
        logits = None
        for blocks, place, received, acts_columns in zip(
            stages, (near_place, far_place), pieces, columns
        ):
            before = [] if logits is None else [logits]
            if in_kernels:
                operands = [
                    pltpu.with_memory_space_constraint(x, pltpu.VMEM)
                    for x in [acts_columns] + received + before
                ]
                logits = pl.pallas_call(
                    functools.partial(logits_kernel, functools.partial(place, n_high=n_high)),
                    out_shape=jax.ShapeDtypeStruct((tokens, experts), bf16 if before else f32),
                    in_specs=[smem] + [vmem] * len(operands),
                    out_specs=vmem,
                    scratch_shapes=[pltpu.VMEM((len(blocks), 2, 2, half, experts), bf16)],
                    compiler_params=params,
                )(where, *operands)
            else:
                at = jnp.stack([((high ^ j) * N_LOW + (low ^ k)) * 2 for k, j in blocks])
                full = jnp.zeros((2 * n_seq, half, experts), bf16)
                rows_at, values = [], []
                for piece, put in zip(received, place(core, rep, n_high)):
                    for index, n, owner, of_rep in put:
                        rows_at.append((at[n] + owner) * n_rep + of_rep)
                        values.append(piece[index])
                full = full.at[jnp.stack(rows_at)].set(jnp.stack(values))
                part = jnp.dot(acts, full.reshape(n_seq * rows, experts), preferred_element_type=f32)
                logits = (logits + part).astype(bf16) if before else part
        return *state, logits

    rows_of, tokens_of = P(AXES[:3], None), P(AXES, None)
    return jax.shard_map(
        per_device,
        mesh=fine,
        in_specs=(tokens_of, tokens_of, rows_of, rows_of, rows_of, P()),
        out_specs=(rows_of, rows_of, rows_of, tokens_of),
        check_vma=False,
    )
```

```python
import functools

import jax
import jax.numpy as jnp
from jax import lax
from jax.experimental import pallas as pl
from jax.experimental.pallas import tpu as pltpu
from jax.sharding import Mesh
from jax.sharding import PartitionSpec as P

AXES = ("high", "low", "core", "rep")
N_LOW = 4
VMEM_LIMIT = 8 * 2**20


def partner(slot, core):
    if slot < 2:
        return 1 + core, 1 ^ slot ^ core
    return 3 * (1 - core), core


def adamw(grad, master, moment_one, moment_two, step_count):
    count = step_count[0].astype(jnp.float32)
    beta_one = 0.9
    beta_two = 0.95
    first = beta_one * moment_one + (1.0 - beta_one) * grad
    second = beta_two * moment_two + (1.0 - beta_two) * grad * grad
    first_hat = first / (1.0 - jnp.power(beta_one, count))
    second_hat = second / (1.0 - jnp.power(beta_two, count))
    updated = master - 0.01 * (first_hat / (jnp.sqrt(second_hat) + 1e-08) + 0.1 * master)
    return updated, first, second


def near_places(core, n_high):
    slot_2 = [(partner(2, c)[0], j) for c in (core, 1 - core) for j in range(n_high)]
    return [(partner(0, c)[0], 0) for c in (core, 1 - core)] + slot_2


def far_places(core, n_high):
    return [(partner(0, c)[0], j) for c in (core, 1 - core) for j in range(1, n_high)]


def load_columns(acts_ref, columns, sems, first_sem, high, low, places):
    wide = columns.shape[-1]
    copies = []
    for n, (k, j) in enumerate(places):
        column = pl.multiple_of(((high ^ j) * N_LOW + (low ^ k)) * wide, wide)
        copy = pltpu.make_async_copy(
            acts_ref.at[:, pl.ds(column, wide)], columns.at[n], sems.at[first_sem + n]
        )
        copy.start()
        copies.append(copy)
    return copies


def grad_kernel(n_high, where_ref, acts_ref, grad_ref, *refs):
    state_refs, refs = refs[:3], refs[3:]
    away_far, away_near, away_rest, kept_far, kept_near, kept_rest = refs[:6]
    mine_ref, near_columns, far_columns, logit_grads, blocks, sems = refs[6:]
    high, low, core, rep = [where_ref[i] for i in range(4)]
    half = blocks.shape[2]
    last = sems.shape[0]
    loads = pltpu.make_async_copy(grad_ref, logit_grads, sems.at[last - 1])
    loads.start()
    places = near_places(core, n_high), far_places(core, n_high)
    loaded = []
    for at, columns in zip(places, (near_columns, far_columns)):
        copies = load_columns(acts_ref, columns, sems, len(loaded), high, low, at)
        loaded += [(copy, columns, n) for n, copy in enumerate(copies)]
    rows = pl.ds(pl.multiple_of(rep * half, half), half)
    state = [
        pltpu.make_async_copy(ref.at[rows], mine_ref.at[i], sems.at[last - 4 + i])
        for i, ref in enumerate(state_refs)
    ]
    for copy in state:
        copy.start()
    loads.wait()
    for copy, columns, m in loaded:
        copy.wait()
        product = lax.dot_general(
            columns[m], logit_grads[...], (((0,), (0,)), ((), ())), preferred_element_type=jnp.float32
        )
        blocks[...] = product.astype(blocks.dtype).reshape(blocks.shape)
        if columns is far_columns:
            p, j = divmod(m, n_high - 1)
            j = j + 1
        else:
            p, j = (m, 0) if m < 2 else divmod(m - 2, n_high)
        far, near, rest = (kept_far, kept_near, kept_rest) if p == 0 else (away_far, away_near, away_rest)
        of_core = core ^ p
        if columns is far_columns or m < 2:
            for slot in range(2):
                of_rep = rep ^ partner(slot, of_core)[1]
                for c in range(2):
                    if j:
                        far[slot, c, j - 1] = blocks[c, of_rep]
                    else:
                        near[slot, c] = blocks[c, of_rep]
        else:
            of_rep = rep ^ partner(2, of_core)[1]
            for c in range(2):
                rest[c, j] = blocks[c, of_rep]
            kept_rest[2 + of_core, j] = blocks[core, of_rep ^ 1]
            away_rest[2 + of_core, j] = blocks[core ^ 1, of_rep ^ 1]
    for copy in state:
        copy.wait()


def columns_kernel(n_high, where_ref, acts_ref, near_columns, far_columns, sems):
    high, low, core = [where_ref[i] for i in range(3)]
    copies = load_columns(acts_ref, near_columns, sems, 0, high, low, near_places(core, n_high))
    copies += load_columns(acts_ref, far_columns, sems, len(copies), high, low, far_places(core, n_high))
    for copy in copies:
        copy.wait()


def logits_kernel(place, where_ref, columns_ref, *refs):
    *pieces, out_ref, weight = refs
    before = None
    if len(pieces[-1].shape) == 2:
        *pieces, before = pieces
    half, experts = weight.shape[-2:]
    for piece, blocks in zip(pieces, place(where_ref[2], where_ref[3])):
        for index, n, owner, of_rep in blocks:
            weight[n, owner, of_rep] = piece[index]
    total = None if before is None else before[...]
    for n in range(weight.shape[0]):
        part = jnp.dot(
            columns_ref[n],
            weight[n].reshape(4 * half, experts),
            preferred_element_type=jnp.float32,
        )
        total = part if total is None else total + part
    out_ref[...] = total.astype(out_ref.dtype)


def near_place(core, rep, n_high):
    pieces = []
    for i in range(2):
        of_rep = [rep ^ partner(slot, core ^ i)[1] for slot in range(2)]
        pieces.append([((slot, c), i, c, of_rep[slot]) for slot in range(2) for c in range(2)])
    low_3, low_0 = 2 + n_high * core, 2 + n_high * (1 - core)
    for i in range(2):
        of_core = core ^ i
        of_rep = rep ^ partner(2, of_core)[1]
        blocks = []
        for j in range(n_high):
            blocks += [((c, j), 2 + n_high * i + j, c, of_rep) for c in range(2)]
            blocks.append(((2, j), low_3 + j, of_core, rep ^ 1))
        pieces.append(blocks)
    pieces.append([((c, j), low_0 + j, c, rep) for c in range(2) for j in range(n_high)])
    return pieces


def far_place(core, rep, n_high):
    pieces = []
    for i in range(2):
        blocks = []
        for slot in range(2):
            of_rep = rep ^ partner(slot, core ^ i)[1]
            for c in range(2):
                for j in range(n_high - 1):
                    blocks.append(((slot, c, j), i * (n_high - 1) + j, c, of_rep))
        pieces.append(blocks)
    return pieces


def solution(mesh):
    n_seq, n_rep = mesh.shape["seq"], mesh.shape["rep"]
    n_high = n_seq // (2 * N_LOW)
    fine = Mesh(mesh.devices.reshape(n_high, N_LOW, 2, n_rep), AXES)

    def swap(x, axis, mask=1):
        return lax.ppermute(x, axis, [(i, i ^ mask) for i in range(fine.shape[axis])])

    def cube_swap(x, change):
        pairs = []
        for low in range(N_LOW):
            for core in range(2):
                d_low, d_rep = change(core)
                for rep in range(n_rep):
                    there = ((low ^ d_low) * 2 + core) * n_rep + (rep ^ d_rep)
                    pairs.append(((low * 2 + core) * n_rep + rep, there))
        return lax.ppermute(x, AXES[1:], pairs)

    def to_partner(x, slot):
        return cube_swap(x, lambda core: partner(slot, core))

    def to_corner(x):
        return cube_swap(x, lambda core: (3, 1))

    def per_device(acts, grad_logits, master, moment_one, moment_two, step_count):
        tokens, experts = grad_logits.shape
        rows = master.shape[0]
        half = rows // n_rep
        high, low, core, rep = (lax.axis_index(a) for a in AXES)
        where = jnp.stack([high, low, core, rep])
        first_core = core == 0
        f32, bf16 = jnp.float32, jnp.bfloat16
        in_kernels = half % 16 == 0 and (4 * half) % 128 == 0

        smem = pl.BlockSpec(memory_space=pltpu.SMEM)
        vmem = pl.BlockSpec(memory_space=pltpu.VMEM)
        anywhere = pl.BlockSpec(memory_space=pl.ANY)
        params = pltpu.CompilerParams(vmem_limit_bytes=VMEM_LIMIT)
        state_in = (master, moment_one, moment_two)

        if in_kernels:
            acts = pltpu.with_memory_space_constraint(acts, pltpu.HBM)
            shapes = [(2, 2, n_high - 1), (2, 2), (4, n_high)] * 2
            outs = [pltpu.VMEM((*shape, half, experts), bf16) for shape in shapes]
            outs.append(pltpu.VMEM((3, half, experts), f32))
            counts = 2 + 2 * n_high, 2 * (n_high - 1)
            columns = [pltpu.VMEM((n, tokens, 4 * half), bf16) for n in counts]
            *sorted_rows, mine = pl.pallas_call(
                functools.partial(grad_kernel, n_high),
                out_shape=outs,
                in_specs=[smem] + [anywhere] * 5,
                out_specs=[vmem] * len(outs),
                scratch_shapes=columns
                + [
                    pltpu.VMEM((tokens, experts), bf16),
                    pltpu.VMEM((2, 2, half, experts), bf16),
                    pltpu.SemaphoreType.DMA((4 * n_high + 4,)),
                ],
                compiler_params=params,
            )(
                where,
                acts,
                *(pltpu.with_memory_space_constraint(x, pltpu.HBM) for x in (grad_logits, *state_in)),
            )
            away, kept = sorted_rows[:3], sorted_rows[3:]
        else:
            product = lax.dot_general(
                acts, grad_logits, (((0,), (0,)), ((), ())), preferred_element_type=f32
            ).astype(bf16)
            product = product.reshape(n_high, N_LOW, 2, n_rep, half, experts)
            product = product[high ^ jnp.arange(n_high)]

            def block(d_low, owner, d_rep):
                at = (0, low ^ d_low, owner, rep ^ d_rep, 0, 0)
                part = lax.dynamic_slice(product, at, (n_high, 1, 1, 1, half, experts))
                return part.reshape(n_high, half, experts)

            def sort_rows(of_core):
                slots = []
                for slot in range(3):
                    d_low, d_rep = partner(slot, of_core)
                    slots.append(jnp.stack([block(d_low, c, d_rep) for c in range(2)]))
                first = jnp.stack(slots[:2])
                rest = [slots[2], block(3, of_core, 1)[None], block(0, of_core, 0)[None]]
                return first[:, :, 1:], first[:, :, 0], jnp.concatenate(rest)

            away, kept = sort_rows(1 - core), sort_rows(core)
            mine = jnp.stack([lax.dynamic_slice_in_dim(x, rep * half, half, 0) for x in state_in])

        far, near, rest = [
            mine_too.astype(f32) + swap(theirs, "core").astype(f32)
            for mine_too, theirs in zip(kept, away)
        ]
        far = [to_partner(far[slot].astype(bf16), slot) for slot in range(2)]
        slot_2 = to_partner(rest[:2].astype(bf16), 2)
        corner = to_corner(rest[2].astype(bf16))
        home = rest[3]
        near = [to_partner(near[slot].astype(bf16), slot) for slot in range(2)]

        *far, slot_2, corner = [x.astype(f32) for x in lax.optimization_barrier((*far, slot_2, corner))]
        mine_only = corner + home
        far = far[0] + far[1] + slot_2[:, 1:]
        far = [far[c] + jnp.where(core == c, mine_only[1:], 0.0) for c in range(2)]
        far = jnp.stack(far, 1).astype(bf16)
        sent = [swap(far[j - 1], "high", j) for j in range(1, n_high)]
        near, late_acts = lax.optimization_barrier((near, acts))
        total = near[0].astype(f32) + near[1].astype(f32) + slot_2[:, 0]
        for part in sent:
            total = total + part.astype(f32)
        if in_kernels:
            columns = pl.pallas_call(
                functools.partial(columns_kernel, n_high),
                out_shape=columns,
                in_specs=[smem, anywhere],
                out_specs=[vmem, vmem],
                scratch_shapes=[pltpu.SemaphoreType.DMA((4 * n_high,))],
                compiler_params=params,
            )(where, pltpu.with_memory_space_constraint(late_acts, pltpu.HBM))
            total, columns = lax.optimization_barrier((total, columns))
        else:
            columns = (None, None)
        theirs = swap(lax.dynamic_index_in_dim(total, 1 - core, 0, keepdims=False), "core")
        grad = lax.dynamic_index_in_dim(total, core, 0, keepdims=False) + theirs + mine_only[0]

        weight = adamw(grad, *mine, step_count)[0].astype(bf16)
        across = swap(weight, "core")
        near = jnp.where(core == 0, jnp.stack([weight, across]), jnp.stack([across, weight]))
        far = [swap(near, "high", j) for j in range(1, n_high)]
        got_near = [to_partner(near, slot) for slot in range(2)]
        got_near, far, grad = lax.optimization_barrier((got_near, far, grad))
        other = swap(grad, "rep")
        chip = jnp.stack([near, *far], 1)
        far = chip[:, 1:]
        slot_2 = to_partner(chip, 2)
        corner = to_corner(lax.dynamic_index_in_dim(chip, core, 0, keepdims=False))
        got_far = [to_partner(far, slot) for slot in range(2)]

        whole = jnp.where(
            rep == 0,
            jnp.concatenate([grad, other], 0),
            jnp.concatenate([other, grad], 0),
        )
        state = adamw(whole, *state_in, step_count)
        got_far, slot_2, corner, state = lax.optimization_barrier((got_far, slot_2, corner, state))
        near = jnp.stack(got_near)
        near_over = swap(near, "core")
        rest = jnp.concatenate([slot_2, corner[None]])
        rest_over = swap(rest, "core")
        far = jnp.stack(got_far)
        far_over = swap(far, "core")

        pieces = ([near, near_over, rest, rest_over, chip], [far, far_over])
        stages = (near_places(core, n_high), far_places(core, n_high))
        logits = None
        for blocks, place, received, acts_columns in zip(
            stages, (near_place, far_place), pieces, columns
        ):
            before = [] if logits is None else [logits]
            if in_kernels:
                operands = [
                    pltpu.with_memory_space_constraint(x, pltpu.VMEM)
                    for x in [acts_columns] + received + before
                ]
                logits = pl.pallas_call(
                    functools.partial(logits_kernel, functools.partial(place, n_high=n_high)),
                    out_shape=jax.ShapeDtypeStruct((tokens, experts), bf16 if before else f32),
                    in_specs=[smem] + [vmem] * len(operands),
                    out_specs=vmem,
                    scratch_shapes=[pltpu.VMEM((len(blocks), 2, 2, half, experts), bf16)],
                    compiler_params=params,
                )(where, *operands)
            else:
                at = jnp.stack([((high ^ j) * N_LOW + (low ^ k)) * 2 for k, j in blocks])
                full = jnp.zeros((2 * n_seq, half, experts), bf16)
                rows_at, values = [], []
                for piece, put in zip(received, place(core, rep, n_high)):
                    for index, n, owner, of_rep in put:
                        rows_at.append((at[n] + owner) * n_rep + of_rep)
                        values.append(piece[index])
                full = full.at[jnp.stack(rows_at)].set(jnp.stack(values))
                part = jnp.dot(acts, full.reshape(n_seq * rows, experts), preferred_element_type=f32)
                logits = (logits + part).astype(bf16) if before else part
        return *state, logits

    rows_of, tokens_of = P(AXES[:3], None), P(AXES, None)
    return jax.shard_map(
        per_device,
        mesh=fine,
        in_specs=(tokens_of, tokens_of, rows_of, rows_of, rows_of, P()),
        out_specs=(rows_of, rows_of, rows_of, tokens_of),
        check_vma=False,
    )
```

```python
import functools

import jax
import jax.numpy as jnp
from jax import lax
from jax.experimental import pallas as pl
from jax.experimental.pallas import tpu as pltpu
from jax.sharding import Mesh
from jax.sharding import PartitionSpec as P

AXES = ("high", "low", "core", "rep")
N_LOW = 4
CHIPS = ((1, 0), (2, 1), (2, 0), (1, 1), (0, 1), (3, 0), (3, 1), (0, 0))
LOWS = ((1, 2), (0, 3))
VMEM_LIMIT = 8 * 2**20


def slot_of(chip, core):
    slot = CHIPS.index(chip)
    return slot if slot >= 6 else slot ^ core


def adamw(grad, master, moment_one, moment_two, step_count):
    count = step_count[0].astype(jnp.float32)
    beta_one = 0.9
    beta_two = 0.95
    first = beta_one * moment_one + (1.0 - beta_one) * grad
    second = beta_two * moment_two + (1.0 - beta_two) * grad * grad
    first_hat = first / (1.0 - jnp.power(beta_one, count))
    second_hat = second / (1.0 - jnp.power(beta_two, count))
    updated = master - 0.01 * (first_hat / (jnp.sqrt(second_hat) + 1e-08) + 0.1 * master)
    return updated, first, second


def load_columns(acts_ref, columns, sems, high, low, lows, n_high):
    wide = columns.shape[-1]
    copies = []
    for p, k in enumerate(lows):
        for j in range(n_high):
            column = pl.multiple_of(((high ^ j) * N_LOW + (low ^ k)) * wide, wide)
            n = p * n_high + j
            copy = pltpu.make_async_copy(acts_ref.at[:, pl.ds(column, wide)], columns.at[n], sems.at[n])
            copy.start()
            copies.append(copy)
    return copies


def grad_kernel(n_high, where_ref, acts_ref, grad_ref, *refs):
    state_refs, refs = refs[:3], refs[3:]
    away, kept, refs = refs[:2], refs[2:4], refs[4:]
    mine_ref, columns, logit_grads, blocks, sems = refs
    high, low, core, rep = [where_ref[i] for i in range(4)]
    half = blocks.shape[2]
    last = sems.shape[0]
    loads = pltpu.make_async_copy(grad_ref, logit_grads, sems.at[last - 1])
    loads.start()
    lows = LOWS[0] + LOWS[1]
    copies = load_columns(acts_ref, columns, sems, high, low, lows, n_high)
    rows = pl.ds(pl.multiple_of(rep * half, half), half)
    state = [
        pltpu.make_async_copy(ref.at[rows], mine_ref.at[i], sems.at[last - 4 + i])
        for i, ref in enumerate(state_refs)
    ]
    for copy in state:
        copy.start()
    loads.wait()
    for n, copy in enumerate(copies):
        copy.wait()
        product = lax.dot_general(
            columns[n], logit_grads[...], (((0,), (0,)), ((), ())), preferred_element_type=jnp.float32
        )
        blocks[...] = product.astype(blocks.dtype).reshape(blocks.shape)
        p, j = divmod(n, n_high)
        for d_rep in range(2):
            for outs, owner in ((kept, core), (away, 1 - core)):
                slot = slot_of((lows[p], d_rep), owner)
                outs[p // 2][slot - 4 * (p // 2), j] = blocks[owner, rep ^ d_rep]
    for copy in state:
        copy.wait()


def columns_kernel(n_high, where_ref, acts_ref, first_ref, second_ref, sems):
    high, low = where_ref[0], where_ref[1]
    copies = []
    for i, (lows, out) in enumerate(zip(LOWS, (first_ref, second_ref))):
        copies += load_columns(acts_ref, out, sems.at[i], high, low, lows, n_high)
    for copy in copies:
        copy.wait()


def logits_kernel(n_high, group, where_ref, columns_ref, *refs):
    *pieces, out_ref, weight = refs
    before = None
    if len(pieces[-1].shape) == 2:
        *pieces, before = pieces
    core, rep = where_ref[2], where_ref[3]
    half, experts = weight.shape[-2:]
    for i, piece in enumerate(pieces):
        owner = core ^ (i % 2)
        for n, place, of_rep in places(group, owner, rep, i // 2, piece.shape[0]):
            for j in range(n_high):
                weight[place, j, owner, of_rep] = piece[n, j]
    total = None if before is None else before[...]
    for n in range(2 * n_high):
        part = jnp.dot(
            columns_ref[n],
            weight[n // n_high, n % n_high].reshape(4 * half, experts),
            preferred_element_type=jnp.float32,
        )
        total = part if total is None else total + part
    out_ref[...] = total.astype(out_ref.dtype)


def places(group, owner, rep, home, count):
    out = []
    for n in range(count):
        slot = 7 if home else 4 * group + n
        chip_low, d_rep = CHIPS[slot]
        flip = owner if slot < 6 else 0
        out.append((n, LOWS[group].index(chip_low) ^ flip, rep ^ d_rep ^ flip))
    return out


def solution(mesh):
    n_seq, n_rep = mesh.shape["seq"], mesh.shape["rep"]
    n_high = n_seq // (2 * N_LOW)
    fine = Mesh(mesh.devices.reshape(n_high, N_LOW, 2, n_rep), AXES)

    def swap(x, axis, mask=1):
        return lax.ppermute(x, axis, [(i, i ^ mask) for i in range(fine.shape[axis])])

    def cube_swap(x, change):
        pairs = []
        for low in range(N_LOW):
            for core in range(2):
                d_low, d_rep = change(core)
                for rep in range(n_rep):
                    there = ((low ^ d_low) * 2 + core) * n_rep + (rep ^ d_rep)
                    pairs.append(((low * 2 + core) * n_rep + rep, there))
        return lax.ppermute(x, AXES[1:], pairs)

    def to_slot(x, slot):
        return cube_swap(x, lambda core: CHIPS[slot ^ core if slot < 6 else slot])

    def per_device(acts, grad_logits, master, moment_one, moment_two, step_count):
        tokens, experts = grad_logits.shape
        rows = master.shape[0]
        half = rows // n_rep
        high, low, core, rep = (lax.axis_index(a) for a in AXES)
        where = jnp.stack([high, low, core, rep])
        f32, bf16 = jnp.float32, jnp.bfloat16
        in_kernels = half % 16 == 0 and (4 * half) % 128 == 0

        smem = pl.BlockSpec(memory_space=pltpu.SMEM)
        vmem = pl.BlockSpec(memory_space=pltpu.VMEM)
        anywhere = pl.BlockSpec(memory_space=pl.ANY)
        params = pltpu.CompilerParams(vmem_limit_bytes=VMEM_LIMIT)
        state_in = (master, moment_one, moment_two)

        if in_kernels:
            acts = pltpu.with_memory_space_constraint(acts, pltpu.HBM)
            shape = pltpu.VMEM((4, n_high, half, experts), bf16)
            *sorted_rows, mine = pl.pallas_call(
                functools.partial(grad_kernel, n_high),
                out_shape=[shape] * 4 + [pltpu.VMEM((3, half, experts), f32)],
                in_specs=[smem] + [anywhere] * 5,
                out_specs=[vmem] * 5,
                scratch_shapes=[
                    pltpu.VMEM((4 * n_high, tokens, 4 * half), bf16),
                    pltpu.VMEM((tokens, experts), bf16),
                    pltpu.VMEM((2, 2, half, experts), bf16),
                    pltpu.SemaphoreType.DMA((4 * n_high + 4,)),
                ],
                compiler_params=params,
            )(
                where,
                acts,
                *(pltpu.with_memory_space_constraint(x, pltpu.HBM) for x in (grad_logits, *state_in)),
            )
            away, kept = sorted_rows[:2], sorted_rows[2:]
        else:
            product = lax.dot_general(
                acts, grad_logits, (((0,), (0,)), ((), ())), preferred_element_type=f32
            ).astype(bf16)
            product = product.reshape(n_high, N_LOW, 2, n_rep, half, experts)
            product = product[high ^ jnp.arange(n_high)]

            def sort_rows(owner):
                blocks = []
                for slot in range(8):
                    flip = owner if slot < 6 else 0
                    d_low, d_rep = CHIPS[slot]
                    at = (0, low ^ d_low ^ (3 * flip), owner, rep ^ d_rep ^ flip, 0, 0)
                    part = lax.dynamic_slice(product, at, (n_high, 1, 1, 1, half, experts))
                    blocks.append(part.reshape(n_high, half, experts))
                return jnp.stack(blocks[:4]), jnp.stack(blocks[4:])

            away, kept = sort_rows(1 - core), sort_rows(core)
            mine = jnp.stack([lax.dynamic_slice_in_dim(x, rep * half, half, 0) for x in state_in])

        parts = []
        for own, theirs in zip(kept, away):
            summed = own.astype(f32) + swap(theirs, "core").astype(f32)
            for n in range(4):
                slot = len(parts)
                parts.append(summed[n] if slot == 7 else to_slot(summed[n].astype(bf16), slot))
        parts = lax.optimization_barrier(parts)
        total = sum(x.astype(f32) for x in parts)

        grad = total[0]
        for j in range(1, n_high):
            grad = grad + swap(total[j].astype(bf16), "high", j).astype(f32)
        weight = adamw(grad, *mine, step_count)[0].astype(bf16)

        column = jnp.stack([swap(weight, "high", j) if j else weight for j in range(n_high)])
        other = swap(grad, "rep")
        column, other = lax.optimization_barrier((column, other))
        got = [to_slot(column, slot) for slot in range(7)]
        across = swap(column, "core")

        whole = jnp.where(
            rep == 0,
            jnp.concatenate([grad, other], 0),
            jnp.concatenate([other, grad], 0),
        )
        got[:2], whole, late_acts = lax.optimization_barrier((got[:2], whole, acts))
        state = adamw(whole, *state_in, step_count)

        columns = [None, None]
        if in_kernels:
            columns = pl.pallas_call(
                functools.partial(columns_kernel, n_high),
                out_shape=(pltpu.VMEM((2 * n_high, tokens, 4 * half), bf16),) * 2,
                in_specs=[smem, anywhere],
                out_specs=(vmem, vmem),
                scratch_shapes=[pltpu.SemaphoreType.DMA((2, 2 * n_high))],
                compiler_params=params,
            )(where, pltpu.with_memory_space_constraint(late_acts, pltpu.HBM))
        got[:4], state, columns = lax.optimization_barrier((got[:4], state, columns))
        first, second = jnp.stack(got[:4]), jnp.stack(got[4:])
        first_over, second_over = swap(first, "core"), swap(second, "core")
        pieces = ([first, first_over], [second, second_over, column[None], across[None]])
        logits = None
        for group, (received, acts_columns) in enumerate(zip(pieces, columns)):
            if in_kernels:
                before = [] if logits is None else [logits]
                operands = [
                    pltpu.with_memory_space_constraint(x, pltpu.VMEM) for x in [acts_columns] + received + before
                ]
                logits = pl.pallas_call(
                    functools.partial(logits_kernel, n_high, group),
                    out_shape=jax.ShapeDtypeStruct((tokens, experts), bf16 if before else f32),
                    in_specs=[smem] + [vmem] * len(operands),
                    out_specs=vmem,
                    scratch_shapes=[pltpu.VMEM((2, n_high, 2, 2, half, experts), bf16)],
                    compiler_params=params,
                )(where, *operands)
            else:
                rows_at, values = [], []
                for i, piece in enumerate(received):
                    owner = core ^ (i % 2)
                    for n, place, of_rep in places(group, owner, rep, i // 2, piece.shape[0]):
                        d_low = jnp.array(LOWS[group])[place]
                        for j in range(n_high):
                            at = ((high ^ j) * N_LOW + (low ^ d_low)) * 2 + owner
                            rows_at.append(at * n_rep + of_rep)
                            values.append(piece[n, j])
                full = jnp.zeros((2 * n_seq, half, experts), bf16)
                full = full.at[jnp.stack(rows_at)].set(jnp.stack(values))
                full = full.reshape(n_seq * rows, experts)
                part = jnp.dot(acts, full, preferred_element_type=f32)
                logits = part if logits is None else (logits + part).astype(bf16)
        return *state, logits

    rows_of, tokens_of = P(AXES[:3], None), P(AXES, None)
    return jax.shard_map(
        per_device,
        mesh=fine,
        in_specs=(tokens_of, tokens_of, rows_of, rows_of, rows_of, P()),
        out_specs=(rows_of, rows_of, rows_of, tokens_of),
        check_vma=False,
    )
```

```python
import functools

import jax
import jax.numpy as jnp
from jax import lax
from jax.experimental import pallas as pl
from jax.experimental.pallas import tpu as pltpu
from jax.sharding import Mesh
from jax.sharding import PartitionSpec as P

AXES = ("high", "low", "core", "rep")
N_LOW = 4
CHIPS = ((1, 0), (2, 1), (2, 0), (1, 1), (0, 1), (3, 0), (3, 1), (0, 0))
LOWS = ((1, 2), (0, 3))
NEXT = ((1, 0), (2, 0), (0, 1))
VMEM_LIMIT = 8 * 2**20


def slot_of(chip, core):
    slot = CHIPS.index(chip)
    return slot if slot >= 6 else slot ^ core


def adamw(grad, master, moment_one, moment_two, step_count):
    count = step_count[0].astype(jnp.float32)
    beta_one = 0.9
    beta_two = 0.95
    first = beta_one * moment_one + (1.0 - beta_one) * grad
    second = beta_two * moment_two + (1.0 - beta_two) * grad * grad
    first_hat = first / (1.0 - jnp.power(beta_one, count))
    second_hat = second / (1.0 - jnp.power(beta_two, count))
    updated = master - 0.01 * (first_hat / (jnp.sqrt(second_hat) + 1e-08) + 0.1 * master)
    return updated, first, second


def load_columns(acts_ref, columns, sems, high, low, lows, n_high):
    wide = columns.shape[-1]
    copies = []
    for p, k in enumerate(lows):
        for j in range(n_high):
            column = pl.multiple_of(((high ^ j) * N_LOW + (low ^ k)) * wide, wide)
            n = p * n_high + j
            copy = pltpu.make_async_copy(acts_ref.at[:, pl.ds(column, wide)], columns.at[n], sems.at[n])
            copy.start()
            copies.append(copy)
    return copies


def grad_kernel(n_high, where_ref, acts_ref, grad_ref, *refs):
    state_refs, refs = refs[:3], refs[3:]
    away, kept, refs = refs[:2], refs[2:4], refs[4:]
    mine_ref, columns, logit_grads, blocks, sems = refs
    high, low, core, rep = [where_ref[i] for i in range(4)]
    half = blocks.shape[2]
    last = sems.shape[0]
    loads = pltpu.make_async_copy(grad_ref, logit_grads, sems.at[last - 1])
    loads.start()
    lows = LOWS[0] + LOWS[1]
    copies = load_columns(acts_ref, columns, sems, high, low, lows, n_high)
    rows = pl.ds(pl.multiple_of(rep * half, half), half)
    state = [
        pltpu.make_async_copy(ref.at[rows], mine_ref.at[i], sems.at[last - 4 + i])
        for i, ref in enumerate(state_refs)
    ]
    for copy in state:
        copy.start()
    loads.wait()
    for n, copy in enumerate(copies):
        copy.wait()
        product = lax.dot_general(
            columns[n], logit_grads[...], (((0,), (0,)), ((), ())), preferred_element_type=jnp.float32
        )
        blocks[...] = product.astype(blocks.dtype).reshape(blocks.shape)
        p, j = divmod(n, n_high)
        for d_rep in range(2):
            for outs, owner in ((kept, core), (away, 1 - core)):
                slot = slot_of((lows[p], d_rep), owner)
                outs[p // 2][slot - 4 * (p // 2), j] = blocks[owner, rep ^ d_rep]
    for copy in state:
        copy.wait()


def columns_kernel(n_high, where_ref, acts_ref, first_ref, second_ref, sems):
    high, low = where_ref[0], where_ref[1]
    copies = []
    for i, (lows, out) in enumerate(zip(LOWS, (first_ref, second_ref))):
        copies += load_columns(acts_ref, out, sems.at[i], high, low, lows, n_high)
    for copy in copies:
        copy.wait()


def logits_kernel(n_high, group, where_ref, columns_ref, *refs):
    *pieces, out_ref, weight = refs
    before = None
    if len(pieces[-1].shape) == 2:
        *pieces, before = pieces
    half, experts = weight.shape[-2:]
    for piece, blocks in zip(pieces, places(group, where_ref[2], where_ref[3])):
        for n, (place, owner, of_rep) in enumerate(blocks):
            for j in range(n_high):
                weight[place, j, owner, of_rep] = piece[n, j]
    total = None if before is None else before[...]
    for n in range(2 * n_high):
        part = jnp.dot(
            columns_ref[n],
            weight[n // n_high, n % n_high].reshape(4 * half, experts),
            preferred_element_type=jnp.float32,
        )
        total = part if total is None else total + part
    out_ref[...] = total.astype(out_ref.dtype)


def places(group, core, rep):
    pieces = []
    for chip in NEXT[:2] if group == 0 else NEXT[2:]:
        for by in (core, 1 - core):
            place = LOWS[group].index(chip[0]) ^ by
            pieces.append([(place, owner, rep ^ chip[1] ^ by) for owner in range(2)])
    if group == 1:
        pieces += [[(1, owner, rep ^ 1)] for owner in (core, 1 - core)]
        pieces += [[(0, owner, rep)] for owner in (core, 1 - core)]
    return pieces


def solution(mesh):
    n_seq, n_rep = mesh.shape["seq"], mesh.shape["rep"]
    n_high = n_seq // (2 * N_LOW)
    fine = Mesh(mesh.devices.reshape(n_high, N_LOW, 2, n_rep), AXES)

    def swap(x, axis, mask=1):
        return lax.ppermute(x, axis, [(i, i ^ mask) for i in range(fine.shape[axis])])

    def cube_swap(x, change):
        pairs = []
        for low in range(N_LOW):
            for core in range(2):
                d_low, d_rep = change(core)
                for rep in range(n_rep):
                    there = ((low ^ d_low) * 2 + core) * n_rep + (rep ^ d_rep)
                    pairs.append(((low * 2 + core) * n_rep + rep, there))
        return lax.ppermute(x, AXES[1:], pairs)

    def to_slot(x, slot):
        return cube_swap(x, lambda core: CHIPS[slot ^ core if slot < 6 else slot])

    def to_next(x, slot):
        d_low, d_rep = NEXT[slot]
        return cube_swap(x, lambda core: (d_low ^ (3 * core), d_rep ^ core))

    def to_corner(x):
        return cube_swap(x, lambda core: (3, 1))

    def per_device(acts, grad_logits, master, moment_one, moment_two, step_count):
        tokens, experts = grad_logits.shape
        rows = master.shape[0]
        half = rows // n_rep
        high, low, core, rep = (lax.axis_index(a) for a in AXES)
        where = jnp.stack([high, low, core, rep])
        f32, bf16 = jnp.float32, jnp.bfloat16
        in_kernels = half % 16 == 0 and (4 * half) % 128 == 0

        smem = pl.BlockSpec(memory_space=pltpu.SMEM)
        vmem = pl.BlockSpec(memory_space=pltpu.VMEM)
        anywhere = pl.BlockSpec(memory_space=pl.ANY)
        params = pltpu.CompilerParams(vmem_limit_bytes=VMEM_LIMIT)
        state_in = (master, moment_one, moment_two)

        if in_kernels:
            acts = pltpu.with_memory_space_constraint(acts, pltpu.HBM)
            shape = pltpu.VMEM((4, n_high, half, experts), bf16)
            *sorted_rows, mine = pl.pallas_call(
                functools.partial(grad_kernel, n_high),
                out_shape=[shape] * 4 + [pltpu.VMEM((3, half, experts), f32)],
                in_specs=[smem] + [anywhere] * 5,
                out_specs=[vmem] * 5,
                scratch_shapes=[
                    pltpu.VMEM((4 * n_high, tokens, 4 * half), bf16),
                    pltpu.VMEM((tokens, experts), bf16),
                    pltpu.VMEM((2, 2, half, experts), bf16),
                    pltpu.SemaphoreType.DMA((4 * n_high + 4,)),
                ],
                compiler_params=params,
            )(
                where,
                acts,
                *(pltpu.with_memory_space_constraint(x, pltpu.HBM) for x in (grad_logits, *state_in)),
            )
            away, kept = sorted_rows[:2], sorted_rows[2:]
        else:
            product = lax.dot_general(
                acts, grad_logits, (((0,), (0,)), ((), ())), preferred_element_type=f32
            ).astype(bf16)
            product = product.reshape(n_high, N_LOW, 2, n_rep, half, experts)
            product = product[high ^ jnp.arange(n_high)]

            def sort_rows(owner):
                blocks = []
                for slot in range(8):
                    flip = owner if slot < 6 else 0
                    d_low, d_rep = CHIPS[slot]
                    at = (0, low ^ d_low ^ (3 * flip), owner, rep ^ d_rep ^ flip, 0, 0)
                    part = lax.dynamic_slice(product, at, (n_high, 1, 1, 1, half, experts))
                    blocks.append(part.reshape(n_high, half, experts))
                return jnp.stack(blocks[:4]), jnp.stack(blocks[4:])

            away, kept = sort_rows(1 - core), sort_rows(core)
            mine = jnp.stack([lax.dynamic_slice_in_dim(x, rep * half, half, 0) for x in state_in])

        parts = []
        for own, theirs in zip(kept, away):
            summed = own.astype(f32) + swap(theirs, "core").astype(f32)
            for n in range(4):
                slot = len(parts)
                parts.append(summed[n] if slot == 7 else to_slot(summed[n].astype(bf16), slot))
        parts = lax.optimization_barrier(parts)
        total = sum(x.astype(f32) for x in parts)

        grad = total[0]
        for j in range(1, n_high):
            grad = grad + swap(total[j].astype(bf16), "high", j).astype(f32)
        weight = adamw(grad, *mine, step_count)[0].astype(bf16)

        column = jnp.stack([swap(weight, "high", j) if j else weight for j in range(n_high)])
        column, grad = lax.optimization_barrier((column, grad))
        other = swap(grad, "rep")
        corner = to_corner(column)
        across = swap(column, "core")
        chip = jnp.where(core == 0, jnp.stack([column, across]), jnp.stack([across, column]))
        got = [to_next(chip, slot) for slot in range(3)]

        whole = jnp.where(
            rep == 0,
            jnp.concatenate([grad, other], 0),
            jnp.concatenate([other, grad], 0),
        )
        state = adamw(whole, *state_in, step_count)

        columns = [None, None]
        if in_kernels:
            state, late_acts = lax.optimization_barrier((state, acts))
            columns = pl.pallas_call(
                functools.partial(columns_kernel, n_high),
                out_shape=(pltpu.VMEM((2 * n_high, tokens, 4 * half), bf16),) * 2,
                in_specs=[smem, anywhere],
                out_specs=(vmem, vmem),
                scratch_shapes=[pltpu.SemaphoreType.DMA((2, 2 * n_high))],
                compiler_params=params,
            )(where, pltpu.with_memory_space_constraint(late_acts, pltpu.HBM))
        got[0], state, columns = lax.optimization_barrier((got[0], state, columns))
        got[2], corner = lax.optimization_barrier((got[2], corner))
        over = [swap(x, "core") for x in got]
        corner_over = swap(corner, "core")
        first = [x[slot] for slot in range(2) for x in (got, over)]
        second = [got[2], over[2], corner[None], corner_over[None], column[None], across[None]]
        pieces = (first, second)
        logits = None
        for group, (received, acts_columns) in enumerate(zip(pieces, columns)):
            if in_kernels:
                before = [] if logits is None else [logits]
                operands = [
                    pltpu.with_memory_space_constraint(x, pltpu.VMEM) for x in [acts_columns] + received + before
                ]
                logits = pl.pallas_call(
                    functools.partial(logits_kernel, n_high, group),
                    out_shape=jax.ShapeDtypeStruct((tokens, experts), bf16 if before else f32),
                    in_specs=[smem] + [vmem] * len(operands),
                    out_specs=vmem,
                    scratch_shapes=[pltpu.VMEM((2, n_high, 2, 2, half, experts), bf16)],
                    compiler_params=params,
                )(where, *operands)
            else:
                rows_at, values = [], []
                for piece, blocks in zip(received, places(group, core, rep)):
                    for n, (place, owner, of_rep) in enumerate(blocks):
                        d_low = jnp.array(LOWS[group])[place]
                        for j in range(n_high):
                            at = ((high ^ j) * N_LOW + (low ^ d_low)) * 2 + owner
                            rows_at.append(at * n_rep + of_rep)
                            values.append(piece[n, j])
                full = jnp.zeros((2 * n_seq, half, experts), bf16)
                full = full.at[jnp.stack(rows_at)].set(jnp.stack(values))
                full = full.reshape(n_seq * rows, experts)
                part = jnp.dot(acts, full, preferred_element_type=f32)
                logits = part if logits is None else (logits + part).astype(bf16)
        return *state, logits

    rows_of, tokens_of = P(AXES[:3], None), P(AXES, None)
    return jax.shard_map(
        per_device,
        mesh=fine,
        in_specs=(tokens_of, tokens_of, rows_of, rows_of, rows_of, P()),
        out_specs=(rows_of, rows_of, rows_of, tokens_of),
        check_vma=False,
    )
```

```python
import functools

import jax
import jax.numpy as jnp
from jax import lax
from jax.experimental import pallas as pl
from jax.experimental.pallas import tpu as pltpu
from jax.sharding import Mesh
from jax.sharding import PartitionSpec as P

AXES = ("high", "low", "core", "rep")
N_LOW = 4
CHIPS = ((1, 0), (2, 1), (2, 0), (1, 1), (0, 1), (3, 0), (3, 1), (0, 0))
LOWS = ((1, 2), (0, 3))
NEXT = ((1, 0), (2, 0), (0, 1))
VMEM_LIMIT = 8 * 2**20


def slot_of(chip, core):
    slot = CHIPS.index(chip)
    return slot if slot >= 6 else slot ^ core


def adamw(grad, master, moment_one, moment_two, step_count):
    count = step_count[0].astype(jnp.float32)
    beta_one = 0.9
    beta_two = 0.95
    first = beta_one * moment_one + (1.0 - beta_one) * grad
    second = beta_two * moment_two + (1.0 - beta_two) * grad * grad
    first_hat = first / (1.0 - jnp.power(beta_one, count))
    second_hat = second / (1.0 - jnp.power(beta_two, count))
    updated = master - 0.01 * (first_hat / (jnp.sqrt(second_hat) + 1e-08) + 0.1 * master)
    return updated, first, second


def load_columns(acts_ref, columns, sems, high, low, lows, n_high):
    wide = columns.shape[-1]
    copies = []
    for p, k in enumerate(lows):
        for j in range(n_high):
            column = pl.multiple_of(((high ^ j) * N_LOW + (low ^ k)) * wide, wide)
            n = p * n_high + j
            copy = pltpu.make_async_copy(acts_ref.at[:, pl.ds(column, wide)], columns.at[n], sems.at[n])
            copy.start()
            copies.append(copy)
    return copies


def grad_kernel(n_high, where_ref, acts_ref, grad_ref, *refs):
    state_refs, refs = refs[:3], refs[3:]
    away, kept, refs = refs[:2], refs[2:4], refs[4:]
    mine_ref, columns, logit_grads, blocks, sems = refs
    high, low, core, rep = [where_ref[i] for i in range(4)]
    half = blocks.shape[2]
    last = sems.shape[0]
    loads = pltpu.make_async_copy(grad_ref, logit_grads, sems.at[last - 1])
    loads.start()
    lows = LOWS[0] + LOWS[1]
    copies = load_columns(acts_ref, columns, sems, high, low, lows, n_high)
    rows = pl.ds(pl.multiple_of(rep * half, half), half)
    state = [
        pltpu.make_async_copy(ref.at[rows], mine_ref.at[i], sems.at[last - 4 + i])
        for i, ref in enumerate(state_refs)
    ]
    for copy in state:
        copy.start()
    loads.wait()
    for n, copy in enumerate(copies):
        copy.wait()
        product = lax.dot_general(
            columns[n], logit_grads[...], (((0,), (0,)), ((), ())), preferred_element_type=jnp.float32
        )
        blocks[...] = product.astype(blocks.dtype).reshape(blocks.shape)
        p, j = divmod(n, n_high)
        for d_rep in range(2):
            for outs, owner in ((kept, core), (away, 1 - core)):
                slot = slot_of((lows[p], d_rep), owner)
                outs[p // 2][slot - 4 * (p // 2), j] = blocks[owner, rep ^ d_rep]
    for copy in state:
        copy.wait()


def columns_kernel(n_high, where_ref, acts_ref, first_ref, second_ref, sems):
    high, low = where_ref[0], where_ref[1]
    copies = []
    for i, (lows, out) in enumerate(zip(LOWS, (first_ref, second_ref))):
        copies += load_columns(acts_ref, out, sems.at[i], high, low, lows, n_high)
    for copy in copies:
        copy.wait()


def logits_kernel(n_high, group, where_ref, columns_ref, *refs):
    *pieces, out_ref, weight = refs
    before = None
    if len(pieces[-1].shape) == 2:
        *pieces, before = pieces
    half, experts = weight.shape[-2:]
    for piece, blocks in zip(pieces, places(group, where_ref[2], where_ref[3])):
        for n, (place, owner, of_rep) in enumerate(blocks):
            for j in range(n_high):
                weight[place, j, owner, of_rep] = piece[n, j]
    total = None if before is None else before[...]
    for n in range(2 * n_high):
        part = jnp.dot(
            columns_ref[n],
            weight[n // n_high, n % n_high].reshape(4 * half, experts),
            preferred_element_type=jnp.float32,
        )
        total = part if total is None else total + part
    out_ref[...] = total.astype(out_ref.dtype)


def places(group, core, rep):
    pieces = []
    for by in (core, 1 - core):
        blocks = []
        for chip in NEXT[:2] if group == 0 else NEXT[2:]:
            place = LOWS[group].index(chip[0]) ^ by
            blocks += [(place, owner, rep ^ chip[1] ^ by) for owner in range(2)]
        if group == 1:
            blocks.append((1, by, rep ^ 1))
        pieces.append(blocks)
    if group == 1:
        pieces += [[(0, owner, rep)] for owner in (core, 1 - core)]
    return pieces


def solution(mesh):
    n_seq, n_rep = mesh.shape["seq"], mesh.shape["rep"]
    n_high = n_seq // (2 * N_LOW)
    fine = Mesh(mesh.devices.reshape(n_high, N_LOW, 2, n_rep), AXES)

    def swap(x, axis, mask=1):
        return lax.ppermute(x, axis, [(i, i ^ mask) for i in range(fine.shape[axis])])

    def cube_swap(x, change):
        pairs = []
        for low in range(N_LOW):
            for core in range(2):
                d_low, d_rep = change(core)
                for rep in range(n_rep):
                    there = ((low ^ d_low) * 2 + core) * n_rep + (rep ^ d_rep)
                    pairs.append(((low * 2 + core) * n_rep + rep, there))
        return lax.ppermute(x, AXES[1:], pairs)

    def to_slot(x, slot):
        return cube_swap(x, lambda core: CHIPS[slot ^ core if slot < 6 else slot])

    def to_next(x, slot):
        d_low, d_rep = NEXT[slot]
        return cube_swap(x, lambda core: (d_low ^ (3 * core), d_rep ^ core))

    def to_corner(x):
        return cube_swap(x, lambda core: (3, 1))

    def per_device(acts, grad_logits, master, moment_one, moment_two, step_count):
        tokens, experts = grad_logits.shape
        rows = master.shape[0]
        half = rows // n_rep
        high, low, core, rep = (lax.axis_index(a) for a in AXES)
        where = jnp.stack([high, low, core, rep])
        f32, bf16 = jnp.float32, jnp.bfloat16
        in_kernels = half % 16 == 0 and (4 * half) % 128 == 0

        smem = pl.BlockSpec(memory_space=pltpu.SMEM)
        vmem = pl.BlockSpec(memory_space=pltpu.VMEM)
        anywhere = pl.BlockSpec(memory_space=pl.ANY)
        params = pltpu.CompilerParams(vmem_limit_bytes=VMEM_LIMIT)
        state_in = (master, moment_one, moment_two)

        if in_kernels:
            acts = pltpu.with_memory_space_constraint(acts, pltpu.HBM)
            shape = pltpu.VMEM((4, n_high, half, experts), bf16)
            *sorted_rows, mine = pl.pallas_call(
                functools.partial(grad_kernel, n_high),
                out_shape=[shape] * 4 + [pltpu.VMEM((3, half, experts), f32)],
                in_specs=[smem] + [anywhere] * 5,
                out_specs=[vmem] * 5,
                scratch_shapes=[
                    pltpu.VMEM((4 * n_high, tokens, 4 * half), bf16),
                    pltpu.VMEM((tokens, experts), bf16),
                    pltpu.VMEM((2, 2, half, experts), bf16),
                    pltpu.SemaphoreType.DMA((4 * n_high + 4,)),
                ],
                compiler_params=params,
            )(
                where,
                acts,
                *(pltpu.with_memory_space_constraint(x, pltpu.HBM) for x in (grad_logits, *state_in)),
            )
            away, kept = sorted_rows[:2], sorted_rows[2:]
        else:
            product = lax.dot_general(
                acts, grad_logits, (((0,), (0,)), ((), ())), preferred_element_type=f32
            ).astype(bf16)
            product = product.reshape(n_high, N_LOW, 2, n_rep, half, experts)
            product = product[high ^ jnp.arange(n_high)]

            def sort_rows(owner):
                blocks = []
                for slot in range(8):
                    flip = owner if slot < 6 else 0
                    d_low, d_rep = CHIPS[slot]
                    at = (0, low ^ d_low ^ (3 * flip), owner, rep ^ d_rep ^ flip, 0, 0)
                    part = lax.dynamic_slice(product, at, (n_high, 1, 1, 1, half, experts))
                    blocks.append(part.reshape(n_high, half, experts))
                return jnp.stack(blocks[:4]), jnp.stack(blocks[4:])

            away, kept = sort_rows(1 - core), sort_rows(core)
            mine = jnp.stack([lax.dynamic_slice_in_dim(x, rep * half, half, 0) for x in state_in])

        parts = []
        for own, theirs in zip(kept, away):
            summed = own.astype(f32) + swap(theirs, "core").astype(f32)
            for n in range(4):
                slot = len(parts)
                parts.append(summed[n] if slot == 7 else to_slot(summed[n].astype(bf16), slot))
        parts = lax.optimization_barrier(parts)
        total = sum(x.astype(f32) for x in parts)

        grad = total[0]
        for j in range(1, n_high):
            grad = grad + swap(total[j].astype(bf16), "high", j).astype(f32)
        weight = adamw(grad, *mine, step_count)[0].astype(bf16)

        column = jnp.stack([swap(weight, "high", j) if j else weight for j in range(n_high)])
        other = swap(grad, "rep")
        corner = to_corner(column)
        across = swap(column, "core")
        across, other = lax.optimization_barrier((across, other))
        chip = jnp.where(core == 0, jnp.stack([column, across]), jnp.stack([across, column]))
        got = [to_next(chip, slot) for slot in range(3)]

        whole = jnp.where(
            rep == 0,
            jnp.concatenate([grad, other], 0),
            jnp.concatenate([other, grad], 0),
        )
        state = adamw(whole, *state_in, step_count)

        columns = [None, None]
        if in_kernels:
            state, late_acts = lax.optimization_barrier((state, acts))
            columns = pl.pallas_call(
                functools.partial(columns_kernel, n_high),
                out_shape=(pltpu.VMEM((2 * n_high, tokens, 4 * half), bf16),) * 2,
                in_specs=[smem, anywhere],
                out_specs=(vmem, vmem),
                scratch_shapes=[pltpu.SemaphoreType.DMA((2, 2 * n_high))],
                compiler_params=params,
            )(where, pltpu.with_memory_space_constraint(late_acts, pltpu.HBM))
        got[0], state, columns = lax.optimization_barrier((got[0], state, columns))
        first, second = jnp.concatenate(got[:2]), jnp.concatenate([got[2], corner[None]])
        first, second = [first, swap(first, "core")], [second, swap(second, "core")]
        second += [column[None], across[None]]
        pieces = (first, second)
        logits = None
        for group, (received, acts_columns) in enumerate(zip(pieces, columns)):
            if in_kernels:
                before = [] if logits is None else [logits]
                operands = [
                    pltpu.with_memory_space_constraint(x, pltpu.VMEM) for x in [acts_columns] + received + before
                ]
                logits = pl.pallas_call(
                    functools.partial(logits_kernel, n_high, group),
                    out_shape=jax.ShapeDtypeStruct((tokens, experts), bf16 if before else f32),
                    in_specs=[smem] + [vmem] * len(operands),
                    out_specs=vmem,
                    scratch_shapes=[pltpu.VMEM((2, n_high, 2, 2, half, experts), bf16)],
                    compiler_params=params,
                )(where, *operands)
            else:
                rows_at, values = [], []
                for piece, blocks in zip(received, places(group, core, rep)):
                    for n, (place, owner, of_rep) in enumerate(blocks):
                        d_low = jnp.array(LOWS[group])[place]
                        for j in range(n_high):
                            at = ((high ^ j) * N_LOW + (low ^ d_low)) * 2 + owner
                            rows_at.append(at * n_rep + of_rep)
                            values.append(piece[n, j])
                full = jnp.zeros((2 * n_seq, half, experts), bf16)
                full = full.at[jnp.stack(rows_at)].set(jnp.stack(values))
                full = full.reshape(n_seq * rows, experts)
                part = jnp.dot(acts, full, preferred_element_type=f32)
                logits = part if logits is None else (logits + part).astype(bf16)
        return *state, logits

    rows_of, tokens_of = P(AXES[:3], None), P(AXES, None)
    return jax.shard_map(
        per_device,
        mesh=fine,
        in_specs=(tokens_of, tokens_of, rows_of, rows_of, rows_of, P()),
        out_specs=(rows_of, rows_of, rows_of, tokens_of),
        check_vma=False,
    )
```

```python
import functools

import jax
import jax.numpy as jnp
from jax import lax
from jax.experimental import pallas as pl
from jax.experimental.pallas import tpu as pltpu
from jax.sharding import Mesh
from jax.sharding import PartitionSpec as P

AXES = ("high", "low", "core", "rep")
N_LOW = 4
CHIPS = ((1, 0), (2, 1), (2, 0), (1, 1), (0, 1), (3, 0), (3, 1), (0, 0))
LOWS = ((1, 2), (0, 3))
NEXT = ((1, 0), (2, 0), (0, 1))
VMEM_LIMIT = 8 * 2**20


def slot_of(chip, core):
    slot = CHIPS.index(chip)
    return slot if slot >= 6 else slot ^ core


def adamw(grad, master, moment_one, moment_two, step_count):
    count = step_count[0].astype(jnp.float32)
    beta_one = 0.9
    beta_two = 0.95
    first = beta_one * moment_one + (1.0 - beta_one) * grad
    second = beta_two * moment_two + (1.0 - beta_two) * grad * grad
    first_hat = first / (1.0 - jnp.power(beta_one, count))
    second_hat = second / (1.0 - jnp.power(beta_two, count))
    updated = master - 0.01 * (first_hat / (jnp.sqrt(second_hat) + 1e-08) + 0.1 * master)
    return updated, first, second


def load_columns(acts_ref, columns, sems, high, low, lows, n_high):
    wide = columns.shape[-1]
    copies = []
    for p, k in enumerate(lows):
        for j in range(n_high):
            column = pl.multiple_of(((high ^ j) * N_LOW + (low ^ k)) * wide, wide)
            n = p * n_high + j
            copy = pltpu.make_async_copy(acts_ref.at[:, pl.ds(column, wide)], columns.at[n], sems.at[n])
            copy.start()
            copies.append(copy)
    return copies


def grad_kernel(n_high, where_ref, acts_ref, grad_ref, *refs):
    state_refs, refs = refs[:3], refs[3:]
    away, kept, refs = refs[:2], refs[2:4], refs[4:]
    mine_ref, columns, logit_grads, blocks, sems = refs
    high, low, core, rep = [where_ref[i] for i in range(4)]
    half = blocks.shape[2]
    last = sems.shape[0]
    loads = pltpu.make_async_copy(grad_ref, logit_grads, sems.at[last - 1])
    loads.start()
    lows = LOWS[0] + LOWS[1]
    copies = load_columns(acts_ref, columns, sems, high, low, lows, n_high)
    rows = pl.ds(pl.multiple_of(rep * half, half), half)
    state = [
        pltpu.make_async_copy(ref.at[rows], mine_ref.at[i], sems.at[last - 4 + i])
        for i, ref in enumerate(state_refs)
    ]
    for copy in state:
        copy.start()
    loads.wait()
    turned = logit_grads[...].T
    for n, copy in enumerate(copies):
        copy.wait()
        product = jnp.dot(turned, columns[n], preferred_element_type=jnp.float32)
        blocks[...] = product.astype(blocks.dtype).T.reshape(blocks.shape)
        p, j = divmod(n, n_high)
        for d_rep in range(2):
            for outs, owner in ((kept, core), (away, 1 - core)):
                slot = slot_of((lows[p], d_rep), owner)
                outs[p // 2][slot - 4 * (p // 2), j] = blocks[owner, rep ^ d_rep]
    for copy in state:
        copy.wait()


def columns_kernel(n_high, where_ref, acts_ref, first_ref, second_ref, sems):
    high, low = where_ref[0], where_ref[1]
    copies = []
    for i, (lows, out) in enumerate(zip(LOWS, (first_ref, second_ref))):
        copies += load_columns(acts_ref, out, sems.at[i], high, low, lows, n_high)
    for copy in copies:
        copy.wait()


def logits_kernel(n_high, group, where_ref, columns_ref, *refs):
    *pieces, out_ref, weight = refs
    before = None
    if len(pieces[-1].shape) == 2:
        *pieces, before = pieces
    half, experts = weight.shape[-2:]
    for piece, blocks in zip(pieces, places(group, where_ref[2], where_ref[3])):
        for n, (place, owner, of_rep) in enumerate(blocks):
            for j in range(n_high):
                weight[place, j, owner, of_rep] = piece[n, j]
    total = None if before is None else before[...]
    for n in range(2 * n_high):
        part = jnp.dot(
            columns_ref[n],
            weight[n // n_high, n % n_high].reshape(4 * half, experts),
            preferred_element_type=jnp.float32,
        )
        total = part if total is None else total + part
    out_ref[...] = total.astype(out_ref.dtype)


def places(group, core, rep):
    pieces = []
    for by in (core, 1 - core):
        blocks = []
        for chip in NEXT[:2] if group == 0 else NEXT[2:]:
            place = LOWS[group].index(chip[0]) ^ by
            blocks += [(place, owner, rep ^ chip[1] ^ by) for owner in range(2)]
        if group == 1:
            blocks.append((1, by, rep ^ 1))
        pieces.append(blocks)
    if group == 1:
        pieces += [[(0, owner, rep)] for owner in (core, 1 - core)]
    return pieces


def solution(mesh):
    n_seq, n_rep = mesh.shape["seq"], mesh.shape["rep"]
    n_high = n_seq // (2 * N_LOW)
    fine = Mesh(mesh.devices.reshape(n_high, N_LOW, 2, n_rep), AXES)

    def swap(x, axis, mask=1):
        return lax.ppermute(x, axis, [(i, i ^ mask) for i in range(fine.shape[axis])])

    def cube_swap(x, change):
        pairs = []
        for low in range(N_LOW):
            for core in range(2):
                d_low, d_rep = change(core)
                for rep in range(n_rep):
                    there = ((low ^ d_low) * 2 + core) * n_rep + (rep ^ d_rep)
                    pairs.append(((low * 2 + core) * n_rep + rep, there))
        return lax.ppermute(x, AXES[1:], pairs)

    def to_slot(x, slot):
        return cube_swap(x, lambda core: CHIPS[slot ^ core if slot < 6 else slot])

    def to_next(x, slot):
        d_low, d_rep = NEXT[slot]
        return cube_swap(x, lambda core: (d_low ^ (3 * core), d_rep ^ core))

    def to_corner(x):
        return cube_swap(x, lambda core: (3, 1))

    def per_device(acts, grad_logits, master, moment_one, moment_two, step_count):
        tokens, experts = grad_logits.shape
        rows = master.shape[0]
        half = rows // n_rep
        high, low, core, rep = (lax.axis_index(a) for a in AXES)
        where = jnp.stack([high, low, core, rep])
        f32, bf16 = jnp.float32, jnp.bfloat16
        in_kernels = half % 16 == 0 and (4 * half) % 128 == 0

        smem = pl.BlockSpec(memory_space=pltpu.SMEM)
        vmem = pl.BlockSpec(memory_space=pltpu.VMEM)
        anywhere = pl.BlockSpec(memory_space=pl.ANY)
        params = pltpu.CompilerParams(vmem_limit_bytes=VMEM_LIMIT)
        state_in = (master, moment_one, moment_two)

        if in_kernels:
            acts = pltpu.with_memory_space_constraint(acts, pltpu.HBM)
            shape = pltpu.VMEM((4, n_high, half, experts), bf16)
            *sorted_rows, mine = pl.pallas_call(
                functools.partial(grad_kernel, n_high),
                out_shape=[shape] * 4 + [pltpu.VMEM((3, half, experts), f32)],
                in_specs=[smem] + [anywhere] * 5,
                out_specs=[vmem] * 5,
                scratch_shapes=[
                    pltpu.VMEM((4 * n_high, tokens, 4 * half), bf16),
                    pltpu.VMEM((tokens, experts), bf16),
                    pltpu.VMEM((2, 2, half, experts), bf16),
                    pltpu.SemaphoreType.DMA((4 * n_high + 4,)),
                ],
                compiler_params=params,
            )(
                where,
                acts,
                *(pltpu.with_memory_space_constraint(x, pltpu.HBM) for x in (grad_logits, *state_in)),
            )
            away, kept = sorted_rows[:2], sorted_rows[2:]
        else:
            product = lax.dot_general(
                acts, grad_logits, (((0,), (0,)), ((), ())), preferred_element_type=f32
            ).astype(bf16)
            product = product.reshape(n_high, N_LOW, 2, n_rep, half, experts)
            product = product[high ^ jnp.arange(n_high)]

            def sort_rows(owner):
                blocks = []
                for slot in range(8):
                    flip = owner if slot < 6 else 0
                    d_low, d_rep = CHIPS[slot]
                    at = (0, low ^ d_low ^ (3 * flip), owner, rep ^ d_rep ^ flip, 0, 0)
                    part = lax.dynamic_slice(product, at, (n_high, 1, 1, 1, half, experts))
                    blocks.append(part.reshape(n_high, half, experts))
                return jnp.stack(blocks[:4]), jnp.stack(blocks[4:])

            away, kept = sort_rows(1 - core), sort_rows(core)
            mine = jnp.stack([lax.dynamic_slice_in_dim(x, rep * half, half, 0) for x in state_in])

        parts = []
        for own, theirs in zip(kept, away):
            summed = own.astype(f32) + swap(theirs, "core").astype(f32)
            for n in range(4):
                slot = len(parts)
                parts.append(summed[n] if slot == 7 else to_slot(summed[n].astype(bf16), slot))
        parts = lax.optimization_barrier(parts)
        total = sum(x.astype(f32) for x in parts)

        grad = total[0]
        for j in range(1, n_high):
            grad = grad + swap(total[j].astype(bf16), "high", j).astype(f32)
        weight = adamw(grad, *mine, step_count)[0].astype(bf16)

        column = jnp.stack([swap(weight, "high", j) if j else weight for j in range(n_high)])
        other = swap(grad, "rep")
        across = swap(column, "core")
        across, other, corner = lax.optimization_barrier((across, other, column))
        corner = to_corner(corner)
        chip = jnp.where(core == 0, jnp.stack([column, across]), jnp.stack([across, column]))
        got = [to_next(chip, slot) for slot in range(3)]

        whole = jnp.where(
            rep == 0,
            jnp.concatenate([grad, other], 0),
            jnp.concatenate([other, grad], 0),
        )
        state = adamw(whole, *state_in, step_count)

        columns = [None, None]
        if in_kernels:
            state, late_acts = lax.optimization_barrier((state, acts))
            columns = pl.pallas_call(
                functools.partial(columns_kernel, n_high),
                out_shape=(pltpu.VMEM((2 * n_high, tokens, 4 * half), bf16),) * 2,
                in_specs=[smem, anywhere],
                out_specs=(vmem, vmem),
                scratch_shapes=[pltpu.SemaphoreType.DMA((2, 2 * n_high))],
                compiler_params=params,
            )(where, pltpu.with_memory_space_constraint(late_acts, pltpu.HBM))
        got[0], state, columns = lax.optimization_barrier((got[0], state, columns))
        first, second = jnp.concatenate(got[:2]), jnp.concatenate([got[2], corner[None]])
        first, second = [first, swap(first, "core")], [second, swap(second, "core")]
        second += [column[None], across[None]]
        pieces = (first, second)
        logits = None
        for group, (received, acts_columns) in enumerate(zip(pieces, columns)):
            if in_kernels:
                before = [] if logits is None else [logits]
                operands = [
                    pltpu.with_memory_space_constraint(x, pltpu.VMEM) for x in [acts_columns] + received + before
                ]
                logits = pl.pallas_call(
                    functools.partial(logits_kernel, n_high, group),
                    out_shape=jax.ShapeDtypeStruct((tokens, experts), bf16 if before else f32),
                    in_specs=[smem] + [vmem] * len(operands),
                    out_specs=vmem,
                    scratch_shapes=[pltpu.VMEM((2, n_high, 2, 2, half, experts), bf16)],
                    compiler_params=params,
                )(where, *operands)
            else:
                rows_at, values = [], []
                for piece, blocks in zip(received, places(group, core, rep)):
                    for n, (place, owner, of_rep) in enumerate(blocks):
                        d_low = jnp.array(LOWS[group])[place]
                        for j in range(n_high):
                            at = ((high ^ j) * N_LOW + (low ^ d_low)) * 2 + owner
                            rows_at.append(at * n_rep + of_rep)
                            values.append(piece[n, j])
                full = jnp.zeros((2 * n_seq, half, experts), bf16)
                full = full.at[jnp.stack(rows_at)].set(jnp.stack(values))
                full = full.reshape(n_seq * rows, experts)
                part = jnp.dot(acts, full, preferred_element_type=f32)
                logits = part if logits is None else (logits + part).astype(bf16)
        return *state, logits

    rows_of, tokens_of = P(AXES[:3], None), P(AXES, None)
    return jax.shard_map(
        per_device,
        mesh=fine,
        in_specs=(tokens_of, tokens_of, rows_of, rows_of, rows_of, P()),
        out_specs=(rows_of, rows_of, rows_of, tokens_of),
        check_vma=False,
    )
```

```python
import functools

import jax
import jax.numpy as jnp
from jax import lax
from jax.experimental import pallas as pl
from jax.experimental.pallas import tpu as pltpu
from jax.sharding import Mesh
from jax.sharding import PartitionSpec as P

AXES = ("high", "low", "core", "rep")
N_LOW = 4
CHIPS = ((1, 0), (2, 1), (2, 0), (1, 1), (0, 1), (3, 0), (3, 1), (0, 0))
LOWS = ((1, 2), (0, 3))
NEXT = ((1, 0), (2, 0), (0, 1))
VMEM_LIMIT = 8 * 2**20


def slot_of(chip, core):
    slot = CHIPS.index(chip)
    return slot if slot >= 6 else slot ^ core


def adamw(grad, master, moment_one, moment_two, step_count):
    count = step_count[0].astype(jnp.float32)
    beta_one = 0.9
    beta_two = 0.95
    first = beta_one * moment_one + (1.0 - beta_one) * grad
    second = beta_two * moment_two + (1.0 - beta_two) * grad * grad
    first_hat = first / (1.0 - jnp.power(beta_one, count))
    second_hat = second / (1.0 - jnp.power(beta_two, count))
    updated = master - 0.01 * (first_hat / (jnp.sqrt(second_hat) + 1e-08) + 0.1 * master)
    return updated, first, second


def load_columns(acts_ref, columns, sems, high, low, lows, n_high):
    wide = columns.shape[-1]
    copies = []
    for p, k in enumerate(lows):
        for j in range(n_high):
            column = pl.multiple_of(((high ^ j) * N_LOW + (low ^ k)) * wide, wide)
            n = p * n_high + j
            copy = pltpu.make_async_copy(acts_ref.at[:, pl.ds(column, wide)], columns.at[n], sems.at[n])
            copy.start()
            copies.append(copy)
    return copies


def sort_products(n_high, group, where_ref, turned, columns, away, kept, blocks, arrived):
    core, rep = where_ref[2], where_ref[3]
    for n in range(2 * n_high):
        arrived(n)
        product = jnp.dot(turned, columns[n], preferred_element_type=jnp.float32)
        blocks[...] = product.astype(blocks.dtype).T.reshape(blocks.shape)
        p, j = divmod(n, n_high)
        for d_rep in range(2):
            for out, owner in ((kept, core), (away, 1 - core)):
                slot = slot_of((LOWS[group][p], d_rep), owner)
                out[slot - 4 * group, j] = blocks[owner, rep ^ d_rep]


def first_grad_kernel(n_high, where_ref, acts_ref, grad_ref, *refs):
    state_refs, refs = refs[:3], refs[3:]
    away, kept, mine_ref, later_ref, turned_ref, columns, logit_grads, blocks, sems = refs
    high, low, _, rep = [where_ref[i] for i in range(4)]
    half = blocks.shape[2]
    loads = pltpu.make_async_copy(grad_ref, logit_grads, sems.at[2, 0])
    loads.start()
    first = load_columns(acts_ref, columns, sems.at[0], high, low, LOWS[1], n_high)
    others = load_columns(acts_ref, later_ref, sems.at[1], high, low, LOWS[0], n_high)
    rows = pl.ds(pl.multiple_of(rep * half, half), half)
    for i, ref in enumerate(state_refs):
        copy = pltpu.make_async_copy(ref.at[rows], mine_ref.at[i], sems.at[2, 1 + i])
        copy.start()
        others.append(copy)
    loads.wait()
    turned = logit_grads[...].T
    turned_ref[...] = turned

    def arrived(n):
        if n % 2 == 0:
            first[n].wait()
            first[n + 1].wait()

    sort_products(n_high, 1, where_ref, turned, columns, away, kept, blocks, arrived)
    for copy in others:
        copy.wait()


def second_grad_kernel(n_high, where_ref, columns, turned_ref, away, kept, blocks):
    sort_products(n_high, 0, where_ref, turned_ref[...], columns, away, kept, blocks, lambda n: None)


def columns_kernel(n_high, where_ref, acts_ref, first_ref, second_ref, sems):
    high, low = where_ref[0], where_ref[1]
    copies = []
    for i, (lows, out) in enumerate(zip(LOWS, (first_ref, second_ref))):
        copies += load_columns(acts_ref, out, sems.at[i], high, low, lows, n_high)
    for copy in copies:
        copy.wait()


def logits_kernel(n_high, group, where_ref, columns_ref, *refs):
    *pieces, out_ref, weight = refs
    before = None
    if len(pieces[-1].shape) == 2:
        *pieces, before = pieces
    half, experts = weight.shape[-2:]
    for piece, blocks in zip(pieces, places(group, where_ref[2], where_ref[3])):
        for n, (place, owner, of_rep) in enumerate(blocks):
            for j in range(n_high):
                weight[place, j, owner, of_rep] = piece[n, j]
    total = None if before is None else before[...]
    for n in range(2 * n_high):
        part = jnp.dot(
            columns_ref[n],
            weight[n // n_high, n % n_high].reshape(4 * half, experts),
            preferred_element_type=jnp.float32,
        )
        total = part if total is None else total + part
    out_ref[...] = total.astype(out_ref.dtype)


def places(group, core, rep):
    pieces = []
    for by in (core, 1 - core):
        blocks = []
        for chip in NEXT[:2] if group == 0 else NEXT[2:]:
            place = LOWS[group].index(chip[0]) ^ by
            blocks += [(place, owner, rep ^ chip[1] ^ by) for owner in range(2)]
        if group == 1:
            blocks.append((1, by, rep ^ 1))
        pieces.append(blocks)
    if group == 1:
        pieces += [[(0, owner, rep)] for owner in (core, 1 - core)]
    return pieces


def solution(mesh):
    n_seq, n_rep = mesh.shape["seq"], mesh.shape["rep"]
    n_high = n_seq // (2 * N_LOW)
    fine = Mesh(mesh.devices.reshape(n_high, N_LOW, 2, n_rep), AXES)

    def swap(x, axis, mask=1):
        return lax.ppermute(x, axis, [(i, i ^ mask) for i in range(fine.shape[axis])])

    def cube_swap(x, change):
        pairs = []
        for low in range(N_LOW):
            for core in range(2):
                d_low, d_rep = change(core)
                for rep in range(n_rep):
                    there = ((low ^ d_low) * 2 + core) * n_rep + (rep ^ d_rep)
                    pairs.append(((low * 2 + core) * n_rep + rep, there))
        return lax.ppermute(x, AXES[1:], pairs)

    def to_slot(x, slot):
        return cube_swap(x, lambda core: CHIPS[slot ^ core if slot < 6 else slot])

    def to_next(x, slot):
        d_low, d_rep = NEXT[slot]
        return cube_swap(x, lambda core: (d_low ^ (3 * core), d_rep ^ core))

    def to_corner(x):
        return cube_swap(x, lambda core: (3, 1))

    def per_device(acts, grad_logits, master, moment_one, moment_two, step_count):
        tokens, experts = grad_logits.shape
        rows = master.shape[0]
        half = rows // n_rep
        high, low, core, rep = (lax.axis_index(a) for a in AXES)
        where = jnp.stack([high, low, core, rep])
        f32, bf16 = jnp.float32, jnp.bfloat16
        in_kernels = half % 16 == 0 and (4 * half) % 128 == 0

        smem = pl.BlockSpec(memory_space=pltpu.SMEM)
        vmem = pl.BlockSpec(memory_space=pltpu.VMEM)
        anywhere = pl.BlockSpec(memory_space=pl.ANY)
        params = pltpu.CompilerParams(vmem_limit_bytes=VMEM_LIMIT)
        state_in = (master, moment_one, moment_two)

        if in_kernels:
            acts = pltpu.with_memory_space_constraint(acts, pltpu.HBM)
            shape = pltpu.VMEM((4, n_high, half, experts), bf16)
            columns_shape = pltpu.VMEM((2 * n_high, tokens, 4 * half), bf16)
            blocks = pltpu.VMEM((2, 2, half, experts), bf16)
            turned = pltpu.VMEM((experts, tokens), bf16)
            away_second, kept_second, mine, later, turned = pl.pallas_call(
                functools.partial(first_grad_kernel, n_high),
                out_shape=[shape, shape, pltpu.VMEM((3, half, experts), f32), columns_shape, turned],
                in_specs=[smem] + [anywhere] * 5,
                out_specs=[vmem] * 5,
                scratch_shapes=[
                    columns_shape,
                    pltpu.VMEM((tokens, experts), bf16),
                    blocks,
                    pltpu.SemaphoreType.DMA((3, max(2 * n_high, 4))),
                ],
                compiler_params=params,
            )(
                where,
                acts,
                *(pltpu.with_memory_space_constraint(x, pltpu.HBM) for x in (grad_logits, *state_in)),
            )
            away_first, kept_first = pl.pallas_call(
                functools.partial(second_grad_kernel, n_high),
                out_shape=[shape, shape],
                in_specs=[smem, vmem, vmem],
                out_specs=[vmem] * 2,
                scratch_shapes=[blocks],
                cost_estimate=pl.CostEstimate(
                    flops=4 * n_high * tokens * experts * 4 * half,
                    bytes_accessed=4 * n_high * tokens * 4 * half,
                    transcendentals=0,
                ),
                compiler_params=params,
            )(where, *(pltpu.with_memory_space_constraint(x, pltpu.VMEM) for x in (later, turned)))
            away, kept = (away_first, away_second), (kept_first, kept_second)
        else:
            product = lax.dot_general(
                acts, grad_logits, (((0,), (0,)), ((), ())), preferred_element_type=f32
            ).astype(bf16)
            product = product.reshape(n_high, N_LOW, 2, n_rep, half, experts)
            product = product[high ^ jnp.arange(n_high)]

            def sort_rows(owner):
                blocks = []
                for slot in range(8):
                    flip = owner if slot < 6 else 0
                    d_low, d_rep = CHIPS[slot]
                    at = (0, low ^ d_low ^ (3 * flip), owner, rep ^ d_rep ^ flip, 0, 0)
                    part = lax.dynamic_slice(product, at, (n_high, 1, 1, 1, half, experts))
                    blocks.append(part.reshape(n_high, half, experts))
                return jnp.stack(blocks[:4]), jnp.stack(blocks[4:])

            away, kept = sort_rows(1 - core), sort_rows(core)
            mine = jnp.stack([lax.dynamic_slice_in_dim(x, rep * half, half, 0) for x in state_in])

        arrived = swap(away[1], "core")
        arrived, away_first = lax.optimization_barrier((arrived, away[0]))
        arrived = swap(away_first, "core"), arrived
        parts = []
        for own, theirs in zip(kept, arrived):
            summed = own.astype(f32) + theirs.astype(f32)
            for n in range(4):
                slot = len(parts)
                parts.append(summed[n] if slot == 7 else to_slot(summed[n].astype(bf16), slot))
        parts = lax.optimization_barrier(parts)
        total = sum(x.astype(f32) for x in parts)

        grad = total[0]
        for j in range(1, n_high):
            grad = grad + swap(total[j].astype(bf16), "high", j).astype(f32)
        weight = adamw(grad, *mine, step_count)[0].astype(bf16)

        column = jnp.stack([swap(weight, "high", j) if j else weight for j in range(n_high)])
        other = swap(grad, "rep")
        across = swap(column, "core")
        across, other = lax.optimization_barrier((across, other))
        corner = to_corner(column)
        chip = jnp.where(core == 0, jnp.stack([column, across]), jnp.stack([across, column]))
        got = [to_next(chip, slot) for slot in range(3)]

        whole = jnp.where(
            rep == 0,
            jnp.concatenate([grad, other], 0),
            jnp.concatenate([other, grad], 0),
        )
        state = adamw(whole, *state_in, step_count)

        columns = [None, None]
        if in_kernels:
            state, late_acts = lax.optimization_barrier((state, acts))
            columns = pl.pallas_call(
                functools.partial(columns_kernel, n_high),
                out_shape=(pltpu.VMEM((2 * n_high, tokens, 4 * half), bf16),) * 2,
                in_specs=[smem, anywhere],
                out_specs=(vmem, vmem),
                scratch_shapes=[pltpu.SemaphoreType.DMA((2, 2 * n_high))],
                compiler_params=params,
            )(where, pltpu.with_memory_space_constraint(late_acts, pltpu.HBM))
        got[0], corner, state, columns = lax.optimization_barrier((got[0], corner, state, columns))
        first, second = jnp.concatenate(got[:2]), jnp.concatenate([got[2], corner[None]])
        first, second = [first, swap(first, "core")], [second, swap(second, "core")]
        second += [column[None], across[None]]
        pieces = (first, second)
        logits = None
        for group, (received, acts_columns) in enumerate(zip(pieces, columns)):
            if in_kernels:
                before = [] if logits is None else [logits]
                operands = [
                    pltpu.with_memory_space_constraint(x, pltpu.VMEM) for x in [acts_columns] + received + before
                ]
                logits = pl.pallas_call(
                    functools.partial(logits_kernel, n_high, group),
                    out_shape=jax.ShapeDtypeStruct((tokens, experts), bf16 if before else f32),
                    in_specs=[smem] + [vmem] * len(operands),
                    out_specs=vmem,
                    scratch_shapes=[pltpu.VMEM((2, n_high, 2, 2, half, experts), bf16)],
                    compiler_params=params,
                )(where, *operands)
            else:
                rows_at, values = [], []
                for piece, blocks in zip(received, places(group, core, rep)):
                    for n, (place, owner, of_rep) in enumerate(blocks):
                        d_low = jnp.array(LOWS[group])[place]
                        for j in range(n_high):
                            at = ((high ^ j) * N_LOW + (low ^ d_low)) * 2 + owner
                            rows_at.append(at * n_rep + of_rep)
                            values.append(piece[n, j])
                full = jnp.zeros((2 * n_seq, half, experts), bf16)
                full = full.at[jnp.stack(rows_at)].set(jnp.stack(values))
                full = full.reshape(n_seq * rows, experts)
                part = jnp.dot(acts, full, preferred_element_type=f32)
                logits = part if logits is None else (logits + part).astype(bf16)
        return *state, logits

    rows_of, tokens_of = P(AXES[:3], None), P(AXES, None)
    return jax.shard_map(
        per_device,
        mesh=fine,
        in_specs=(tokens_of, tokens_of, rows_of, rows_of, rows_of, P()),
        out_specs=(rows_of, rows_of, rows_of, tokens_of),
        check_vma=False,
    )
```

```python
import functools

import jax
import jax.numpy as jnp
from jax import lax
from jax.experimental import pallas as pl
from jax.experimental.pallas import tpu as pltpu
from jax.sharding import Mesh
from jax.sharding import PartitionSpec as P

AXES = ("high", "low", "core", "rep")
N_LOW = 4
NEXT = ((1, 0), (2, 0), (0, 1))
LOWS = ((1, 2), (0, 3))
VMEM_LIMIT = 8 * 2**20


def adamw(grad, master, moment_one, moment_two, step_count):
    count = step_count[0].astype(jnp.float32)
    beta_one = 0.9
    beta_two = 0.95
    first = beta_one * moment_one + (1.0 - beta_one) * grad
    second = beta_two * moment_two + (1.0 - beta_two) * grad * grad
    first_hat = first / (1.0 - jnp.power(beta_one, count))
    second_hat = second / (1.0 - jnp.power(beta_two, count))
    updated = master - 0.01 * (first_hat / (jnp.sqrt(second_hat) + 1e-08) + 0.1 * master)
    return updated, first, second


def load_columns(acts_ref, columns, sems, high, low, lows, n_high):
    wide = columns.shape[-1]
    copies = []
    for p, k in enumerate(lows):
        for j in range(n_high):
            column = pl.multiple_of(((high ^ j) * N_LOW + (low ^ k)) * wide, wide)
            n = p * n_high + j
            copy = pltpu.make_async_copy(acts_ref.at[:, pl.ds(column, wide)], columns.at[n], sems.at[n])
            copy.start()
            copies.append(copy)
    return copies


def grad_lows(group, core):
    return LOWS[0] if group == 0 else (3 * core, 3 * (1 - core))


def sort_products(n_high, group, where_ref, turned, columns, away, kept, blocks, arrived):
    core, rep = where_ref[2], where_ref[3]
    here = rep ^ core
    for n in range(2 * n_high):
        arrived(n)
        product = jnp.dot(turned, columns[n], preferred_element_type=jnp.float32)
        blocks[...] = product.astype(blocks.dtype).T.reshape(blocks.shape)
        p, j = divmod(n, n_high)
        if group == 0:
            for c in range(2):
                kept[p ^ core, c, j] = blocks[c, here]
                away[p ^ core ^ 1, c, j] = blocks[c, here ^ 1]
        else:
            slot = kept if p == 0 else away
            for c in range(2):
                slot[c, j] = blocks[c, here ^ 1 ^ p]
            at = 3 - core if p == 0 else 2 + core
            kept[at, j] = blocks[core, here ^ p]
            away[at, j] = blocks[1 - core, here ^ p]


def first_grad_kernel(n_high, where_ref, acts_ref, grad_ref, *refs):
    state_refs, refs = refs[:3], refs[3:]
    away, kept, mine_ref, later_ref, turned_ref, columns, logit_grads, blocks, sems = refs
    high, low, core, rep = [where_ref[i] for i in range(4)]
    half = blocks.shape[2]
    loads = pltpu.make_async_copy(grad_ref, logit_grads, sems.at[2, 0])
    loads.start()
    first = load_columns(acts_ref, columns, sems.at[0], high, low, grad_lows(1, core), n_high)
    others = load_columns(acts_ref, later_ref, sems.at[1], high, low, grad_lows(0, core), n_high)
    rows = pl.ds(pl.multiple_of(rep * half, half), half)
    for i, ref in enumerate(state_refs):
        copy = pltpu.make_async_copy(ref.at[rows], mine_ref.at[i], sems.at[2, 1 + i])
        copy.start()
        others.append(copy)
    loads.wait()
    turned = logit_grads[...].T
    turned_ref[...] = turned

    def arrived(n):
        if n % 2 == 0:
            first[n].wait()
            first[n + 1].wait()

    sort_products(n_high, 1, where_ref, turned, columns, away, kept, blocks, arrived)
    for copy in others:
        copy.wait()


def second_grad_kernel(n_high, where_ref, columns, turned_ref, away, kept, blocks):
    sort_products(n_high, 0, where_ref, turned_ref[...], columns, away, kept, blocks, lambda n: None)


def columns_kernel(n_high, where_ref, acts_ref, first_ref, second_ref, sems):
    high, low = where_ref[0], where_ref[1]
    copies = []
    for i, (lows, out) in enumerate(zip(LOWS, (first_ref, second_ref))):
        copies += load_columns(acts_ref, out, sems.at[i], high, low, lows, n_high)
    for copy in copies:
        copy.wait()


def logits_kernel(n_high, group, where_ref, columns_ref, *refs):
    *pieces, out_ref, weight = refs
    before = None
    if len(pieces[-1].shape) == 2:
        *pieces, before = pieces
    half, experts = weight.shape[-2:]
    for piece, blocks in zip(pieces, places(group, where_ref[2], where_ref[3])):
        for n, (place, owner, of_rep) in enumerate(blocks):
            for j in range(n_high):
                weight[place, j, owner, of_rep] = piece[n, j]
    total = None if before is None else before[...]
    for n in range(2 * n_high):
        part = jnp.dot(
            columns_ref[n],
            weight[n // n_high, n % n_high].reshape(4 * half, experts),
            preferred_element_type=jnp.float32,
        )
        total = part if total is None else total + part
    out_ref[...] = total.astype(out_ref.dtype)


def places(group, core, rep):
    pieces = []
    for by in (core, 1 - core):
        blocks = []
        for chip in NEXT[:2] if group == 0 else NEXT[2:]:
            place = LOWS[group].index(chip[0]) ^ by
            blocks += [(place, owner, rep ^ chip[1] ^ by) for owner in range(2)]
        if group == 1:
            blocks.append((1, by, rep ^ 1))
        pieces.append(blocks)
    if group == 1:
        pieces += [[(0, owner, rep)] for owner in (core, 1 - core)]
    return pieces


def solution(mesh):
    n_seq, n_rep = mesh.shape["seq"], mesh.shape["rep"]
    n_high = n_seq // (2 * N_LOW)
    fine = Mesh(mesh.devices.reshape(n_high, N_LOW, 2, n_rep), AXES)

    def swap(x, axis, mask=1):
        return lax.ppermute(x, axis, [(i, i ^ mask) for i in range(fine.shape[axis])])

    def cube_swap(x, change):
        pairs = []
        for low in range(N_LOW):
            for core in range(2):
                d_low, d_rep = change(core)
                for rep in range(n_rep):
                    there = ((low ^ d_low) * 2 + core) * n_rep + (rep ^ d_rep)
                    pairs.append(((low * 2 + core) * n_rep + rep, there))
        return lax.ppermute(x, AXES[1:], pairs)

    def to_next(x, slot):
        d_low, d_rep = NEXT[slot]
        return cube_swap(x, lambda core: (d_low ^ (3 * core), d_rep ^ core))

    def to_corner(x):
        return cube_swap(x, lambda core: (3, 1))

    def per_device(acts, grad_logits, master, moment_one, moment_two, step_count):
        tokens, experts = grad_logits.shape
        rows = master.shape[0]
        half = rows // n_rep
        high, low, core, rep = (lax.axis_index(a) for a in AXES)
        where = jnp.stack([high, low, core, rep])
        f32, bf16 = jnp.float32, jnp.bfloat16
        in_kernels = half % 16 == 0 and (4 * half) % 128 == 0

        smem = pl.BlockSpec(memory_space=pltpu.SMEM)
        vmem = pl.BlockSpec(memory_space=pltpu.VMEM)
        anywhere = pl.BlockSpec(memory_space=pl.ANY)
        params = pltpu.CompilerParams(vmem_limit_bytes=VMEM_LIMIT)
        state_in = (master, moment_one, moment_two)

        if in_kernels:
            acts = pltpu.with_memory_space_constraint(acts, pltpu.HBM)
            first = pltpu.VMEM((2, 2, n_high, half, experts), bf16)
            second = pltpu.VMEM((4, n_high, half, experts), bf16)
            columns_shape = pltpu.VMEM((2 * n_high, tokens, 4 * half), bf16)
            blocks = pltpu.VMEM((2, 2, half, experts), bf16)
            turned = pltpu.VMEM((experts, tokens), bf16)
            away_second, kept_second, mine, later, turned = pl.pallas_call(
                functools.partial(first_grad_kernel, n_high),
                out_shape=[second, second, pltpu.VMEM((3, half, experts), f32), columns_shape, turned],
                in_specs=[smem] + [anywhere] * 5,
                out_specs=[vmem] * 5,
                scratch_shapes=[
                    columns_shape,
                    pltpu.VMEM((tokens, experts), bf16),
                    blocks,
                    pltpu.SemaphoreType.DMA((3, max(2 * n_high, 4))),
                ],
                compiler_params=params,
            )(
                where,
                acts,
                *(pltpu.with_memory_space_constraint(x, pltpu.HBM) for x in (grad_logits, *state_in)),
            )
            away_first, kept_first = pl.pallas_call(
                functools.partial(second_grad_kernel, n_high),
                out_shape=[first, first],
                in_specs=[smem, vmem, vmem],
                out_specs=[vmem] * 2,
                scratch_shapes=[blocks],
                cost_estimate=pl.CostEstimate(
                    flops=4 * n_high * tokens * experts * 4 * half,
                    bytes_accessed=4 * n_high * tokens * 4 * half,
                    transcendentals=0,
                ),
                compiler_params=params,
            )(where, *(pltpu.with_memory_space_constraint(x, pltpu.VMEM) for x in (later, turned)))
            away, kept = (away_first, away_second), (kept_first, kept_second)
        else:
            product = lax.dot_general(
                acts, grad_logits, (((0,), (0,)), ((), ())), preferred_element_type=f32
            ).astype(bf16)
            product = product.reshape(n_high, N_LOW, 2, n_rep, half, experts)
            product = product[high ^ jnp.arange(n_high)]

            def block(d_low, owner, d_rep):
                at = (0, low ^ d_low, owner, rep ^ d_rep, 0, 0)
                part = lax.dynamic_slice(product, at, (n_high, 1, 1, 1, half, experts))
                return part.reshape(n_high, half, experts)

            def sort_rows(by):
                slots = [
                    jnp.stack([block(d_low ^ (3 * by), c, d_rep ^ by) for c in range(2)])
                    for d_low, d_rep in NEXT
                ]
                rest = [slots[2], block(3, by, 1)[None], block(0, by, 0)[None]]
                return jnp.stack(slots[:2]), jnp.concatenate(rest)

            away, kept = sort_rows(1 - core), sort_rows(core)
            mine = jnp.stack([lax.dynamic_slice_in_dim(x, rep * half, half, 0) for x in state_in])

        arrived = swap(away[1], "core")
        arrived, away_first = lax.optimization_barrier((arrived, away[0]))
        arrived = swap(away_first, "core"), arrived
        first, second = [x.astype(f32) + y.astype(f32) for x, y in zip(kept, arrived)]
        slots = [first[0], first[1], second[:2]]
        slots = [to_next(x.astype(bf16), slot) for slot, x in enumerate(slots)]
        corner = to_corner(second[2].astype(bf16))
        home = second[3]
        *slots, corner = [x.astype(f32) for x in lax.optimization_barrier((*slots, corner))]
        total = slots[0] + slots[1] + slots[2]
        theirs = swap(lax.dynamic_index_in_dim(total, 1 - core, 0, keepdims=False), "core")
        total = lax.dynamic_index_in_dim(total, core, 0, keepdims=False) + theirs + home + corner

        grad = total[0]
        for j in range(1, n_high):
            grad = grad + swap(total[j].astype(bf16), "high", j).astype(f32)
        weight = adamw(grad, *mine, step_count)[0].astype(bf16)

        column = jnp.stack([swap(weight, "high", j) if j else weight for j in range(n_high)])
        other = swap(grad, "rep")
        across = swap(column, "core")
        across, other, late_column = lax.optimization_barrier((across, other, column))
        corner = to_corner(late_column)
        chip = jnp.where(core == 0, jnp.stack([column, across]), jnp.stack([across, column]))
        got = [to_next(chip, slot) for slot in range(3)]

        whole = jnp.where(
            rep == 0,
            jnp.concatenate([grad, other], 0),
            jnp.concatenate([other, grad], 0),
        )
        state = adamw(whole, *state_in, step_count)

        columns = [None, None]
        if in_kernels:
            state, late_acts = lax.optimization_barrier((state, acts))
            columns = pl.pallas_call(
                functools.partial(columns_kernel, n_high),
                out_shape=(pltpu.VMEM((2 * n_high, tokens, 4 * half), bf16),) * 2,
                in_specs=[smem, anywhere],
                out_specs=(vmem, vmem),
                scratch_shapes=[pltpu.SemaphoreType.DMA((2, 2 * n_high))],
                compiler_params=params,
            )(where, pltpu.with_memory_space_constraint(late_acts, pltpu.HBM))
        got[0], corner, state, columns = lax.optimization_barrier((got[0], corner, state, columns))
        first, second = jnp.concatenate(got[:2]), jnp.concatenate([got[2], corner[None]])
        first, second = [first, swap(first, "core")], [second, swap(second, "core")]
        second += [column[None], across[None]]
        pieces = (first, second)
        logits = None
        for group, (received, acts_columns) in enumerate(zip(pieces, columns)):
            if in_kernels:
                before = [] if logits is None else [logits]
                operands = [
                    pltpu.with_memory_space_constraint(x, pltpu.VMEM) for x in [acts_columns] + received + before
                ]
                logits = pl.pallas_call(
                    functools.partial(logits_kernel, n_high, group),
                    out_shape=jax.ShapeDtypeStruct((tokens, experts), bf16 if before else f32),
                    in_specs=[smem] + [vmem] * len(operands),
                    out_specs=vmem,
                    scratch_shapes=[pltpu.VMEM((2, n_high, 2, 2, half, experts), bf16)],
                    compiler_params=params,
                )(where, *operands)
            else:
                rows_at, values = [], []
                for piece, blocks in zip(received, places(group, core, rep)):
                    for n, (place, owner, of_rep) in enumerate(blocks):
                        d_low = jnp.array(LOWS[group])[place]
                        for j in range(n_high):
                            at = ((high ^ j) * N_LOW + (low ^ d_low)) * 2 + owner
                            rows_at.append(at * n_rep + of_rep)
                            values.append(piece[n, j])
                full = jnp.zeros((2 * n_seq, half, experts), bf16)
                full = full.at[jnp.stack(rows_at)].set(jnp.stack(values))
                full = full.reshape(n_seq * rows, experts)
                part = jnp.dot(acts, full, preferred_element_type=f32)
                logits = part if logits is None else (logits + part).astype(bf16)
        return *state, logits

    rows_of, tokens_of = P(AXES[:3], None), P(AXES, None)
    return jax.shard_map(
        per_device,
        mesh=fine,
        in_specs=(tokens_of, tokens_of, rows_of, rows_of, rows_of, P()),
        out_specs=(rows_of, rows_of, rows_of, tokens_of),
        check_vma=False,
    )
```

```python
import functools

import jax
import jax.numpy as jnp
from jax import lax
from jax.experimental import pallas as pl
from jax.experimental.pallas import tpu as pltpu
from jax.sharding import Mesh
from jax.sharding import PartitionSpec as P

AXES = ("high", "low", "core", "rep")
N_LOW = 4
CHIPS = ((1, 0), (2, 1), (2, 0), (1, 1), (0, 1), (3, 0), (3, 1), (0, 0))
LOWS = ((1, 2), (0, 3))
NEXT = ((1, 0), (2, 0), (0, 1))
VMEM_LIMIT = 8 * 2**20


def slot_of(chip, core):
    slot = CHIPS.index(chip)
    return slot if slot >= 6 else slot ^ core


def position():
    return [lax.axis_index(axis) for axis in AXES]


def adamw(grad, master, moment_one, moment_two, step_count):
    count = step_count[0].astype(jnp.float32)
    beta_one = 0.9
    beta_two = 0.95
    first = beta_one * moment_one + (1.0 - beta_one) * grad
    second = beta_two * moment_two + (1.0 - beta_two) * grad * grad
    first_hat = first / (1.0 - jnp.power(beta_one, count))
    second_hat = second / (1.0 - jnp.power(beta_two, count))
    updated = master - 0.01 * (first_hat / (jnp.sqrt(second_hat) + 1e-08) + 0.1 * master)
    return updated, first, second


def load_columns(acts_ref, slices, sems, lows, n_high, wide):
    high, low, _, _ = position()
    copies = []
    for p, k in enumerate(lows):
        for j in range(n_high):
            column = pl.multiple_of(((high ^ j) * N_LOW + (low ^ k)) * wide, wide)
            n = p * n_high + j
            copy = pltpu.make_async_copy(acts_ref.at[:, pl.ds(column, wide)], slices(n), sems.at[n])
            copy.start()
            copies.append(copy)
    return copies


def sort_products(n_high, group, turned, columns, away, kept, blocks, arrived):
    _, _, core, rep = position()
    for n in range(2 * n_high):
        arrived(n)
        product = jnp.dot(turned, columns[n], preferred_element_type=jnp.float32)
        blocks[...] = product.astype(blocks.dtype).T.reshape(blocks.shape)
        p, j = divmod(n, n_high)
        for d_rep in range(2):
            for out, owner in ((kept, core), (away, 1 - core)):
                slot = slot_of((LOWS[group][p], d_rep), owner)
                out[slot - 4 * group, j] = blocks[owner, rep ^ d_rep]


def first_grad_kernel(n_high, acts_ref, grad_ref, *refs):
    state_refs, refs = refs[:3], refs[3:]
    away, kept, mine_ref, later_ref, turned_ref, columns, logit_grads, blocks, sems = refs
    _, _, _, rep = position()
    half = blocks.shape[2]
    loads = pltpu.make_async_copy(grad_ref, logit_grads, sems.at[2, 0])
    loads.start()
    first = load_columns(acts_ref, lambda n: columns.at[n], sems.at[0], LOWS[1], n_high, 4 * half)
    others = load_columns(acts_ref, lambda n: later_ref.at[n], sems.at[1], LOWS[0], n_high, 4 * half)
    rows = pl.ds(pl.multiple_of(rep * half, half), half)
    for i, ref in enumerate(state_refs):
        copy = pltpu.make_async_copy(ref.at[rows], mine_ref.at[i], sems.at[2, 1 + i])
        copy.start()
        others.append(copy)
    loads.wait()
    turned = logit_grads[...].T
    turned_ref[...] = turned

    def arrived(n):
        if n % 2 == 0:
            first[n].wait()
            first[n + 1].wait()

    sort_products(n_high, 1, turned, columns, away, kept, blocks, arrived)
    for copy in others:
        copy.wait()


def second_grad_kernel(n_high, columns, turned_ref, away, kept, blocks):
    sort_products(n_high, 0, turned_ref[...], columns, away, kept, blocks, lambda n: None)


def columns_kernel(n_high, wide, acts_ref, first_ref, second_ref, sems):
    copies = []
    for i, (lows, out) in enumerate(zip(LOWS, (first_ref, second_ref))):
        slices = lambda n, out=out: out.at[:, pl.ds(n * wide, wide)]
        copies += load_columns(acts_ref, slices, sems.at[i], lows, n_high, wide)
    for copy in copies:
        copy.wait()


def logits_kernel(n_high, group, columns_ref, *refs):
    *pieces, out_ref, weight = refs
    before = None
    if len(pieces[-1].shape) == 2:
        *pieces, before = pieces
    _, _, core, rep = position()
    half, experts = weight.shape[-2:]
    for piece, blocks in zip(pieces, places(group, core, rep)):
        for n, (place, owner, of_rep) in enumerate(blocks):
            for j in range(n_high):
                weight[place, j, owner, of_rep] = piece[n, j]
    total = jnp.dot(
        columns_ref[...],
        weight[...].reshape(8 * n_high * half, experts),
        preferred_element_type=jnp.float32,
    )
    if before is not None:
        total = total + before[...]
    out_ref[...] = total.astype(out_ref.dtype)


def places(group, core, rep):
    pieces = []
    for by in (core, 1 - core):
        blocks = []
        for chip in NEXT[:2] if group == 0 else NEXT[2:]:
            place = LOWS[group].index(chip[0]) ^ by
            blocks += [(place, owner, rep ^ chip[1] ^ by) for owner in range(2)]
        if group == 1:
            blocks.append((1, by, rep ^ 1))
        pieces.append(blocks)
    if group == 1:
        pieces += [[(0, owner, rep)] for owner in (core, 1 - core)]
    return pieces


def solution(mesh):
    n_seq, n_rep = mesh.shape["seq"], mesh.shape["rep"]
    n_high = n_seq // (2 * N_LOW)
    fine = Mesh(mesh.devices.reshape(n_high, N_LOW, 2, n_rep), AXES)

    def swap(x, axis, mask=1):
        return lax.ppermute(x, axis, [(i, i ^ mask) for i in range(fine.shape[axis])])

    def cube_swap(x, change):
        pairs = []
        for low in range(N_LOW):
            for core in range(2):
                d_low, d_rep = change(core)
                for rep in range(n_rep):
                    there = ((low ^ d_low) * 2 + core) * n_rep + (rep ^ d_rep)
                    pairs.append(((low * 2 + core) * n_rep + rep, there))
        return lax.ppermute(x, AXES[1:], pairs)

    def to_slot(x, slot):
        return cube_swap(x, lambda core: CHIPS[slot ^ core if slot < 6 else slot])

    def to_next(x, slot):
        d_low, d_rep = NEXT[slot]
        return cube_swap(x, lambda core: (d_low ^ (3 * core), d_rep ^ core))

    def to_corner(x):
        return cube_swap(x, lambda core: (3, 1))

    def per_device(acts, grad_logits, master, moment_one, moment_two, step_count):
        tokens, experts = grad_logits.shape
        rows = master.shape[0]
        half = rows // n_rep
        high, low, core, rep = position()
        f32, bf16 = jnp.float32, jnp.bfloat16
        in_kernels = half % 16 == 0 and (4 * half) % 128 == 0

        vmem = pl.BlockSpec(memory_space=pltpu.VMEM)
        anywhere = pl.BlockSpec(memory_space=pl.ANY)
        params = pltpu.CompilerParams(vmem_limit_bytes=VMEM_LIMIT)
        state_in = (master, moment_one, moment_two)

        if in_kernels:
            acts = pltpu.with_memory_space_constraint(acts, pltpu.HBM)
            shape = pltpu.VMEM((4, n_high, half, experts), bf16)
            columns_shape = pltpu.VMEM((2 * n_high, tokens, 4 * half), bf16)
            blocks = pltpu.VMEM((2, 2, half, experts), bf16)
            turned = pltpu.VMEM((experts, tokens), bf16)
            away_second, kept_second, mine, later, turned = pl.pallas_call(
                functools.partial(first_grad_kernel, n_high),
                out_shape=[shape, shape, pltpu.VMEM((3, half, experts), f32), columns_shape, turned],
                in_specs=[anywhere] * 5,
                out_specs=[vmem] * 5,
                scratch_shapes=[
                    columns_shape,
                    pltpu.VMEM((tokens, experts), bf16),
                    blocks,
                    pltpu.SemaphoreType.DMA((3, max(2 * n_high, 4))),
                ],
                compiler_params=params,
            )(
                acts,
                *(pltpu.with_memory_space_constraint(x, pltpu.HBM) for x in (grad_logits, *state_in)),
            )
            away_first, kept_first = pl.pallas_call(
                functools.partial(second_grad_kernel, n_high),
                out_shape=[shape, shape],
                in_specs=[vmem, vmem],
                out_specs=[vmem] * 2,
                scratch_shapes=[blocks],
                cost_estimate=pl.CostEstimate(
                    flops=4 * n_high * tokens * experts * 4 * half,
                    bytes_accessed=4 * n_high * tokens * 4 * half,
                    transcendentals=0,
                ),
                compiler_params=params,
            )(*(pltpu.with_memory_space_constraint(x, pltpu.VMEM) for x in (later, turned)))
            away, kept = (away_first, away_second), (kept_first, kept_second)
        else:
            product = lax.dot_general(
                acts, grad_logits, (((0,), (0,)), ((), ())), preferred_element_type=f32
            ).astype(bf16)
            product = product.reshape(n_high, N_LOW, 2, n_rep, half, experts)
            product = product[high ^ jnp.arange(n_high)]

            def sort_rows(owner):
                blocks = []
                for slot in range(8):
                    flip = owner if slot < 6 else 0
                    d_low, d_rep = CHIPS[slot]
                    at = (0, low ^ d_low ^ (3 * flip), owner, rep ^ d_rep ^ flip, 0, 0)
                    part = lax.dynamic_slice(product, at, (n_high, 1, 1, 1, half, experts))
                    blocks.append(part.reshape(n_high, half, experts))
                return jnp.stack(blocks[:4]), jnp.stack(blocks[4:])

            away, kept = sort_rows(1 - core), sort_rows(core)
            mine = jnp.stack([lax.dynamic_slice_in_dim(x, rep * half, half, 0) for x in state_in])

        arrived = swap(away[1], "core")
        arrived, away_first = lax.optimization_barrier((arrived, away[0]))
        arrived = swap(away_first, "core"), arrived
        parts = []
        for own, theirs in zip(kept, arrived):
            summed = own.astype(f32) + theirs.astype(f32)
            for n in range(4):
                slot = len(parts)
                parts.append(summed[n] if slot == 7 else to_slot(summed[n].astype(bf16), slot))
        parts = lax.optimization_barrier(parts)
        total = sum(x.astype(f32) for x in parts)

        grad = total[0]
        for j in range(1, n_high):
            grad = grad + swap(total[j].astype(bf16), "high", j).astype(f32)
        weight = adamw(grad, *mine, step_count)[0].astype(bf16)

        column = jnp.stack([swap(weight, "high", j) if j else weight for j in range(n_high)])
        other = swap(grad, "rep")
        across = swap(column, "core")
        across, other = lax.optimization_barrier((across, other))
        corner = to_corner(column)
        chip = jnp.where(core == 0, jnp.stack([column, across]), jnp.stack([across, column]))
        got = [to_next(chip, slot) for slot in range(3)]

        whole = jnp.where(
            rep == 0,
            jnp.concatenate([grad, other], 0),
            jnp.concatenate([other, grad], 0),
        )
        state = adamw(whole, *state_in, step_count)

        columns = [None, None]
        if in_kernels:
            state, late_acts = lax.optimization_barrier((state, acts))
            columns = pl.pallas_call(
                functools.partial(columns_kernel, n_high, 4 * half),
                out_shape=(pltpu.VMEM((tokens, 8 * n_high * half), bf16),) * 2,
                in_specs=[anywhere],
                out_specs=(vmem, vmem),
                scratch_shapes=[pltpu.SemaphoreType.DMA((2, 2 * n_high))],
                compiler_params=params,
            )(pltpu.with_memory_space_constraint(late_acts, pltpu.HBM))
        got[0], corner, state, columns = lax.optimization_barrier((got[0], corner, state, columns))
        first, second = jnp.concatenate(got[:2]), jnp.concatenate([got[2], corner[None]])
        first, second = [first, swap(first, "core")], [second, swap(second, "core")]
        second += [column[None], across[None]]
        pieces = (first, second)
        logits = None
        for group, (received, acts_columns) in enumerate(zip(pieces, columns)):
            if in_kernels:
                before = [] if logits is None else [logits]
                operands = [
                    pltpu.with_memory_space_constraint(x, pltpu.VMEM) for x in [acts_columns] + received + before
                ]
                logits = pl.pallas_call(
                    functools.partial(logits_kernel, n_high, group),
                    out_shape=jax.ShapeDtypeStruct((tokens, experts), bf16 if before else f32),
                    in_specs=[vmem] * len(operands),
                    out_specs=vmem,
                    scratch_shapes=[pltpu.VMEM((2, n_high, 2, 2, half, experts), bf16)],
                    compiler_params=params,
                )(*operands)
            else:
                rows_at, values = [], []
                for piece, blocks in zip(received, places(group, core, rep)):
                    for n, (place, owner, of_rep) in enumerate(blocks):
                        d_low = jnp.array(LOWS[group])[place]
                        for j in range(n_high):
                            at = ((high ^ j) * N_LOW + (low ^ d_low)) * 2 + owner
                            rows_at.append(at * n_rep + of_rep)
                            values.append(piece[n, j])
                full = jnp.zeros((2 * n_seq, half, experts), bf16)
                full = full.at[jnp.stack(rows_at)].set(jnp.stack(values))
                full = full.reshape(n_seq * rows, experts)
                part = jnp.dot(acts, full, preferred_element_type=f32)
                logits = part if logits is None else (logits + part).astype(bf16)
        return *state, logits

    rows_of, tokens_of = P(AXES[:3], None), P(AXES, None)
    return jax.shard_map(
        per_device,
        mesh=fine,
        in_specs=(tokens_of, tokens_of, rows_of, rows_of, rows_of, P()),
        out_specs=(rows_of, rows_of, rows_of, tokens_of),
        check_vma=False,
    )
```

```python
import functools

import jax
import jax.numpy as jnp
from jax import lax
from jax.experimental import pallas as pl
from jax.experimental.pallas import tpu as pltpu
from jax.sharding import Mesh
from jax.sharding import PartitionSpec as P

AXES = ("high", "low", "core", "rep")
N_LOW = 4
CHIPS = ((1, 0), (2, 1), (2, 0), (1, 1), (0, 1), (3, 0), (3, 1), (0, 0))
LOWS = ((1, 2), (0, 3))
GATHERED = (((1, 0), (2, 0), (1, 1), (2, 1)), ((0, 1), (3, 0), (3, 1)))
VMEM_LIMIT = 8 * 2**20


def slot_of(chip, core):
    slot = CHIPS.index(chip)
    return slot if slot >= 6 else slot ^ core


def position():
    return [lax.axis_index(axis) for axis in AXES]


def adamw(grad, master, moment_one, moment_two, step_count):
    count = step_count[0].astype(jnp.float32)
    beta_one = 0.9
    beta_two = 0.95
    first = beta_one * moment_one + (1.0 - beta_one) * grad
    second = beta_two * moment_two + (1.0 - beta_two) * grad * grad
    first_hat = first / (1.0 - jnp.power(beta_one, count))
    second_hat = second / (1.0 - jnp.power(beta_two, count))
    updated = master - 0.01 * (first_hat / (jnp.sqrt(second_hat) + 1e-08) + 0.1 * master)
    return updated, first, second


def load_columns(acts_ref, slices, sems, lows, n_high, wide):
    high, low, _, _ = position()
    copies = []
    for p, k in enumerate(lows):
        for j in range(n_high):
            column = pl.multiple_of(((high ^ j) * N_LOW + (low ^ k)) * wide, wide)
            n = p * n_high + j
            copy = pltpu.make_async_copy(acts_ref.at[:, pl.ds(column, wide)], slices(n), sems.at[n])
            copy.start()
            copies.append(copy)
    return copies


def sort_products(n_high, group, turned, columns, away, kept, blocks, arrived):
    _, _, core, rep = position()
    for n in range(2 * n_high):
        arrived(n)
        product = jnp.dot(turned, columns[n], preferred_element_type=jnp.float32)
        blocks[...] = product.astype(blocks.dtype).T.reshape(blocks.shape)
        p, j = divmod(n, n_high)
        for d_rep in range(2):
            for out, owner in ((kept, core), (away, 1 - core)):
                slot = slot_of((LOWS[group][p], d_rep), owner)
                out[slot - 4 * group, j] = blocks[owner, rep ^ d_rep]


def first_grad_kernel(n_high, acts_ref, grad_ref, *refs):
    state_refs, refs = refs[:3], refs[3:]
    away, kept, mine_ref, later_ref, turned_ref, columns, logit_grads, blocks, sems = refs
    _, _, _, rep = position()
    half = blocks.shape[2]
    loads = pltpu.make_async_copy(grad_ref, logit_grads, sems.at[2, 0])
    loads.start()
    first = load_columns(acts_ref, lambda n: columns.at[n], sems.at[0], LOWS[1], n_high, 4 * half)
    others = load_columns(acts_ref, lambda n: later_ref.at[n], sems.at[1], LOWS[0], n_high, 4 * half)
    rows = pl.ds(pl.multiple_of(rep * half, half), half)
    for i, ref in enumerate(state_refs):
        copy = pltpu.make_async_copy(ref.at[rows], mine_ref.at[i], sems.at[2, 1 + i])
        copy.start()
        others.append(copy)
    loads.wait()
    turned = logit_grads[...].T
    turned_ref[...] = turned

    def arrived(n):
        if n % 2 == 0:
            first[n].wait()
            first[n + 1].wait()

    sort_products(n_high, 1, turned, columns, away, kept, blocks, arrived)
    for copy in others:
        copy.wait()


def second_grad_kernel(n_high, columns, turned_ref, away, kept, blocks):
    sort_products(n_high, 0, turned_ref[...], columns, away, kept, blocks, lambda n: None)


def columns_kernel(n_high, wide, acts_ref, first_ref, second_ref, sems):
    copies = []
    for i, (lows, out) in enumerate(zip(LOWS, (first_ref, second_ref))):
        slices = lambda n, out=out: out.at[:, pl.ds(n * wide, wide)]
        copies += load_columns(acts_ref, slices, sems.at[i], lows, n_high, wide)
    for copy in copies:
        copy.wait()


def logits_kernel(n_high, group, columns_ref, *refs):
    *pieces, out_ref, weight = refs
    before = None
    if len(pieces[-1].shape) == 2:
        *pieces, before = pieces
    _, _, core, rep = position()
    half, experts = weight.shape[-2:]
    for piece, blocks in zip(pieces, places(group, core, rep)):
        for n, (place, owner, of_rep) in enumerate(blocks):
            for j in range(n_high):
                weight[place, j, owner, of_rep] = piece[n, j]
    total = jnp.dot(
        columns_ref[...],
        weight[...].reshape(8 * n_high * half, experts),
        preferred_element_type=jnp.float32,
    )
    if before is not None:
        total = total + before[...]
    out_ref[...] = total.astype(out_ref.dtype)


def places(group, core, rep):
    pieces = []
    for owner in (core, 1 - core):
        pieces.append([(LOWS[group].index(low), owner, rep ^ d_rep) for low, d_rep in GATHERED[group]])
    if group == 1:
        pieces += [[(0, owner, rep)] for owner in (core, 1 - core)]
    return pieces


def solution(mesh):
    n_seq, n_rep = mesh.shape["seq"], mesh.shape["rep"]
    n_high = n_seq // (2 * N_LOW)
    fine = Mesh(mesh.devices.reshape(n_high, N_LOW, 2, n_rep), AXES)

    def swap(x, axis, mask=1):
        return lax.ppermute(x, axis, [(i, i ^ mask) for i in range(fine.shape[axis])])

    def cube_swap(x, change):
        pairs = []
        for low in range(N_LOW):
            for core in range(2):
                d_low, d_rep = change(core)
                for rep in range(n_rep):
                    there = ((low ^ d_low) * 2 + core) * n_rep + (rep ^ d_rep)
                    pairs.append(((low * 2 + core) * n_rep + rep, there))
        return lax.ppermute(x, AXES[1:], pairs)

    def to_slot(x, slot):
        return cube_swap(x, lambda core: CHIPS[slot ^ core if slot < 6 else slot])

    def to_neighbour(x, axis):
        change = {"x": (1, 0), "z": (2, 0), "y": (0, 1)}[axis]
        return cube_swap(x, lambda core: change)

    def per_device(acts, grad_logits, master, moment_one, moment_two, step_count):
        tokens, experts = grad_logits.shape
        rows = master.shape[0]
        half = rows // n_rep
        high, low, core, rep = position()
        f32, bf16 = jnp.float32, jnp.bfloat16
        in_kernels = half % 16 == 0 and (4 * half) % 128 == 0

        vmem = pl.BlockSpec(memory_space=pltpu.VMEM)
        anywhere = pl.BlockSpec(memory_space=pl.ANY)
        params = pltpu.CompilerParams(vmem_limit_bytes=VMEM_LIMIT)
        state_in = (master, moment_one, moment_two)

        if in_kernels:
            acts = pltpu.with_memory_space_constraint(acts, pltpu.HBM)
            shape = pltpu.VMEM((4, n_high, half, experts), bf16)
            columns_shape = pltpu.VMEM((2 * n_high, tokens, 4 * half), bf16)
            blocks = pltpu.VMEM((2, 2, half, experts), bf16)
            turned = pltpu.VMEM((experts, tokens), bf16)
            away_second, kept_second, mine, later, turned = pl.pallas_call(
                functools.partial(first_grad_kernel, n_high),
                out_shape=[shape, shape, pltpu.VMEM((3, half, experts), f32), columns_shape, turned],
                in_specs=[anywhere] * 5,
                out_specs=[vmem] * 5,
                scratch_shapes=[
                    columns_shape,
                    pltpu.VMEM((tokens, experts), bf16),
                    blocks,
                    pltpu.SemaphoreType.DMA((3, max(2 * n_high, 4))),
                ],
                compiler_params=params,
            )(
                acts,
                *(pltpu.with_memory_space_constraint(x, pltpu.HBM) for x in (grad_logits, *state_in)),
            )
            away_first, kept_first = pl.pallas_call(
                functools.partial(second_grad_kernel, n_high),
                out_shape=[shape, shape],
                in_specs=[vmem, vmem],
                out_specs=[vmem] * 2,
                scratch_shapes=[blocks],
                cost_estimate=pl.CostEstimate(
                    flops=4 * n_high * tokens * experts * 4 * half,
                    bytes_accessed=4 * n_high * tokens * 4 * half,
                    transcendentals=0,
                ),
                compiler_params=params,
            )(*(pltpu.with_memory_space_constraint(x, pltpu.VMEM) for x in (later, turned)))
            away, kept = (away_first, away_second), (kept_first, kept_second)
        else:
            product = lax.dot_general(
                acts, grad_logits, (((0,), (0,)), ((), ())), preferred_element_type=f32
            ).astype(bf16)
            product = product.reshape(n_high, N_LOW, 2, n_rep, half, experts)
            product = product[high ^ jnp.arange(n_high)]

            def sort_rows(owner):
                blocks = []
                for slot in range(8):
                    flip = owner if slot < 6 else 0
                    d_low, d_rep = CHIPS[slot]
                    at = (0, low ^ d_low ^ (3 * flip), owner, rep ^ d_rep ^ flip, 0, 0)
                    part = lax.dynamic_slice(product, at, (n_high, 1, 1, 1, half, experts))
                    blocks.append(part.reshape(n_high, half, experts))
                return jnp.stack(blocks[:4]), jnp.stack(blocks[4:])

            away, kept = sort_rows(1 - core), sort_rows(core)
            mine = jnp.stack([lax.dynamic_slice_in_dim(x, rep * half, half, 0) for x in state_in])

        arrived = swap(away[1], "core")
        arrived, away_first = lax.optimization_barrier((arrived, away[0]))
        arrived = swap(away_first, "core"), arrived
        parts = []
        for own, theirs in zip(kept, arrived):
            summed = own.astype(f32) + theirs.astype(f32)
            for n in range(4):
                slot = len(parts)
                parts.append(summed[n] if slot == 7 else to_slot(summed[n].astype(bf16), slot))
        parts = lax.optimization_barrier(parts)
        total = sum(x.astype(f32) for x in parts)

        grad = total[0]
        for j in range(1, n_high):
            grad = grad + swap(total[j].astype(bf16), "high", j).astype(f32)
        weight = adamw(grad, *mine, step_count)[0].astype(bf16)

        column = jnp.stack([swap(weight, "high", j) if j else weight for j in range(n_high)])
        other = swap(grad, "rep")
        x, y, z = (to_neighbour(column, axis) for axis in "xyz")
        x, other = lax.optimization_barrier((x, other))
        xy, yz, zx = to_neighbour(x, "y"), to_neighbour(y, "z"), to_neighbour(z, "x")
        xy, other, late_acts, late_column = lax.optimization_barrier((xy, other, acts, column))
        across = swap(late_column, "core")
        xyz = to_neighbour(xy, "z")

        whole = jnp.where(
            rep == 0,
            jnp.concatenate([grad, other], 0),
            jnp.concatenate([other, grad], 0),
        )
        state = adamw(whole, *state_in, step_count)

        columns = [None, None]
        if in_kernels:
            columns = pl.pallas_call(
                functools.partial(columns_kernel, n_high, 4 * half),
                out_shape=(pltpu.VMEM((tokens, 8 * n_high * half), bf16),) * 2,
                in_specs=[anywhere],
                out_specs=(vmem, vmem),
                scratch_shapes=[pltpu.SemaphoreType.DMA((2, 2 * n_high))],
                compiler_params=params,
            )(pltpu.with_memory_space_constraint(late_acts, pltpu.HBM))
        xyz, state, columns = lax.optimization_barrier((xyz, state, columns))
        first, second = jnp.stack([x, z, xy, yz]), jnp.stack([y, zx, xyz])
        first, second = [first, swap(first, "core")], [second, swap(second, "core")]
        second += [column[None], across[None]]
        pieces = (first, second)
        logits = None
        for group, (received, acts_columns) in enumerate(zip(pieces, columns)):
            if in_kernels:
                before = [] if logits is None else [logits]
                operands = [
                    pltpu.with_memory_space_constraint(x, pltpu.VMEM) for x in [acts_columns] + received + before
                ]
                logits = pl.pallas_call(
                    functools.partial(logits_kernel, n_high, group),
                    out_shape=jax.ShapeDtypeStruct((tokens, experts), bf16 if before else f32),
                    in_specs=[vmem] * len(operands),
                    out_specs=vmem,
                    scratch_shapes=[pltpu.VMEM((2, n_high, 2, 2, half, experts), bf16)],
                    compiler_params=params,
                )(*operands)
            else:
                rows_at, values = [], []
                for piece, blocks in zip(received, places(group, core, rep)):
                    for n, (place, owner, of_rep) in enumerate(blocks):
                        d_low = jnp.array(LOWS[group])[place]
                        for j in range(n_high):
                            at = ((high ^ j) * N_LOW + (low ^ d_low)) * 2 + owner
                            rows_at.append(at * n_rep + of_rep)
                            values.append(piece[n, j])
                full = jnp.zeros((2 * n_seq, half, experts), bf16)
                full = full.at[jnp.stack(rows_at)].set(jnp.stack(values))
                full = full.reshape(n_seq * rows, experts)
                part = jnp.dot(acts, full, preferred_element_type=f32)
                logits = part if logits is None else (logits + part).astype(bf16)
        return *state, logits

    rows_of, tokens_of = P(AXES[:3], None), P(AXES, None)
    return jax.shard_map(
        per_device,
        mesh=fine,
        in_specs=(tokens_of, tokens_of, rows_of, rows_of, rows_of, P()),
        out_specs=(rows_of, rows_of, rows_of, tokens_of),
        check_vma=False,
    )
```

```python
import functools

import jax
import jax.numpy as jnp
from jax import lax
from jax.experimental import pallas as pl
from jax.experimental.pallas import tpu as pltpu
from jax.sharding import Mesh
from jax.sharding import PartitionSpec as P

AXES = ("high", "low", "core", "rep")
N_LOW = 4
CHIPS = ((1, 0), (2, 1), (2, 0), (1, 1), (0, 1), (3, 0), (3, 1), (0, 0))
LOWS = ((1, 2), (0, 3))
GATHERED = (((1, 0), (2, 0), (1, 1), (2, 1)), ((0, 1), (3, 0), (3, 1)))
VMEM_LIMIT = 8 * 2**20


def slot_of(chip, core):
    slot = CHIPS.index(chip)
    return slot if slot >= 6 else slot ^ core


def position():
    return [lax.axis_index(axis) for axis in AXES]


def adamw(grad, master, moment_one, moment_two, step_count):
    count = step_count[0].astype(jnp.float32)
    beta_one = 0.9
    beta_two = 0.95
    first = beta_one * moment_one + (1.0 - beta_one) * grad
    second = beta_two * moment_two + (1.0 - beta_two) * grad * grad
    first_hat = first / (1.0 - jnp.power(beta_one, count))
    second_hat = second / (1.0 - jnp.power(beta_two, count))
    updated = master - 0.01 * (first_hat / (jnp.sqrt(second_hat) + 1e-08) + 0.1 * master)
    return updated, first, second


def load_columns(acts_ref, slices, sems, lows, n_high, wide):
    high, low, _, _ = position()
    copies = []
    for p, k in enumerate(lows):
        for j in range(n_high):
            column = pl.multiple_of(((high ^ j) * N_LOW + (low ^ k)) * wide, wide)
            n = p * n_high + j
            copy = pltpu.make_async_copy(acts_ref.at[:, pl.ds(column, wide)], slices(n), sems.at[n])
            copy.start()
            copies.append(copy)
    return copies


def sort_products(n_high, group, turned, columns, away, kept, blocks, arrived):
    _, _, core, rep = position()
    for n in range(2 * n_high):
        arrived(n)
        product = jnp.dot(turned, columns[n], preferred_element_type=jnp.float32)
        blocks[...] = product.astype(blocks.dtype).T.reshape(blocks.shape)
        p, j = divmod(n, n_high)
        for d_rep in range(2):
            for out, owner in ((kept, core), (away, 1 - core)):
                slot = slot_of((LOWS[group][p], d_rep), owner)
                out[slot - 4 * group, j] = blocks[owner, rep ^ d_rep]


def first_grad_kernel(n_high, acts_ref, grad_ref, *refs):
    state_refs, refs = refs[:3], refs[3:]
    away, kept, mine_ref, later_ref, turned_ref, columns, logit_grads, blocks, sems = refs
    _, _, _, rep = position()
    half = blocks.shape[2]
    loads = pltpu.make_async_copy(grad_ref, logit_grads, sems.at[2, 0])
    loads.start()
    first = load_columns(acts_ref, lambda n: columns.at[n], sems.at[0], LOWS[1], n_high, 4 * half)
    others = load_columns(acts_ref, lambda n: later_ref.at[n], sems.at[1], LOWS[0], n_high, 4 * half)
    rows = pl.ds(pl.multiple_of(rep * half, half), half)
    for i, ref in enumerate(state_refs):
        copy = pltpu.make_async_copy(ref.at[rows], mine_ref.at[i], sems.at[2, 1 + i])
        copy.start()
        others.append(copy)
    loads.wait()
    turned = logit_grads[...].T
    turned_ref[...] = turned

    def arrived(n):
        if n % 2 == 0:
            first[n].wait()
            first[n + 1].wait()

    sort_products(n_high, 1, turned, columns, away, kept, blocks, arrived)
    for copy in others:
        copy.wait()


def second_grad_kernel(n_high, columns, turned_ref, away, kept, blocks):
    sort_products(n_high, 0, turned_ref[...], columns, away, kept, blocks, lambda n: None)


def columns_kernel(n_high, wide, acts_ref, first_ref, second_ref, sems):
    copies = []
    for i, (lows, out) in enumerate(zip(LOWS, (first_ref, second_ref))):
        slices = lambda n, out=out: out.at[:, pl.ds(n * wide, wide)]
        copies += load_columns(acts_ref, slices, sems.at[i], lows, n_high, wide)
    for copy in copies:
        copy.wait()


def logits_kernel(n_high, group, columns_ref, *refs):
    *pieces, out_ref, weight = refs
    before = None
    if len(pieces[-1].shape) == 2:
        *pieces, before = pieces
    _, _, core, rep = position()
    half, experts = weight.shape[-2:]
    for piece, blocks in zip(pieces, places(group, core, rep)):
        for n, (place, owner, of_rep) in enumerate(blocks):
            for j in range(n_high):
                weight[place, j, owner, of_rep] = piece[n, j]
    total = jnp.dot(
        columns_ref[...],
        weight[...].reshape(8 * n_high * half, experts),
        preferred_element_type=jnp.float32,
    )
    if before is not None:
        total = total + before[...]
    out_ref[...] = total.astype(out_ref.dtype)


def places(group, core, rep):
    pieces = []
    for owner in (core, 1 - core):
        pieces.append([(LOWS[group].index(low), owner, rep ^ d_rep) for low, d_rep in GATHERED[group]])
    if group == 1:
        pieces += [[(0, owner, rep)] for owner in (core, 1 - core)]
    return pieces


def solution(mesh):
    n_seq, n_rep = mesh.shape["seq"], mesh.shape["rep"]
    n_high = n_seq // (2 * N_LOW)
    fine = Mesh(mesh.devices.reshape(n_high, N_LOW, 2, n_rep), AXES)

    def swap(x, axis, mask=1):
        return lax.ppermute(x, axis, [(i, i ^ mask) for i in range(fine.shape[axis])])

    def cube_swap(x, change):
        pairs = []
        for low in range(N_LOW):
            for core in range(2):
                d_low, d_rep = change(core)
                for rep in range(n_rep):
                    there = ((low ^ d_low) * 2 + core) * n_rep + (rep ^ d_rep)
                    pairs.append(((low * 2 + core) * n_rep + rep, there))
        return lax.ppermute(x, AXES[1:], pairs)

    def to_slot(x, slot):
        return cube_swap(x, lambda core: CHIPS[slot ^ core if slot < 6 else slot])

    def to_neighbour(x, axis):
        change = {"x": (1, 0), "z": (2, 0), "y": (0, 1)}[axis]
        return cube_swap(x, lambda core: change)

    def per_device(acts, grad_logits, master, moment_one, moment_two, step_count):
        tokens, experts = grad_logits.shape
        rows = master.shape[0]
        half = rows // n_rep
        high, low, core, rep = position()
        f32, bf16 = jnp.float32, jnp.bfloat16
        in_kernels = half % 16 == 0 and (4 * half) % 128 == 0

        vmem = pl.BlockSpec(memory_space=pltpu.VMEM)
        anywhere = pl.BlockSpec(memory_space=pl.ANY)
        params = pltpu.CompilerParams(vmem_limit_bytes=VMEM_LIMIT)
        state_in = (master, moment_one, moment_two)

        if in_kernels:
            acts = pltpu.with_memory_space_constraint(acts, pltpu.HBM)
            shape = pltpu.VMEM((4, n_high, half, experts), bf16)
            columns_shape = pltpu.VMEM((2 * n_high, tokens, 4 * half), bf16)
            blocks = pltpu.VMEM((2, 2, half, experts), bf16)
            turned = pltpu.VMEM((experts, tokens), bf16)
            away_second, kept_second, mine, later, turned = pl.pallas_call(
                functools.partial(first_grad_kernel, n_high),
                out_shape=[shape, shape, pltpu.VMEM((3, half, experts), f32), columns_shape, turned],
                in_specs=[anywhere] * 5,
                out_specs=[vmem] * 5,
                scratch_shapes=[
                    columns_shape,
                    pltpu.VMEM((tokens, experts), bf16),
                    blocks,
                    pltpu.SemaphoreType.DMA((3, max(2 * n_high, 4))),
                ],
                compiler_params=params,
            )(
                acts,
                *(pltpu.with_memory_space_constraint(x, pltpu.HBM) for x in (grad_logits, *state_in)),
            )
            away_first, kept_first = pl.pallas_call(
                functools.partial(second_grad_kernel, n_high),
                out_shape=[shape, shape],
                in_specs=[vmem, vmem],
                out_specs=[vmem] * 2,
                scratch_shapes=[blocks],
                cost_estimate=pl.CostEstimate(
                    flops=4 * n_high * tokens * experts * 4 * half,
                    bytes_accessed=4 * n_high * tokens * 4 * half,
                    transcendentals=0,
                ),
                compiler_params=params,
            )(*(pltpu.with_memory_space_constraint(x, pltpu.VMEM) for x in (later, turned)))
            away, kept = (away_first, away_second), (kept_first, kept_second)
        else:
            product = lax.dot_general(
                acts, grad_logits, (((0,), (0,)), ((), ())), preferred_element_type=f32
            ).astype(bf16)
            product = product.reshape(n_high, N_LOW, 2, n_rep, half, experts)
            product = product[high ^ jnp.arange(n_high)]

            def sort_rows(owner):
                blocks = []
                for slot in range(8):
                    flip = owner if slot < 6 else 0
                    d_low, d_rep = CHIPS[slot]
                    at = (0, low ^ d_low ^ (3 * flip), owner, rep ^ d_rep ^ flip, 0, 0)
                    part = lax.dynamic_slice(product, at, (n_high, 1, 1, 1, half, experts))
                    blocks.append(part.reshape(n_high, half, experts))
                return jnp.stack(blocks[:4]), jnp.stack(blocks[4:])

            away, kept = sort_rows(1 - core), sort_rows(core)
            mine = jnp.stack([lax.dynamic_slice_in_dim(x, rep * half, half, 0) for x in state_in])

        arrived = swap(away[1], "core")
        arrived, away_first = lax.optimization_barrier((arrived, away[0]))
        arrived = swap(away_first, "core"), arrived
        parts = []
        for own, theirs in zip(kept, arrived):
            summed = own.astype(f32) + theirs.astype(f32)
            for n in range(4):
                slot = len(parts)
                parts.append(summed[n] if slot == 7 else to_slot(summed[n].astype(bf16), slot))
        parts = lax.optimization_barrier(parts)
        total = sum(x.astype(f32) for x in parts)

        grad = total[0]
        for j in range(1, n_high):
            grad = grad + swap(total[j].astype(bf16), "high", j).astype(f32)
        weight = adamw(grad, *mine, step_count)[0].astype(bf16)

        far = [swap(weight, "high", j) for j in range(1, n_high)]
        other = swap(grad, "rep")
        columns = [None, None]
        if in_kernels:
            weight, late_acts = lax.optimization_barrier((weight, acts))
            columns = pl.pallas_call(
                functools.partial(columns_kernel, n_high, 4 * half),
                out_shape=(pltpu.VMEM((tokens, 8 * n_high * half), bf16),) * 2,
                in_specs=[anywhere],
                out_specs=(vmem, vmem),
                scratch_shapes=[pltpu.SemaphoreType.DMA((2, 2 * n_high))],
                compiler_params=params,
            )(pltpu.with_memory_space_constraint(late_acts, pltpu.HBM))
            far, columns = lax.optimization_barrier((far, columns))
        column = jnp.stack([weight, *far])
        x, y, z = (to_neighbour(column, axis) for axis in "xyz")
        x, other = lax.optimization_barrier((x, other))
        xy, yz, zx = to_neighbour(x, "y"), to_neighbour(y, "z"), to_neighbour(z, "x")
        xy, late_column = lax.optimization_barrier((xy, column))
        across = swap(late_column, "core")
        xyz = to_neighbour(xy, "z")

        whole = jnp.where(
            rep == 0,
            jnp.concatenate([grad, other], 0),
            jnp.concatenate([other, grad], 0),
        )
        state = adamw(whole, *state_in, step_count)

        first, second = jnp.stack([x, z, xy, yz]), jnp.stack([y, zx, xyz])
        first, second = [first, swap(first, "core")], [second, swap(second, "core")]
        second += [column[None], across[None]]
        pieces = (first, second)
        logits = None
        for group, (received, acts_columns) in enumerate(zip(pieces, columns)):
            if in_kernels:
                before = [] if logits is None else [logits]
                operands = [
                    pltpu.with_memory_space_constraint(x, pltpu.VMEM) for x in [acts_columns] + received + before
                ]
                logits = pl.pallas_call(
                    functools.partial(logits_kernel, n_high, group),
                    out_shape=jax.ShapeDtypeStruct((tokens, experts), bf16 if before else f32),
                    in_specs=[vmem] * len(operands),
                    out_specs=vmem,
                    scratch_shapes=[pltpu.VMEM((2, n_high, 2, 2, half, experts), bf16)],
                    compiler_params=params,
                )(*operands)
            else:
                rows_at, values = [], []
                for piece, blocks in zip(received, places(group, core, rep)):
                    for n, (place, owner, of_rep) in enumerate(blocks):
                        d_low = jnp.array(LOWS[group])[place]
                        for j in range(n_high):
                            at = ((high ^ j) * N_LOW + (low ^ d_low)) * 2 + owner
                            rows_at.append(at * n_rep + of_rep)
                            values.append(piece[n, j])
                full = jnp.zeros((2 * n_seq, half, experts), bf16)
                full = full.at[jnp.stack(rows_at)].set(jnp.stack(values))
                full = full.reshape(n_seq * rows, experts)
                part = jnp.dot(acts, full, preferred_element_type=f32)
                logits = part if logits is None else (logits + part).astype(bf16)
        return *state, logits

    rows_of, tokens_of = P(AXES[:3], None), P(AXES, None)
    return jax.shard_map(
        per_device,
        mesh=fine,
        in_specs=(tokens_of, tokens_of, rows_of, rows_of, rows_of, P()),
        out_specs=(rows_of, rows_of, rows_of, tokens_of),
        check_vma=False,
    )
```

```python
import functools

import jax
import jax.numpy as jnp
from jax import lax
from jax.experimental import pallas as pl
from jax.experimental.pallas import tpu as pltpu
from jax.sharding import Mesh
from jax.sharding import PartitionSpec as P

AXES = ("high", "low", "core", "rep")
N_LOW = 4
CHIPS = ((1, 0), (2, 1), (2, 0), (1, 1), (0, 1), (3, 0), (3, 1), (0, 0))
LOWS = ((1, 2), (0, 3))
NEXT = ((1, 0), (2, 0), (0, 1))
VMEM_LIMIT = 8 * 2**20


def position():
    return [lax.axis_index(axis) for axis in AXES]


def adamw(grad, master, moment_one, moment_two, step_count):
    count = step_count[0].astype(jnp.float32)
    beta_one = 0.9
    beta_two = 0.95
    first = beta_one * moment_one + (1.0 - beta_one) * grad
    second = beta_two * moment_two + (1.0 - beta_two) * grad * grad
    first_hat = first / (1.0 - jnp.power(beta_one, count))
    second_hat = second / (1.0 - jnp.power(beta_two, count))
    updated = master - 0.01 * (first_hat / (jnp.sqrt(second_hat) + 1e-08) + 0.1 * master)
    return updated, first, second


def load_columns(acts_ref, slices, sems, lows, n_high, wide):
    high, low, _, _ = position()
    copies = []
    for p, k in enumerate(lows):
        for j in range(n_high):
            column = pl.multiple_of(((high ^ j) * N_LOW + (low ^ k)) * wide, wide)
            n = p * n_high + j
            copy = pltpu.make_async_copy(acts_ref.at[:, pl.ds(column, wide)], slices(n), sems.at[n])
            copy.start()
            copies.append(copy)
    return copies


def sort_products(n_high, group, turned, columns, away, kept, blocks, arrived):
    _, _, core, rep = position()
    for n in range(2 * n_high):
        arrived(n)
        product = jnp.dot(turned, columns[n], preferred_element_type=jnp.float32)
        blocks[...] = product.astype(blocks.dtype).T.reshape(blocks.shape)
        p, j = divmod(n, n_high)
        for d_rep in range(2):
            chip = CHIPS.index((LOWS[group][p], d_rep)) - 4 * group
            for out, owner in ((kept, core), (away, 1 - core)):
                out[chip, j] = blocks[owner, rep ^ d_rep]


def first_grad_kernel(n_high, acts_ref, grad_ref, *refs):
    state_refs, refs = refs[:3], refs[3:]
    away, kept, mine_ref, later_ref, turned_ref, columns, logit_grads, blocks, sems = refs
    _, _, _, rep = position()
    half = blocks.shape[2]
    loads = pltpu.make_async_copy(grad_ref, logit_grads, sems.at[2, 0])
    loads.start()
    first = load_columns(acts_ref, lambda n: columns.at[n], sems.at[0], LOWS[1], n_high, 4 * half)
    others = load_columns(acts_ref, lambda n: later_ref.at[n], sems.at[1], LOWS[0], n_high, 4 * half)
    rows = pl.ds(pl.multiple_of(rep * half, half), half)
    for i, ref in enumerate(state_refs):
        copy = pltpu.make_async_copy(ref.at[rows], mine_ref.at[i], sems.at[2, 1 + i])
        copy.start()
        others.append(copy)
    loads.wait()
    turned = logit_grads[...].T
    turned_ref[...] = turned

    def arrived(n):
        if n % 2 == 0:
            first[n].wait()
            first[n + 1].wait()

    sort_products(n_high, 1, turned, columns, away, kept, blocks, arrived)
    for copy in others:
        copy.wait()


def second_grad_kernel(n_high, columns, turned_ref, away, kept, blocks):
    sort_products(n_high, 0, turned_ref[...], columns, away, kept, blocks, lambda n: None)


def columns_kernel(n_high, wide, acts_ref, first_ref, second_ref, sems):
    copies = []
    for i, (lows, out) in enumerate(zip(LOWS, (first_ref, second_ref))):
        slices = lambda n, out=out: out.at[:, pl.ds(n * wide, wide)]
        copies += load_columns(acts_ref, slices, sems.at[i], lows, n_high, wide)
    for copy in copies:
        copy.wait()


def logits_kernel(n_high, group, columns_ref, *refs):
    *pieces, out_ref, weight = refs
    before = None
    if len(pieces[-1].shape) == 2:
        *pieces, before = pieces
    _, _, core, rep = position()
    half, experts = weight.shape[-2:]
    for piece, blocks in zip(pieces, places(group, core, rep)):
        for n, (place, owner, of_rep) in enumerate(blocks):
            for j in range(n_high):
                weight[place, j, owner, of_rep] = piece[n, j]
    total = jnp.dot(
        columns_ref[...],
        weight[...].reshape(8 * n_high * half, experts),
        preferred_element_type=jnp.float32,
    )
    if before is not None:
        total = total + before[...]
    out_ref[...] = total.astype(out_ref.dtype)


def places(group, core, rep):
    pieces = []
    for by in (core, 1 - core):
        blocks = []
        for chip in NEXT[:2] if group == 0 else NEXT[2:]:
            place = LOWS[group].index(chip[0]) ^ by
            blocks += [(place, owner, rep ^ chip[1] ^ by) for owner in range(2)]
        if group == 1:
            blocks.append((1, by, rep ^ 1))
        pieces.append(blocks)
    if group == 1:
        pieces += [[(0, owner, rep)] for owner in (core, 1 - core)]
    return pieces


def solution(mesh):
    n_seq, n_rep = mesh.shape["seq"], mesh.shape["rep"]
    n_high = n_seq // (2 * N_LOW)
    fine = Mesh(mesh.devices.reshape(n_high, N_LOW, 2, n_rep), AXES)

    def swap(x, axis, mask=1):
        return lax.ppermute(x, axis, [(i, i ^ mask) for i in range(fine.shape[axis])])

    def cube_swap(x, change):
        pairs = []
        for low in range(N_LOW):
            for core in range(2):
                d_low, d_rep = change(core)
                for rep in range(n_rep):
                    there = ((low ^ d_low) * 2 + core) * n_rep + (rep ^ d_rep)
                    pairs.append(((low * 2 + core) * n_rep + rep, there))
        return lax.ppermute(x, AXES[1:], pairs)

    def to_neighbour(x, axis):
        change = {"x": (1, 0), "z": (2, 0), "y": (0, 1)}[axis]
        return cube_swap(x, lambda core: change)

    def to_next(x, slot):
        d_low, d_rep = NEXT[slot]
        return cube_swap(x, lambda core: (d_low ^ (3 * core), d_rep ^ core))

    def to_corner(x):
        return cube_swap(x, lambda core: (3, 1))

    def per_device(acts, grad_logits, master, moment_one, moment_two, step_count):
        tokens, experts = grad_logits.shape
        rows = master.shape[0]
        half = rows // n_rep
        high, low, core, rep = position()
        f32, bf16 = jnp.float32, jnp.bfloat16
        in_kernels = half % 16 == 0 and (4 * half) % 128 == 0

        vmem = pl.BlockSpec(memory_space=pltpu.VMEM)
        anywhere = pl.BlockSpec(memory_space=pl.ANY)
        params = pltpu.CompilerParams(vmem_limit_bytes=VMEM_LIMIT)
        state_in = (master, moment_one, moment_two)

        if in_kernels:
            acts = pltpu.with_memory_space_constraint(acts, pltpu.HBM)
            shape = pltpu.VMEM((4, n_high, half, experts), bf16)
            columns_shape = pltpu.VMEM((2 * n_high, tokens, 4 * half), bf16)
            blocks = pltpu.VMEM((2, 2, half, experts), bf16)
            turned = pltpu.VMEM((experts, tokens), bf16)
            away_second, kept_second, mine, later, turned = pl.pallas_call(
                functools.partial(first_grad_kernel, n_high),
                out_shape=[shape, shape, pltpu.VMEM((3, half, experts), f32), columns_shape, turned],
                in_specs=[anywhere] * 5,
                out_specs=[vmem] * 5,
                scratch_shapes=[
                    columns_shape,
                    pltpu.VMEM((tokens, experts), bf16),
                    blocks,
                    pltpu.SemaphoreType.DMA((3, max(2 * n_high, 4))),
                ],
                compiler_params=params,
            )(
                acts,
                *(pltpu.with_memory_space_constraint(x, pltpu.HBM) for x in (grad_logits, *state_in)),
            )
            away_first, kept_first = pl.pallas_call(
                functools.partial(second_grad_kernel, n_high),
                out_shape=[shape, shape],
                in_specs=[vmem, vmem],
                out_specs=[vmem] * 2,
                scratch_shapes=[blocks],
                cost_estimate=pl.CostEstimate(
                    flops=4 * n_high * tokens * experts * 4 * half,
                    bytes_accessed=4 * n_high * tokens * 4 * half,
                    transcendentals=0,
                ),
                compiler_params=params,
            )(*(pltpu.with_memory_space_constraint(x, pltpu.VMEM) for x in (later, turned)))
            away, kept = (away_first, away_second), (kept_first, kept_second)
        else:
            product = lax.dot_general(
                acts, grad_logits, (((0,), (0,)), ((), ())), preferred_element_type=f32
            ).astype(bf16)
            product = product.reshape(n_high, N_LOW, 2, n_rep, half, experts)
            product = product[high ^ jnp.arange(n_high)]

            def sort_rows(owner):
                blocks = []
                for d_low, d_rep in CHIPS:
                    at = (0, low ^ d_low, owner, rep ^ d_rep, 0, 0)
                    part = lax.dynamic_slice(product, at, (n_high, 1, 1, 1, half, experts))
                    blocks.append(part.reshape(n_high, half, experts))
                return jnp.stack(blocks[:4]), jnp.stack(blocks[4:])

            away, kept = sort_rows(1 - core), sort_rows(core)
            mine = jnp.stack([lax.dynamic_slice_in_dim(x, rep * half, half, 0) for x in state_in])

        arrived = swap(away[1], "core")
        arrived, away_first = lax.optimization_barrier((arrived, away[0]))
        arrived = swap(away_first, "core"), arrived
        (x, yz, z, xy), (y, zx, corner, home) = [
            own.astype(f32) + theirs.astype(f32) for own, theirs in zip(kept, arrived)
        ]
        corner = to_corner(corner.astype(bf16))
        z = z + to_neighbour(zx.astype(bf16), "x").astype(f32)
        y = y + to_neighbour(yz.astype(bf16), "z").astype(f32)
        x = x + to_neighbour(xy.astype(bf16), "y").astype(f32)
        parts = [to_neighbour(part.astype(bf16), axis) for part, axis in ((z, "z"), (y, "y"), (x, "x"))]
        parts = lax.optimization_barrier((corner, *parts))
        total = home + sum(part.astype(f32) for part in parts)

        grad = total[0]
        for j in range(1, n_high):
            grad = grad + swap(total[j].astype(bf16), "high", j).astype(f32)
        weight = adamw(grad, *mine, step_count)[0].astype(bf16)

        column = jnp.stack([swap(weight, "high", j) if j else weight for j in range(n_high)])
        other = swap(grad, "rep")
        across = swap(column, "core")
        across, other = lax.optimization_barrier((across, other))
        corner = to_corner(column)
        chip = jnp.where(core == 0, jnp.stack([column, across]), jnp.stack([across, column]))
        got = [to_next(chip, slot) for slot in range(3)]

        whole = jnp.where(
            rep == 0,
            jnp.concatenate([grad, other], 0),
            jnp.concatenate([other, grad], 0),
        )
        state = adamw(whole, *state_in, step_count)

        columns = [None, None]
        if in_kernels:
            state, late_acts = lax.optimization_barrier((state, acts))
            columns = pl.pallas_call(
                functools.partial(columns_kernel, n_high, 4 * half),
                out_shape=(pltpu.VMEM((tokens, 8 * n_high * half), bf16),) * 2,
                in_specs=[anywhere],
                out_specs=(vmem, vmem),
                scratch_shapes=[pltpu.SemaphoreType.DMA((2, 2 * n_high))],
                compiler_params=params,
            )(pltpu.with_memory_space_constraint(late_acts, pltpu.HBM))
        got[0], corner, state, columns = lax.optimization_barrier((got[0], corner, state, columns))
        first, second = jnp.concatenate(got[:2]), jnp.concatenate([got[2], corner[None]])
        first, second = [first, swap(first, "core")], [second, swap(second, "core")]
        second += [column[None], across[None]]
        pieces = (first, second)
        logits = None
        for group, (received, acts_columns) in enumerate(zip(pieces, columns)):
            if in_kernels:
                before = [] if logits is None else [logits]
                operands = [
                    pltpu.with_memory_space_constraint(x, pltpu.VMEM) for x in [acts_columns] + received + before
                ]
                logits = pl.pallas_call(
                    functools.partial(logits_kernel, n_high, group),
                    out_shape=jax.ShapeDtypeStruct((tokens, experts), bf16 if before else f32),
                    in_specs=[vmem] * len(operands),
                    out_specs=vmem,
                    scratch_shapes=[pltpu.VMEM((2, n_high, 2, 2, half, experts), bf16)],
                    compiler_params=params,
                )(*operands)
            else:
                rows_at, values = [], []
                for piece, blocks in zip(received, places(group, core, rep)):
                    for n, (place, owner, of_rep) in enumerate(blocks):
                        d_low = jnp.array(LOWS[group])[place]
                        for j in range(n_high):
                            at = ((high ^ j) * N_LOW + (low ^ d_low)) * 2 + owner
                            rows_at.append(at * n_rep + of_rep)
                            values.append(piece[n, j])
                full = jnp.zeros((2 * n_seq, half, experts), bf16)
                full = full.at[jnp.stack(rows_at)].set(jnp.stack(values))
                full = full.reshape(n_seq * rows, experts)
                part = jnp.dot(acts, full, preferred_element_type=f32)
                logits = part if logits is None else (logits + part).astype(bf16)
        return *state, logits

    rows_of, tokens_of = P(AXES[:3], None), P(AXES, None)
    return jax.shard_map(
        per_device,
        mesh=fine,
        in_specs=(tokens_of, tokens_of, rows_of, rows_of, rows_of, P()),
        out_specs=(rows_of, rows_of, rows_of, tokens_of),
        check_vma=False,
    )
```

```python
import functools

import jax
import jax.numpy as jnp
from jax import lax
from jax.experimental import pallas as pl
from jax.experimental.pallas import tpu as pltpu
from jax.sharding import Mesh
from jax.sharding import PartitionSpec as P

AXES = ("high", "low", "core", "rep")
N_LOW = 4
CHIPS = ((1, 0), (2, 1), (2, 0), (1, 1), (0, 1), (3, 0), (3, 1), (0, 0))
LOWS = ((1, 2), (0, 3))
NEXT = ((1, 0), (2, 0), (0, 1))
VMEM_LIMIT = 8 * 2**20


def slot_of(chip, core):
    slot = CHIPS.index(chip)
    return slot if slot >= 6 else slot ^ core


def position():
    return [lax.axis_index(axis) for axis in AXES]


def adamw(grad, master, moment_one, moment_two, step_count):
    count = step_count[0].astype(jnp.float32)
    beta_one = 0.9
    beta_two = 0.95
    first = beta_one * moment_one + (1.0 - beta_one) * grad
    second = beta_two * moment_two + (1.0 - beta_two) * grad * grad
    first_hat = first / (1.0 - jnp.power(beta_one, count))
    second_hat = second / (1.0 - jnp.power(beta_two, count))
    updated = master - 0.01 * (first_hat / (jnp.sqrt(second_hat) + 1e-08) + 0.1 * master)
    return updated, first, second


def load_columns(acts_ref, slices, sems, lows, n_high, wide):
    high, low, _, _ = position()
    copies = []
    for p, k in enumerate(lows):
        for j in range(n_high):
            column = pl.multiple_of(((high ^ j) * N_LOW + (low ^ k)) * wide, wide)
            n = p * n_high + j
            copy = pltpu.make_async_copy(acts_ref.at[:, pl.ds(column, wide)], slices(n), sems.at[n])
            copy.start()
            copies.append(copy)
    return copies


def sort_products(n_high, group, turned, columns, away, kept, blocks, arrived):
    _, _, core, rep = position()
    for n in range(2 * n_high):
        arrived(n)
        product = jnp.dot(turned, columns[n], preferred_element_type=jnp.float32)
        blocks[...] = product.astype(blocks.dtype).T.reshape(blocks.shape)
        p, j = divmod(n, n_high)
        for d_rep in range(2):
            chip = LOWS[group][p], d_rep
            left = CHIPS.index(chip) >= 6
            for outs, owner in ((kept, core), (away, 1 - core)):
                outs[left][slot_of(chip, owner) - (6 if left else 4 * group), j] = blocks[owner, rep ^ d_rep]


def first_grad_kernel(n_high, acts_ref, grad_ref, *refs):
    state_refs, refs = refs[:3], refs[3:]
    away, kept, refs = refs[:2], refs[2:4], refs[4:]
    mine_ref, later_ref, turned_ref, columns, logit_grads, blocks, sems = refs
    _, _, _, rep = position()
    half = blocks.shape[2]
    loads = pltpu.make_async_copy(grad_ref, logit_grads, sems.at[2, 0])
    loads.start()
    first = load_columns(acts_ref, lambda n: columns.at[n], sems.at[0], LOWS[1], n_high, 4 * half)
    others = load_columns(acts_ref, lambda n: later_ref.at[n], sems.at[1], LOWS[0], n_high, 4 * half)
    rows = pl.ds(pl.multiple_of(rep * half, half), half)
    for i, ref in enumerate(state_refs):
        copy = pltpu.make_async_copy(ref.at[rows], mine_ref.at[i], sems.at[2, 1 + i])
        copy.start()
        others.append(copy)
    loads.wait()
    turned = logit_grads[...].T
    turned_ref[...] = turned

    def arrived(n):
        if n % 2 == 0:
            first[n].wait()
            first[n + 1].wait()

    sort_products(n_high, 1, turned, columns, away, kept, blocks, arrived)
    for copy in others:
        copy.wait()


def second_grad_kernel(n_high, columns, turned_ref, away, kept, blocks):
    sort_products(n_high, 0, turned_ref[...], columns, [away], [kept], blocks, lambda n: None)


def columns_kernel(n_high, wide, acts_ref, first_ref, second_ref, sems):
    copies = []
    for i, (lows, out) in enumerate(zip(LOWS, (first_ref, second_ref))):
        slices = lambda n, out=out: out.at[:, pl.ds(n * wide, wide)]
        copies += load_columns(acts_ref, slices, sems.at[i], lows, n_high, wide)
    for copy in copies:
        copy.wait()


def logits_kernel(n_high, group, columns_ref, *refs):
    *pieces, out_ref, weight = refs
    before = None
    if len(pieces[-1].shape) == 2:
        *pieces, before = pieces
    _, _, core, rep = position()
    half, experts = weight.shape[-2:]
    for piece, blocks in zip(pieces, places(group, core, rep)):
        for n, (place, owner, of_rep) in enumerate(blocks):
            for j in range(n_high):
                weight[place, j, owner, of_rep] = piece[n, j]
    total = jnp.dot(
        columns_ref[...],
        weight[...].reshape(8 * n_high * half, experts),
        preferred_element_type=jnp.float32,
    )
    if before is not None:
        total = total + before[...]
    out_ref[...] = total.astype(out_ref.dtype)


def places(group, core, rep):
    pieces = []
    for by in (core, 1 - core):
        blocks = []
        for chip in NEXT[:2] if group == 0 else NEXT[2:]:
            place = LOWS[group].index(chip[0]) ^ by
            blocks += [(place, owner, rep ^ chip[1] ^ by) for owner in range(2)]
        if group == 1:
            blocks.append((1, by, rep ^ 1))
        pieces.append(blocks)
    if group == 1:
        pieces += [[(0, owner, rep)] for owner in (core, 1 - core)]
    return pieces


def solution(mesh):
    n_seq, n_rep = mesh.shape["seq"], mesh.shape["rep"]
    n_high = n_seq // (2 * N_LOW)
    fine = Mesh(mesh.devices.reshape(n_high, N_LOW, 2, n_rep), AXES)

    def swap(x, axis, mask=1):
        return lax.ppermute(x, axis, [(i, i ^ mask) for i in range(fine.shape[axis])])

    def cube_swap(x, change):
        pairs = []
        for low in range(N_LOW):
            for core in range(2):
                d_low, d_rep = change(core)
                for rep in range(n_rep):
                    there = ((low ^ d_low) * 2 + core) * n_rep + (rep ^ d_rep)
                    pairs.append(((low * 2 + core) * n_rep + rep, there))
        return lax.ppermute(x, AXES[1:], pairs)

    def to_slot(x, slot):
        return cube_swap(x, lambda core: CHIPS[slot ^ core if slot < 6 else slot])

    def to_next(x, slot):
        d_low, d_rep = NEXT[slot]
        return cube_swap(x, lambda core: (d_low ^ (3 * core), d_rep ^ core))

    def to_corner(x):
        return cube_swap(x, lambda core: (3, 1))

    def per_device(acts, grad_logits, master, moment_one, moment_two, step_count):
        tokens, experts = grad_logits.shape
        rows = master.shape[0]
        half = rows // n_rep
        high, low, core, rep = position()
        f32, bf16 = jnp.float32, jnp.bfloat16
        in_kernels = half % 16 == 0 and (4 * half) % 128 == 0

        vmem = pl.BlockSpec(memory_space=pltpu.VMEM)
        anywhere = pl.BlockSpec(memory_space=pl.ANY)
        params = pltpu.CompilerParams(vmem_limit_bytes=VMEM_LIMIT)
        state_in = (master, moment_one, moment_two)

        if in_kernels:
            acts = pltpu.with_memory_space_constraint(acts, pltpu.HBM)
            shape = pltpu.VMEM((4, n_high, half, experts), bf16)
            columns_shape = pltpu.VMEM((2 * n_high, tokens, 4 * half), bf16)
            blocks = pltpu.VMEM((2, 2, half, experts), bf16)
            turned = pltpu.VMEM((experts, tokens), bf16)
            pair = pltpu.VMEM((2, n_high, half, experts), bf16)
            *sorted_rows, mine, later, turned = pl.pallas_call(
                functools.partial(first_grad_kernel, n_high),
                out_shape=[pair] * 4 + [pltpu.VMEM((3, half, experts), f32), columns_shape, turned],
                in_specs=[anywhere] * 5,
                out_specs=[vmem] * 7,
                scratch_shapes=[
                    columns_shape,
                    pltpu.VMEM((tokens, experts), bf16),
                    blocks,
                    pltpu.SemaphoreType.DMA((3, max(2 * n_high, 4))),
                ],
                compiler_params=params,
            )(
                acts,
                *(pltpu.with_memory_space_constraint(x, pltpu.HBM) for x in (grad_logits, *state_in)),
            )
            away_first, kept_first = pl.pallas_call(
                functools.partial(second_grad_kernel, n_high),
                out_shape=[shape, shape],
                in_specs=[vmem, vmem],
                out_specs=[vmem] * 2,
                scratch_shapes=[blocks],
                cost_estimate=pl.CostEstimate(
                    flops=4 * n_high * tokens * experts * 4 * half,
                    bytes_accessed=4 * n_high * tokens * 4 * half,
                    transcendentals=0,
                ),
                compiler_params=params,
            )(*(pltpu.with_memory_space_constraint(x, pltpu.VMEM) for x in (later, turned)))
            away, kept = (*sorted_rows[:2], away_first), (*sorted_rows[2:], kept_first)
        else:
            product = lax.dot_general(
                acts, grad_logits, (((0,), (0,)), ((), ())), preferred_element_type=f32
            ).astype(bf16)
            product = product.reshape(n_high, N_LOW, 2, n_rep, half, experts)
            product = product[high ^ jnp.arange(n_high)]

            def sort_rows(owner):
                blocks = []
                for slot in range(8):
                    flip = owner if slot < 6 else 0
                    d_low, d_rep = CHIPS[slot]
                    at = (0, low ^ d_low ^ (3 * flip), owner, rep ^ d_rep ^ flip, 0, 0)
                    part = lax.dynamic_slice(product, at, (n_high, 1, 1, 1, half, experts))
                    blocks.append(part.reshape(n_high, half, experts))
                return jnp.stack(blocks[4:6]), jnp.stack(blocks[6:]), jnp.stack(blocks[:4])

            away, kept = sort_rows(1 - core), sort_rows(core)
            mine = jnp.stack([lax.dynamic_slice_in_dim(x, rep * half, half, 0) for x in state_in])

        arrived = swap(away[0], "core")
        arrived, *rest = lax.optimization_barrier((arrived, *away[1:]))
        arrived = [arrived] + [swap(x, "core") for x in rest]
        pair, left, first = [own.astype(f32) + x.astype(f32) for own, x in zip(kept, arrived)]
        parts = [to_slot(x.astype(bf16), 4 + n) for n, x in enumerate(pair)]
        parts += [to_slot(left[0].astype(bf16), 6)]
        parts += [to_slot(x.astype(bf16), n) for n, x in enumerate(first)]
        parts = [left[1], *lax.optimization_barrier(parts)]
        total = sum(x.astype(f32) for x in parts)

        grad = total[0]
        for j in range(1, n_high):
            grad = grad + swap(total[j].astype(bf16), "high", j).astype(f32)
        weight = adamw(grad, *mine, step_count)[0].astype(bf16)

        column = jnp.stack([swap(weight, "high", j) if j else weight for j in range(n_high)])
        other = swap(grad, "rep")
        across = swap(column, "core")
        across, other = lax.optimization_barrier((across, other))
        corner = to_corner(column)
        chip = jnp.where(core == 0, jnp.stack([column, across]), jnp.stack([across, column]))
        got = [to_next(chip, slot) for slot in range(3)]

        whole = jnp.where(
            rep == 0,
            jnp.concatenate([grad, other], 0),
            jnp.concatenate([other, grad], 0),
        )
        state = adamw(whole, *state_in, step_count)

        columns = [None, None]
        if in_kernels:
            state, late_acts = lax.optimization_barrier((state, acts))
            columns = pl.pallas_call(
                functools.partial(columns_kernel, n_high, 4 * half),
                out_shape=(pltpu.VMEM((tokens, 8 * n_high * half), bf16),) * 2,
                in_specs=[anywhere],
                out_specs=(vmem, vmem),
                scratch_shapes=[pltpu.SemaphoreType.DMA((2, 2 * n_high))],
                compiler_params=params,
            )(pltpu.with_memory_space_constraint(late_acts, pltpu.HBM))
        got[0], corner, state, columns = lax.optimization_barrier((got[0], corner, state, columns))
        first, second = jnp.concatenate(got[:2]), jnp.concatenate([got[2], corner[None]])
        first, second = [first, swap(first, "core")], [second, swap(second, "core")]
        second += [column[None], across[None]]
        pieces = (first, second)
        logits = None
        for group, (received, acts_columns) in enumerate(zip(pieces, columns)):
            if in_kernels:
                before = [] if logits is None else [logits]
                operands = [
                    pltpu.with_memory_space_constraint(x, pltpu.VMEM) for x in [acts_columns] + received + before
                ]
                logits = pl.pallas_call(
                    functools.partial(logits_kernel, n_high, group),
                    out_shape=jax.ShapeDtypeStruct((tokens, experts), bf16 if before else f32),
                    in_specs=[vmem] * len(operands),
                    out_specs=vmem,
                    scratch_shapes=[pltpu.VMEM((2, n_high, 2, 2, half, experts), bf16)],
                    compiler_params=params,
                )(*operands)
            else:
                rows_at, values = [], []
                for piece, blocks in zip(received, places(group, core, rep)):
                    for n, (place, owner, of_rep) in enumerate(blocks):
                        d_low = jnp.array(LOWS[group])[place]
                        for j in range(n_high):
                            at = ((high ^ j) * N_LOW + (low ^ d_low)) * 2 + owner
                            rows_at.append(at * n_rep + of_rep)
                            values.append(piece[n, j])
                full = jnp.zeros((2 * n_seq, half, experts), bf16)
                full = full.at[jnp.stack(rows_at)].set(jnp.stack(values))
                full = full.reshape(n_seq * rows, experts)
                part = jnp.dot(acts, full, preferred_element_type=f32)
                logits = part if logits is None else (logits + part).astype(bf16)
        return *state, logits

    rows_of, tokens_of = P(AXES[:3], None), P(AXES, None)
    return jax.shard_map(
        per_device,
        mesh=fine,
        in_specs=(tokens_of, tokens_of, rows_of, rows_of, rows_of, P()),
        out_specs=(rows_of, rows_of, rows_of, tokens_of),
        check_vma=False,
    )
```

```python
import functools

import jax
import jax.numpy as jnp
from jax import lax
from jax.experimental import pallas as pl
from jax.experimental.pallas import tpu as pltpu
from jax.sharding import Mesh
from jax.sharding import PartitionSpec as P

AXES = ("high", "low", "core", "rep")
N_LOW = 4
CHIPS = ((1, 0), (2, 1), (2, 0), (1, 1), (0, 1), (3, 0), (3, 1), (0, 0))
LOWS = ((1, 2), (0, 3))
GATHERED = (((1, 0), (2, 0), (1, 1), (2, 1)), ((0, 1), (3, 0), (3, 1)))
VMEM_LIMIT = 8 * 2**20


def slot_of(chip, core):
    slot = CHIPS.index(chip)
    return slot if slot >= 6 else slot ^ core


def position():
    return [lax.axis_index(axis) for axis in AXES]


def adamw(grad, master, moment_one, moment_two, step_count):
    count = step_count[0].astype(jnp.float32)
    beta_one = 0.9
    beta_two = 0.95
    first = beta_one * moment_one + (1.0 - beta_one) * grad
    second = beta_two * moment_two + (1.0 - beta_two) * grad * grad
    first_hat = first / (1.0 - jnp.power(beta_one, count))
    second_hat = second / (1.0 - jnp.power(beta_two, count))
    updated = master - 0.01 * (first_hat / (jnp.sqrt(second_hat) + 1e-08) + 0.1 * master)
    return updated, first, second


def load_columns(acts_ref, slices, sems, lows, n_high, wide):
    high, low, _, _ = position()
    copies = []
    for p, k in enumerate(lows):
        for j in range(n_high):
            column = pl.multiple_of(((high ^ j) * N_LOW + (low ^ k)) * wide, wide)
            n = p * n_high + j
            copy = pltpu.make_async_copy(acts_ref.at[:, pl.ds(column, wide)], slices(n), sems.at[n])
            copy.start()
            copies.append(copy)
    return copies


def sort_products(n_high, group, turned, columns, away, kept, blocks, arrived):
    _, _, core, rep = position()
    for n in range(2 * n_high):
        arrived(n)
        product = jnp.dot(turned, columns[n], preferred_element_type=jnp.float32)
        blocks[...] = product.astype(blocks.dtype).T.reshape(blocks.shape)
        p, j = divmod(n, n_high)
        for d_rep in range(2):
            for out, owner in ((kept, core), (away, 1 - core)):
                slot = slot_of((LOWS[group][p], d_rep), owner)
                out[slot - 4 * group, j] = blocks[owner, rep ^ d_rep]


def first_grad_kernel(n_high, acts_ref, grad_ref, *refs):
    state_refs, refs = refs[:3], refs[3:]
    away, kept, mine_ref, later_ref, turned_ref, columns, logit_grads, blocks, sems = refs
    _, _, _, rep = position()
    half = blocks.shape[2]
    loads = pltpu.make_async_copy(grad_ref, logit_grads, sems.at[2, 0])
    loads.start()
    first = load_columns(acts_ref, lambda n: columns.at[n], sems.at[0], LOWS[1], n_high, 4 * half)
    others = load_columns(acts_ref, lambda n: later_ref.at[n], sems.at[1], LOWS[0], n_high, 4 * half)
    rows = pl.ds(pl.multiple_of(rep * half, half), half)
    for i, ref in enumerate(state_refs):
        copy = pltpu.make_async_copy(ref.at[rows], mine_ref.at[i], sems.at[2, 1 + i])
        copy.start()
        others.append(copy)
    loads.wait()
    turned = logit_grads[...].T
    turned_ref[...] = turned

    def arrived(n):
        if n % 2 == 0:
            first[n].wait()
            first[n + 1].wait()

    sort_products(n_high, 1, turned, columns, away, kept, blocks, arrived)
    for copy in others:
        copy.wait()


def second_grad_kernel(n_high, columns, turned_ref, away, kept, blocks):
    sort_products(n_high, 0, turned_ref[...], columns, away, kept, blocks, lambda n: None)


def columns_of(group, n_high, wide, acts_ref, out_ref, sems):
    slices = lambda n: out_ref.at[:, pl.ds(n * wide, wide)]
    return load_columns(acts_ref, slices, sems, LOWS[group], n_high, wide)


def columns_kernel(n_high, wide, acts_ref, out_ref, sems):
    for copy in columns_of(0, n_high, wide, acts_ref, out_ref, sems):
        copy.wait()


def first_logits_kernel(n_high, wide, acts_ref, columns_ref, *refs):
    *pieces, out_ref, later_ref, weight, sems = refs
    copies = columns_of(1, n_high, wide, acts_ref, later_ref, sems)
    logits_kernel(n_high, 0, columns_ref, *pieces, out_ref, weight)
    for copy in copies:
        copy.wait()


def logits_kernel(n_high, group, columns_ref, *refs):
    *pieces, out_ref, weight = refs
    before = None
    if len(pieces[-1].shape) == 2:
        *pieces, before = pieces
    _, _, core, rep = position()
    half, experts = weight.shape[-2:]
    for piece, blocks in zip(pieces, places(group, core, rep)):
        for n, (place, owner, of_rep) in enumerate(blocks):
            for j in range(n_high):
                weight[place, j, owner, of_rep] = piece[n, j]
    total = jnp.dot(
        columns_ref[...],
        weight[...].reshape(8 * n_high * half, experts),
        preferred_element_type=jnp.float32,
    )
    if before is not None:
        total = total + before[...]
    out_ref[...] = total.astype(out_ref.dtype)


def places(group, core, rep):
    pieces = []
    for owner in (core, 1 - core):
        pieces.append([(LOWS[group].index(low), owner, rep ^ d_rep) for low, d_rep in GATHERED[group]])
    if group == 1:
        pieces += [[(0, owner, rep)] for owner in (core, 1 - core)]
    return pieces


def solution(mesh):
    n_seq, n_rep = mesh.shape["seq"], mesh.shape["rep"]
    n_high = n_seq // (2 * N_LOW)
    fine = Mesh(mesh.devices.reshape(n_high, N_LOW, 2, n_rep), AXES)

    def swap(x, axis, mask=1):
        return lax.ppermute(x, axis, [(i, i ^ mask) for i in range(fine.shape[axis])])

    def cube_swap(x, change):
        pairs = []
        for low in range(N_LOW):
            for core in range(2):
                d_low, d_rep = change(core)
                for rep in range(n_rep):
                    there = ((low ^ d_low) * 2 + core) * n_rep + (rep ^ d_rep)
                    pairs.append(((low * 2 + core) * n_rep + rep, there))
        return lax.ppermute(x, AXES[1:], pairs)

    def to_slot(x, slot):
        return cube_swap(x, lambda core: CHIPS[slot ^ core if slot < 6 else slot])

    def to_neighbour(x, axis):
        change = {"x": (1, 0), "z": (2, 0), "y": (0, 1)}[axis]
        return cube_swap(x, lambda core: change)

    def per_device(acts, grad_logits, master, moment_one, moment_two, step_count):
        tokens, experts = grad_logits.shape
        rows = master.shape[0]
        half = rows // n_rep
        high, low, core, rep = position()
        f32, bf16 = jnp.float32, jnp.bfloat16
        in_kernels = half % 16 == 0 and (4 * half) % 128 == 0

        vmem = pl.BlockSpec(memory_space=pltpu.VMEM)
        anywhere = pl.BlockSpec(memory_space=pl.ANY)
        params = pltpu.CompilerParams(vmem_limit_bytes=VMEM_LIMIT)
        state_in = (master, moment_one, moment_two)

        if in_kernels:
            acts = pltpu.with_memory_space_constraint(acts, pltpu.HBM)
            shape = pltpu.VMEM((4, n_high, half, experts), bf16)
            columns_shape = pltpu.VMEM((2 * n_high, tokens, 4 * half), bf16)
            blocks = pltpu.VMEM((2, 2, half, experts), bf16)
            turned = pltpu.VMEM((experts, tokens), bf16)
            away_second, kept_second, mine, later, turned = pl.pallas_call(
                functools.partial(first_grad_kernel, n_high),
                out_shape=[shape, shape, pltpu.VMEM((3, half, experts), f32), columns_shape, turned],
                in_specs=[anywhere] * 5,
                out_specs=[vmem] * 5,
                scratch_shapes=[
                    columns_shape,
                    pltpu.VMEM((tokens, experts), bf16),
                    blocks,
                    pltpu.SemaphoreType.DMA((3, max(2 * n_high, 4))),
                ],
                compiler_params=params,
            )(
                acts,
                *(pltpu.with_memory_space_constraint(x, pltpu.HBM) for x in (grad_logits, *state_in)),
            )
            away_first, kept_first = pl.pallas_call(
                functools.partial(second_grad_kernel, n_high),
                out_shape=[shape, shape],
                in_specs=[vmem, vmem],
                out_specs=[vmem] * 2,
                scratch_shapes=[blocks],
                cost_estimate=pl.CostEstimate(
                    flops=4 * n_high * tokens * experts * 4 * half,
                    bytes_accessed=4 * n_high * tokens * 4 * half,
                    transcendentals=0,
                ),
                compiler_params=params,
            )(*(pltpu.with_memory_space_constraint(x, pltpu.VMEM) for x in (later, turned)))
            away, kept = (away_first, away_second), (kept_first, kept_second)
        else:
            product = lax.dot_general(
                acts, grad_logits, (((0,), (0,)), ((), ())), preferred_element_type=f32
            ).astype(bf16)
            product = product.reshape(n_high, N_LOW, 2, n_rep, half, experts)
            product = product[high ^ jnp.arange(n_high)]

            def sort_rows(owner):
                blocks = []
                for slot in range(8):
                    flip = owner if slot < 6 else 0
                    d_low, d_rep = CHIPS[slot]
                    at = (0, low ^ d_low ^ (3 * flip), owner, rep ^ d_rep ^ flip, 0, 0)
                    part = lax.dynamic_slice(product, at, (n_high, 1, 1, 1, half, experts))
                    blocks.append(part.reshape(n_high, half, experts))
                return jnp.stack(blocks[:4]), jnp.stack(blocks[4:])

            away, kept = sort_rows(1 - core), sort_rows(core)
            mine = jnp.stack([lax.dynamic_slice_in_dim(x, rep * half, half, 0) for x in state_in])

        arrived = swap(away[1], "core")
        arrived, away_first = lax.optimization_barrier((arrived, away[0]))
        arrived = swap(away_first, "core"), arrived
        parts = []
        for own, theirs in zip(kept, arrived):
            summed = own.astype(f32) + theirs.astype(f32)
            for n in range(4):
                slot = len(parts)
                parts.append(summed[n] if slot == 7 else to_slot(summed[n].astype(bf16), slot))
        parts = lax.optimization_barrier(parts)
        total = sum(x.astype(f32) for x in parts)

        grad = total[0]
        for j in range(1, n_high):
            grad = grad + swap(total[j].astype(bf16), "high", j).astype(f32)
        weight = adamw(grad, *mine, step_count)[0].astype(bf16)

        far = [swap(weight, "high", j) for j in range(1, n_high)]
        other = swap(grad, "rep")
        columns_shape = pltpu.VMEM((tokens, 8 * n_high * half), bf16)
        column_sems = pltpu.SemaphoreType.DMA((2 * n_high,))
        columns = None
        if in_kernels:
            weight, late_acts = lax.optimization_barrier((weight, acts))
            columns = pl.pallas_call(
                functools.partial(columns_kernel, n_high, 4 * half),
                out_shape=columns_shape,
                in_specs=[anywhere],
                out_specs=vmem,
                scratch_shapes=[column_sems],
                compiler_params=params,
            )(pltpu.with_memory_space_constraint(late_acts, pltpu.HBM))
            far, columns = lax.optimization_barrier((far, columns))
        column = jnp.stack([weight, *far])
        x, y, z = (to_neighbour(column, axis) for axis in "xyz")
        x, other = lax.optimization_barrier((x, other))
        xy, yz, zx = to_neighbour(x, "y"), to_neighbour(y, "z"), to_neighbour(z, "x")
        xy, late_column = lax.optimization_barrier((xy, column))
        across = swap(late_column, "core")
        xyz = to_neighbour(xy, "z")

        whole = jnp.where(
            rep == 0,
            jnp.concatenate([grad, other], 0),
            jnp.concatenate([other, grad], 0),
        )
        state = adamw(whole, *state_in, step_count)

        first, second = jnp.stack([x, z, xy, yz]), jnp.stack([y, zx, xyz])
        first, second = [first, swap(first, "core")], [second, swap(second, "core")]
        second += [column[None], across[None]]
        pieces = (first, second)
        logits = None
        for group, received in enumerate(pieces):
            if in_kernels:
                before = [] if logits is None else [logits]
                operands = [
                    pltpu.with_memory_space_constraint(x, pltpu.VMEM)
                    for x in [columns] + received + before
                ]
                scratch = [pltpu.VMEM((2, n_high, 2, 2, half, experts), bf16)]
                if before:
                    logits = pl.pallas_call(
                        functools.partial(logits_kernel, n_high, group),
                        out_shape=jax.ShapeDtypeStruct((tokens, experts), bf16),
                        in_specs=[vmem] * len(operands),
                        out_specs=vmem,
                        scratch_shapes=scratch,
                        compiler_params=params,
                    )(*operands)
                else:
                    logits, columns = pl.pallas_call(
                        functools.partial(first_logits_kernel, n_high, 4 * half),
                        out_shape=(pltpu.VMEM((tokens, experts), f32), columns_shape),
                        in_specs=[anywhere] + [vmem] * len(operands),
                        out_specs=(vmem, vmem),
                        scratch_shapes=scratch + [column_sems],
                        compiler_params=params,
                    )(acts, *operands)
            else:
                rows_at, values = [], []
                for piece, blocks in zip(received, places(group, core, rep)):
                    for n, (place, owner, of_rep) in enumerate(blocks):
                        d_low = jnp.array(LOWS[group])[place]
                        for j in range(n_high):
                            at = ((high ^ j) * N_LOW + (low ^ d_low)) * 2 + owner
                            rows_at.append(at * n_rep + of_rep)
                            values.append(piece[n, j])
                full = jnp.zeros((2 * n_seq, half, experts), bf16)
                full = full.at[jnp.stack(rows_at)].set(jnp.stack(values))
                full = full.reshape(n_seq * rows, experts)
                part = jnp.dot(acts, full, preferred_element_type=f32)
                logits = part if logits is None else (logits + part).astype(bf16)
        return *state, logits

    rows_of, tokens_of = P(AXES[:3], None), P(AXES, None)
    return jax.shard_map(
        per_device,
        mesh=fine,
        in_specs=(tokens_of, tokens_of, rows_of, rows_of, rows_of, P()),
        out_specs=(rows_of, rows_of, rows_of, tokens_of),
        check_vma=False,
    )
```

```python
import functools

import jax
import jax.numpy as jnp
from jax import lax
from jax.experimental import pallas as pl
from jax.experimental.pallas import tpu as pltpu
from jax.sharding import Mesh
from jax.sharding import PartitionSpec as P

AXES = ("high", "low", "core", "rep")
N_LOW = 4
CHIPS = ((1, 0), (2, 1), (2, 0), (1, 1), (0, 1), (3, 0), (3, 1), (0, 0))
LOWS = ((1, 2), (0, 3))
NEXT = ((1, 0), (2, 0), (0, 1))
VMEM_LIMIT = 8 * 2**20


def position():
    return [lax.axis_index(axis) for axis in AXES]


def adamw(grad, master, moment_one, moment_two, step_count):
    count = step_count[0].astype(jnp.float32)
    beta_one = 0.9
    beta_two = 0.95
    first = beta_one * moment_one + (1.0 - beta_one) * grad
    second = beta_two * moment_two + (1.0 - beta_two) * grad * grad
    first_hat = first / (1.0 - jnp.power(beta_one, count))
    second_hat = second / (1.0 - jnp.power(beta_two, count))
    updated = master - 0.01 * (first_hat / (jnp.sqrt(second_hat) + 1e-08) + 0.1 * master)
    return updated, first, second


def load_columns(acts_ref, slices, sems, lows, n_high, wide):
    high, low, _, _ = position()
    copies = []
    for p, k in enumerate(lows):
        for j in range(n_high):
            column = pl.multiple_of(((high ^ j) * N_LOW + (low ^ k)) * wide, wide)
            n = p * n_high + j
            copy = pltpu.make_async_copy(acts_ref.at[:, pl.ds(column, wide)], slices(n), sems.at[n])
            copy.start()
            copies.append(copy)
    return copies


def sort_products(n_high, group, turned, columns, away, kept, blocks, arrived):
    _, _, core, rep = position()
    for n in range(2 * n_high):
        arrived(n)
        product = jnp.dot(turned, columns[n], preferred_element_type=jnp.float32)
        blocks[...] = product.astype(blocks.dtype).T.reshape(blocks.shape)
        p, j = divmod(n, n_high)
        for d_rep in range(2):
            chip = CHIPS.index((LOWS[group][p], d_rep)) - 4 * group
            for out, owner in ((kept, core), (away, 1 - core)):
                out[chip, j] = blocks[owner, rep ^ d_rep]


def first_grad_kernel(n_high, acts_ref, grad_ref, *refs):
    state_refs, refs = refs[:3], refs[3:]
    away, kept, mine_ref, later_ref, turned_ref, columns, logit_grads, blocks, sems = refs
    _, _, _, rep = position()
    half = blocks.shape[2]
    loads = pltpu.make_async_copy(grad_ref, logit_grads, sems.at[2, 0])
    loads.start()
    first = load_columns(acts_ref, lambda n: columns.at[n], sems.at[0], LOWS[1], n_high, 4 * half)
    others = load_columns(acts_ref, lambda n: later_ref.at[n], sems.at[1], LOWS[0], n_high, 4 * half)
    rows = pl.ds(pl.multiple_of(rep * half, half), half)
    for i, ref in enumerate(state_refs):
        copy = pltpu.make_async_copy(ref.at[rows], mine_ref.at[i], sems.at[2, 1 + i])
        copy.start()
        others.append(copy)
    loads.wait()
    turned = logit_grads[...].T
    turned_ref[...] = turned

    def arrived(n):
        if n % 2 == 0:
            first[n].wait()
            first[n + 1].wait()

    sort_products(n_high, 1, turned, columns, away, kept, blocks, arrived)
    for copy in others:
        copy.wait()


def second_grad_kernel(n_high, columns, turned_ref, away, kept, blocks):
    sort_products(n_high, 0, turned_ref[...], columns, away, kept, blocks, lambda n: None)


def columns_kernel(n_high, wide, acts_ref, first_ref, second_ref, sems):
    copies = []
    for i, (lows, out) in enumerate(zip(LOWS, (first_ref, second_ref))):
        slices = lambda n, out=out: out.at[:, pl.ds(n * wide, wide)]
        copies += load_columns(acts_ref, slices, sems.at[i], lows, n_high, wide)
    for copy in copies:
        copy.wait()


def logits_kernel(n_high, group, columns_ref, *refs):
    *pieces, out_ref, weight = refs
    before = None
    if len(pieces[-1].shape) == 2:
        *pieces, before = pieces
    _, _, core, rep = position()
    half, experts = weight.shape[-2:]
    for piece, blocks in zip(pieces, places(group, core, rep)):
        for n, (place, owner, of_rep) in enumerate(blocks):
            for j in range(n_high):
                weight[place, j, owner, of_rep] = piece[n, j]
    total = jnp.dot(
        columns_ref[...],
        weight[...].reshape(8 * n_high * half, experts),
        preferred_element_type=jnp.float32,
    )
    if before is not None:
        total = total + before[...]
    out_ref[...] = total.astype(out_ref.dtype)


def places(group, core, rep):
    pieces = []
    for by in (core, 1 - core):
        blocks = []
        for chip in NEXT[:2] if group == 0 else NEXT[2:]:
            place = LOWS[group].index(chip[0]) ^ by
            blocks += [(place, owner, rep ^ chip[1] ^ by) for owner in range(2)]
        if group == 1:
            blocks.append((1, by, rep ^ 1))
        pieces.append(blocks)
    if group == 1:
        pieces += [[(0, owner, rep)] for owner in (core, 1 - core)]
    return pieces


def solution(mesh):
    n_seq, n_rep = mesh.shape["seq"], mesh.shape["rep"]
    n_high = n_seq // (2 * N_LOW)
    fine = Mesh(mesh.devices.reshape(n_high, N_LOW, 2, n_rep), AXES)

    def swap(x, axis, mask=1):
        return lax.ppermute(x, axis, [(i, i ^ mask) for i in range(fine.shape[axis])])

    def cube_swap(x, change):
        pairs = []
        for low in range(N_LOW):
            for core in range(2):
                d_low, d_rep = change(core)
                for rep in range(n_rep):
                    there = ((low ^ d_low) * 2 + core) * n_rep + (rep ^ d_rep)
                    pairs.append(((low * 2 + core) * n_rep + rep, there))
        return lax.ppermute(x, AXES[1:], pairs)

    def to_neighbour(x, axis):
        change = {"x": (1, 0), "z": (2, 0), "y": (0, 1)}[axis]
        return cube_swap(x, lambda core: change)

    def to_next(x, slot):
        d_low, d_rep = NEXT[slot]
        return cube_swap(x, lambda core: (d_low ^ (3 * core), d_rep ^ core))

    def to_corner(x):
        return cube_swap(x, lambda core: (3, 1))

    def per_device(acts, grad_logits, master, moment_one, moment_two, step_count):
        tokens, experts = grad_logits.shape
        rows = master.shape[0]
        half = rows // n_rep
        high, low, core, rep = position()
        f32, bf16 = jnp.float32, jnp.bfloat16
        in_kernels = half % 16 == 0 and (4 * half) % 128 == 0

        vmem = pl.BlockSpec(memory_space=pltpu.VMEM)
        anywhere = pl.BlockSpec(memory_space=pl.ANY)
        params = pltpu.CompilerParams(vmem_limit_bytes=VMEM_LIMIT)
        state_in = (master, moment_one, moment_two)

        if in_kernels:
            acts = pltpu.with_memory_space_constraint(acts, pltpu.HBM)
            shape = pltpu.VMEM((4, n_high, half, experts), bf16)
            columns_shape = pltpu.VMEM((2 * n_high, tokens, 4 * half), bf16)
            blocks = pltpu.VMEM((2, 2, half, experts), bf16)
            turned = pltpu.VMEM((experts, tokens), bf16)
            away_second, kept_second, mine, later, turned = pl.pallas_call(
                functools.partial(first_grad_kernel, n_high),
                out_shape=[shape, shape, pltpu.VMEM((3, half, experts), f32), columns_shape, turned],
                in_specs=[anywhere] * 5,
                out_specs=[vmem] * 5,
                scratch_shapes=[
                    columns_shape,
                    pltpu.VMEM((tokens, experts), bf16),
                    blocks,
                    pltpu.SemaphoreType.DMA((3, max(2 * n_high, 4))),
                ],
                compiler_params=params,
            )(
                acts,
                *(pltpu.with_memory_space_constraint(x, pltpu.HBM) for x in (grad_logits, *state_in)),
            )
            away_first, kept_first = pl.pallas_call(
                functools.partial(second_grad_kernel, n_high),
                out_shape=[shape, shape],
                in_specs=[vmem, vmem],
                out_specs=[vmem] * 2,
                scratch_shapes=[blocks],
                cost_estimate=pl.CostEstimate(
                    flops=4 * n_high * tokens * experts * 4 * half,
                    bytes_accessed=4 * n_high * tokens * 4 * half,
                    transcendentals=0,
                ),
                compiler_params=params,
            )(*(pltpu.with_memory_space_constraint(x, pltpu.VMEM) for x in (later, turned)))
            away, kept = (away_first, away_second), (kept_first, kept_second)
        else:
            product = lax.dot_general(
                acts, grad_logits, (((0,), (0,)), ((), ())), preferred_element_type=f32
            ).astype(bf16)
            product = product.reshape(n_high, N_LOW, 2, n_rep, half, experts)
            product = product[high ^ jnp.arange(n_high)]

            def sort_rows(owner):
                blocks = []
                for d_low, d_rep in CHIPS:
                    at = (0, low ^ d_low, owner, rep ^ d_rep, 0, 0)
                    part = lax.dynamic_slice(product, at, (n_high, 1, 1, 1, half, experts))
                    blocks.append(part.reshape(n_high, half, experts))
                return jnp.stack(blocks[:4]), jnp.stack(blocks[4:])

            away, kept = sort_rows(1 - core), sort_rows(core)
            mine = jnp.stack([lax.dynamic_slice_in_dim(x, rep * half, half, 0) for x in state_in])

        arrived = swap(away[1], "core")
        arrived, away_first = lax.optimization_barrier((arrived, away[0]))
        arrived = swap(away_first, "core"), arrived
        (x, yz, z, xy), (y, zx, corner, home) = [
            own.astype(f32) + theirs.astype(f32) for own, theirs in zip(kept, arrived)
        ]
        zx, yz, xy = [
            to_neighbour(part.astype(bf16), axis) for part, axis in ((zx, "x"), (yz, "z"), (xy, "y"))
        ]
        yz, corner = lax.optimization_barrier((yz, corner.astype(bf16)))
        corner = to_corner(corner)
        z, y, x = z + zx.astype(f32), y + yz.astype(f32), x + xy.astype(f32)
        parts = [to_neighbour(part.astype(bf16), axis) for part, axis in ((z, "z"), (y, "y"), (x, "x"))]
        parts = lax.optimization_barrier((corner, *parts))
        total = home + sum(part.astype(f32) for part in parts)

        grad = total[0]
        for j in range(1, n_high):
            grad = grad + swap(total[j].astype(bf16), "high", j).astype(f32)
        weight = adamw(grad, *mine, step_count)[0].astype(bf16)

        column = jnp.stack([swap(weight, "high", j) if j else weight for j in range(n_high)])
        other = swap(grad, "rep")
        across = swap(column, "core")
        across, other = lax.optimization_barrier((across, other))
        corner = to_corner(column)
        chip = jnp.where(core == 0, jnp.stack([column, across]), jnp.stack([across, column]))
        got = [to_next(chip, slot) for slot in range(3)]

        whole = jnp.where(
            rep == 0,
            jnp.concatenate([grad, other], 0),
            jnp.concatenate([other, grad], 0),
        )
        state = adamw(whole, *state_in, step_count)

        columns = [None, None]
        if in_kernels:
            state, late_acts = lax.optimization_barrier((state, acts))
            columns = pl.pallas_call(
                functools.partial(columns_kernel, n_high, 4 * half),
                out_shape=(pltpu.VMEM((tokens, 8 * n_high * half), bf16),) * 2,
                in_specs=[anywhere],
                out_specs=(vmem, vmem),
                scratch_shapes=[pltpu.SemaphoreType.DMA((2, 2 * n_high))],
                compiler_params=params,
            )(pltpu.with_memory_space_constraint(late_acts, pltpu.HBM))
        got[0], corner, state, columns = lax.optimization_barrier((got[0], corner, state, columns))
        first, second = jnp.concatenate(got[:2]), jnp.concatenate([got[2], corner[None]])
        first, second = [first, swap(first, "core")], [second, swap(second, "core")]
        second += [column[None], across[None]]
        pieces = (first, second)
        logits = None
        for group, (received, acts_columns) in enumerate(zip(pieces, columns)):
            if in_kernels:
                before = [] if logits is None else [logits]
                operands = [
                    pltpu.with_memory_space_constraint(x, pltpu.VMEM) for x in [acts_columns] + received + before
                ]
                logits = pl.pallas_call(
                    functools.partial(logits_kernel, n_high, group),
                    out_shape=jax.ShapeDtypeStruct((tokens, experts), bf16 if before else f32),
                    in_specs=[vmem] * len(operands),
                    out_specs=vmem,
                    scratch_shapes=[pltpu.VMEM((2, n_high, 2, 2, half, experts), bf16)],
                    compiler_params=params,
                )(*operands)
            else:
                rows_at, values = [], []
                for piece, blocks in zip(received, places(group, core, rep)):
                    for n, (place, owner, of_rep) in enumerate(blocks):
                        d_low = jnp.array(LOWS[group])[place]
                        for j in range(n_high):
                            at = ((high ^ j) * N_LOW + (low ^ d_low)) * 2 + owner
                            rows_at.append(at * n_rep + of_rep)
                            values.append(piece[n, j])
                full = jnp.zeros((2 * n_seq, half, experts), bf16)
                full = full.at[jnp.stack(rows_at)].set(jnp.stack(values))
                full = full.reshape(n_seq * rows, experts)
                part = jnp.dot(acts, full, preferred_element_type=f32)
                logits = part if logits is None else (logits + part).astype(bf16)
        return *state, logits

    rows_of, tokens_of = P(AXES[:3], None), P(AXES, None)
    return jax.shard_map(
        per_device,
        mesh=fine,
        in_specs=(tokens_of, tokens_of, rows_of, rows_of, rows_of, P()),
        out_specs=(rows_of, rows_of, rows_of, tokens_of),
        check_vma=False,
    )
```

```python
import functools

import jax
import jax.numpy as jnp
from jax import lax
from jax.experimental import pallas as pl
from jax.experimental.pallas import tpu as pltpu
from jax.sharding import Mesh
from jax.sharding import PartitionSpec as P

AXES = ("high", "low", "core", "rep")
N_LOW = 4
CHIPS = ((1, 0), (2, 1), (2, 0), (1, 1), (0, 1), (3, 0), (3, 1), (0, 0))
LOWS = ((1, 2), (0, 3))
NEXT = ((1, 0), (2, 0), (0, 1))
VMEM_LIMIT = 8 * 2**20


def slot_of(chip, core):
    slot = CHIPS.index(chip)
    return slot if slot >= 6 else slot ^ core


def position():
    return [lax.axis_index(axis) for axis in AXES]


def adamw(grad, master, moment_one, moment_two, step_count):
    count = step_count[0].astype(jnp.float32)
    beta_one = 0.9
    beta_two = 0.95
    first = beta_one * moment_one + (1.0 - beta_one) * grad
    second = beta_two * moment_two + (1.0 - beta_two) * grad * grad
    first_hat = first / (1.0 - jnp.power(beta_one, count))
    second_hat = second / (1.0 - jnp.power(beta_two, count))
    updated = master - 0.01 * (first_hat / (jnp.sqrt(second_hat) + 1e-08) + 0.1 * master)
    return updated, first, second


def load_columns(acts_ref, slices, sems, lows, n_high, wide):
    high, low, _, _ = position()
    copies = []
    for p, k in enumerate(lows):
        for j in range(n_high):
            column = pl.multiple_of(((high ^ j) * N_LOW + (low ^ k)) * wide, wide)
            n = p * n_high + j
            copy = pltpu.make_async_copy(acts_ref.at[:, pl.ds(column, wide)], slices(n), sems.at[n])
            copy.start()
            copies.append(copy)
    return copies


def sort_products(n_high, group, turned, columns, away, kept, blocks, arrived):
    _, _, core, rep = position()
    for n in range(2 * n_high):
        arrived(n)
        product = jnp.dot(turned, columns[n], preferred_element_type=jnp.float32)
        blocks[...] = product.astype(blocks.dtype).T.reshape(blocks.shape)
        p, j = divmod(n, n_high)
        for d_rep in range(2):
            chip = LOWS[group][p], d_rep
            left = CHIPS.index(chip) >= 6
            for outs, owner in ((kept, core), (away, 1 - core)):
                outs[left][slot_of(chip, owner) - (6 if left else 4 * group), j] = blocks[owner, rep ^ d_rep]


def first_grad_kernel(n_high, acts_ref, grad_ref, *refs):
    state_refs, refs = refs[:3], refs[3:]
    away, kept, refs = refs[:2], refs[2:4], refs[4:]
    mine_ref, later_ref, turned_ref, columns, logit_grads, blocks, sems = refs
    _, _, _, rep = position()
    half = blocks.shape[2]
    loads = pltpu.make_async_copy(grad_ref, logit_grads, sems.at[2, 0])
    loads.start()
    first = load_columns(acts_ref, lambda n: columns.at[n], sems.at[0], LOWS[1], n_high, 4 * half)
    others = load_columns(acts_ref, lambda n: later_ref.at[n], sems.at[1], LOWS[0], n_high, 4 * half)
    rows = pl.ds(pl.multiple_of(rep * half, half), half)
    for i, ref in enumerate(state_refs):
        copy = pltpu.make_async_copy(ref.at[rows], mine_ref.at[i], sems.at[2, 1 + i])
        copy.start()
        others.append(copy)
    loads.wait()
    turned = logit_grads[...].T
    turned_ref[...] = turned

    def arrived(n):
        if n % 2 == 0:
            first[n].wait()
            first[n + 1].wait()

    sort_products(n_high, 1, turned, columns, away, kept, blocks, arrived)
    for copy in others:
        copy.wait()


def second_grad_kernel(n_high, columns, turned_ref, away, kept, blocks):
    sort_products(n_high, 0, turned_ref[...], columns, [away], [kept], blocks, lambda n: None)


def columns_kernel(n_high, wide, acts_ref, first_ref, second_ref, sems):
    copies = []
    for i, (lows, out) in enumerate(zip(LOWS, (first_ref, second_ref))):
        slices = lambda n, out=out: out.at[:, pl.ds(n * wide, wide)]
        copies += load_columns(acts_ref, slices, sems.at[i], lows, n_high, wide)
    for copy in copies:
        copy.wait()


def logits_kernel(n_high, group, columns_ref, *refs):
    *pieces, out_ref, weight = refs
    before = None
    if len(pieces[-1].shape) == 2:
        *pieces, before = pieces
    _, _, core, rep = position()
    half, experts = weight.shape[-2:]
    for piece, blocks in zip(pieces, places(group, core, rep)):
        for n, (place, owner, of_rep) in enumerate(blocks):
            for j in range(n_high):
                weight[place, j, owner, of_rep] = piece[n, j]
    total = jnp.dot(
        columns_ref[...],
        weight[...].reshape(8 * n_high * half, experts),
        preferred_element_type=jnp.float32,
    )
    if before is not None:
        total = total + before[...]
    out_ref[...] = total.astype(out_ref.dtype)


def places(group, core, rep):
    pieces = []
    for by in (core, 1 - core):
        blocks = []
        for chip in NEXT[:2] if group == 0 else NEXT[2:]:
            place = LOWS[group].index(chip[0]) ^ by
            blocks += [(place, owner, rep ^ chip[1] ^ by) for owner in range(2)]
        pieces.append(blocks)
    if group == 1:
        pieces += [[(1, owner, rep ^ 1)] for owner in (core, 1 - core)]
        pieces += [[(0, owner, rep)] for owner in (core, 1 - core)]
    return pieces


def solution(mesh):
    n_seq, n_rep = mesh.shape["seq"], mesh.shape["rep"]
    n_high = n_seq // (2 * N_LOW)
    fine = Mesh(mesh.devices.reshape(n_high, N_LOW, 2, n_rep), AXES)

    def swap(x, axis, mask=1):
        return lax.ppermute(x, axis, [(i, i ^ mask) for i in range(fine.shape[axis])])

    def cube_swap(x, change):
        pairs = []
        for low in range(N_LOW):
            for core in range(2):
                d_low, d_rep = change(core)
                for rep in range(n_rep):
                    there = ((low ^ d_low) * 2 + core) * n_rep + (rep ^ d_rep)
                    pairs.append(((low * 2 + core) * n_rep + rep, there))
        return lax.ppermute(x, AXES[1:], pairs)

    def to_slot(x, slot):
        return cube_swap(x, lambda core: CHIPS[slot ^ core if slot < 6 else slot])

    def to_next(x, slot):
        d_low, d_rep = NEXT[slot]
        return cube_swap(x, lambda core: (d_low ^ (3 * core), d_rep ^ core))

    def to_corner(x):
        return cube_swap(x, lambda core: (3, 1))

    def per_device(acts, grad_logits, master, moment_one, moment_two, step_count):
        tokens, experts = grad_logits.shape
        rows = master.shape[0]
        half = rows // n_rep
        high, low, core, rep = position()
        f32, bf16 = jnp.float32, jnp.bfloat16
        in_kernels = half % 16 == 0 and (4 * half) % 128 == 0

        vmem = pl.BlockSpec(memory_space=pltpu.VMEM)
        anywhere = pl.BlockSpec(memory_space=pl.ANY)
        params = pltpu.CompilerParams(vmem_limit_bytes=VMEM_LIMIT)
        state_in = (master, moment_one, moment_two)

        if in_kernels:
            acts = pltpu.with_memory_space_constraint(acts, pltpu.HBM)
            shape = pltpu.VMEM((4, n_high, half, experts), bf16)
            columns_shape = pltpu.VMEM((2 * n_high, tokens, 4 * half), bf16)
            blocks = pltpu.VMEM((2, 2, half, experts), bf16)
            turned = pltpu.VMEM((experts, tokens), bf16)
            pair = pltpu.VMEM((2, n_high, half, experts), bf16)
            *sorted_rows, mine, later, turned = pl.pallas_call(
                functools.partial(first_grad_kernel, n_high),
                out_shape=[pair] * 4 + [pltpu.VMEM((3, half, experts), f32), columns_shape, turned],
                in_specs=[anywhere] * 5,
                out_specs=[vmem] * 7,
                scratch_shapes=[
                    columns_shape,
                    pltpu.VMEM((tokens, experts), bf16),
                    blocks,
                    pltpu.SemaphoreType.DMA((3, max(2 * n_high, 4))),
                ],
                compiler_params=params,
            )(
                acts,
                *(pltpu.with_memory_space_constraint(x, pltpu.HBM) for x in (grad_logits, *state_in)),
            )
            away_first, kept_first = pl.pallas_call(
                functools.partial(second_grad_kernel, n_high),
                out_shape=[shape, shape],
                in_specs=[vmem, vmem],
                out_specs=[vmem] * 2,
                scratch_shapes=[blocks],
                cost_estimate=pl.CostEstimate(
                    flops=4 * n_high * tokens * experts * 4 * half,
                    bytes_accessed=4 * n_high * tokens * 4 * half,
                    transcendentals=0,
                ),
                compiler_params=params,
            )(*(pltpu.with_memory_space_constraint(x, pltpu.VMEM) for x in (later, turned)))
            away, kept = (*sorted_rows[:2], away_first), (*sorted_rows[2:], kept_first)
        else:
            product = lax.dot_general(
                acts, grad_logits, (((0,), (0,)), ((), ())), preferred_element_type=f32
            ).astype(bf16)
            product = product.reshape(n_high, N_LOW, 2, n_rep, half, experts)
            product = product[high ^ jnp.arange(n_high)]

            def sort_rows(owner):
                blocks = []
                for slot in range(8):
                    flip = owner if slot < 6 else 0
                    d_low, d_rep = CHIPS[slot]
                    at = (0, low ^ d_low ^ (3 * flip), owner, rep ^ d_rep ^ flip, 0, 0)
                    part = lax.dynamic_slice(product, at, (n_high, 1, 1, 1, half, experts))
                    blocks.append(part.reshape(n_high, half, experts))
                return jnp.stack(blocks[4:6]), jnp.stack(blocks[6:]), jnp.stack(blocks[:4])

            away, kept = sort_rows(1 - core), sort_rows(core)
            mine = jnp.stack([lax.dynamic_slice_in_dim(x, rep * half, half, 0) for x in state_in])

        arrived = swap(away[0], "core")
        arrived, *rest = lax.optimization_barrier((arrived, *away[1:]))
        arrived = [arrived] + [swap(x, "core") for x in rest]
        pair, left, first = [own.astype(f32) + x.astype(f32) for own, x in zip(kept, arrived)]
        parts = [to_slot(x.astype(bf16), 4 + n) for n, x in enumerate(pair)]
        parts += [to_slot(left[0].astype(bf16), 6)]
        parts += [to_slot(x.astype(bf16), n) for n, x in enumerate(first)]
        parts = [left[1], *lax.optimization_barrier(parts)]
        total = sum(x.astype(f32) for x in parts)

        grad = total[0]
        for j in range(1, n_high):
            grad = grad + swap(total[j].astype(bf16), "high", j).astype(f32)
        weight = adamw(grad, *mine, step_count)[0].astype(bf16)

        column = jnp.stack([swap(weight, "high", j) if j else weight for j in range(n_high)])
        other = swap(grad, "rep")
        across = swap(column, "core")
        across, other = lax.optimization_barrier((across, other))
        corner = to_corner(column)
        chip = jnp.where(core == 0, jnp.stack([column, across]), jnp.stack([across, column]))
        got = [to_next(chip, slot) for slot in range(3)]

        whole = jnp.where(
            rep == 0,
            jnp.concatenate([grad, other], 0),
            jnp.concatenate([other, grad], 0),
        )
        state = adamw(whole, *state_in, step_count)

        columns = [None, None]
        if in_kernels:
            state, late_acts = lax.optimization_barrier((state, acts))
            columns = pl.pallas_call(
                functools.partial(columns_kernel, n_high, 4 * half),
                out_shape=(pltpu.VMEM((tokens, 8 * n_high * half), bf16),) * 2,
                in_specs=[anywhere],
                out_specs=(vmem, vmem),
                scratch_shapes=[pltpu.SemaphoreType.DMA((2, 2 * n_high))],
                compiler_params=params,
            )(pltpu.with_memory_space_constraint(late_acts, pltpu.HBM))
        got, corner, state, columns = lax.optimization_barrier((got, corner, state, columns))
        first, second = jnp.concatenate([*got[:2], corner[None]]), got[2]
        first_over, second_over = swap(first, "core"), swap(second, "core")
        pieces = (
            [first, first_over],
            [second, second_over, corner[None], first_over[4:], column[None], across[None]],
        )
        logits = None
        for group, (received, acts_columns) in enumerate(zip(pieces, columns)):
            if in_kernels:
                before = [] if logits is None else [logits]
                operands = [
                    pltpu.with_memory_space_constraint(x, pltpu.VMEM) for x in [acts_columns] + received + before
                ]
                logits = pl.pallas_call(
                    functools.partial(logits_kernel, n_high, group),
                    out_shape=jax.ShapeDtypeStruct((tokens, experts), bf16 if before else f32),
                    in_specs=[vmem] * len(operands),
                    out_specs=vmem,
                    scratch_shapes=[pltpu.VMEM((2, n_high, 2, 2, half, experts), bf16)],
                    compiler_params=params,
                )(*operands)
            else:
                rows_at, values = [], []
                for piece, blocks in zip(received, places(group, core, rep)):
                    for n, (place, owner, of_rep) in enumerate(blocks):
                        d_low = jnp.array(LOWS[group])[place]
                        for j in range(n_high):
                            at = ((high ^ j) * N_LOW + (low ^ d_low)) * 2 + owner
                            rows_at.append(at * n_rep + of_rep)
                            values.append(piece[n, j])
                full = jnp.zeros((2 * n_seq, half, experts), bf16)
                full = full.at[jnp.stack(rows_at)].set(jnp.stack(values))
                full = full.reshape(n_seq * rows, experts)
                part = jnp.dot(acts, full, preferred_element_type=f32)
                logits = part if logits is None else (logits + part).astype(bf16)
        return *state, logits

    rows_of, tokens_of = P(AXES[:3], None), P(AXES, None)
    return jax.shard_map(
        per_device,
        mesh=fine,
        in_specs=(tokens_of, tokens_of, rows_of, rows_of, rows_of, P()),
        out_specs=(rows_of, rows_of, rows_of, tokens_of),
        check_vma=False,
    )
```

```python
import functools

import jax
import jax.numpy as jnp
from jax import lax
from jax.experimental import pallas as pl
from jax.experimental.pallas import tpu as pltpu
from jax.sharding import Mesh
from jax.sharding import PartitionSpec as P

AXES = ("high", "low", "core", "rep")
N_LOW = 4
CHIPS = ((1, 0), (2, 1), (2, 0), (1, 1), (0, 1), (3, 0), (3, 1), (0, 0))
LOWS = ((1, 2), (0, 3))
NEXT = ((1, 0), (2, 0), (0, 1))
VMEM_LIMIT = 8 * 2**20


def slot_of(chip, core):
    slot = CHIPS.index(chip)
    return slot if slot >= 6 else slot ^ core


def position():
    return [lax.axis_index(axis) for axis in AXES]


def adamw(grad, master, moment_one, moment_two, step_count):
    count = step_count[0].astype(jnp.float32)
    beta_one = 0.9
    beta_two = 0.95
    first = beta_one * moment_one + (1.0 - beta_one) * grad
    second = beta_two * moment_two + (1.0 - beta_two) * grad * grad
    first_hat = first / (1.0 - jnp.power(beta_one, count))
    second_hat = second / (1.0 - jnp.power(beta_two, count))
    updated = master - 0.01 * (first_hat / (jnp.sqrt(second_hat) + 1e-08) + 0.1 * master)
    return updated, first, second


def load_columns(acts_ref, slices, sems, lows, n_high, wide):
    high, low, _, _ = position()
    copies = []
    for p, k in enumerate(lows):
        for j in range(n_high):
            column = pl.multiple_of(((high ^ j) * N_LOW + (low ^ k)) * wide, wide)
            n = p * n_high + j
            copy = pltpu.make_async_copy(acts_ref.at[:, pl.ds(column, wide)], slices(n), sems.at[n])
            copy.start()
            copies.append(copy)
    return copies


def sort_products(n_high, group, turned, columns, away, kept, blocks, arrived):
    _, _, core, rep = position()
    for n in range(2 * n_high):
        arrived(n)
        product = jnp.dot(turned, columns[n], preferred_element_type=jnp.float32)
        blocks[...] = product.astype(blocks.dtype).T.reshape(blocks.shape)
        p, j = divmod(n, n_high)
        for d_rep in range(2):
            chip = LOWS[group][p], d_rep
            left = CHIPS.index(chip) >= 6
            for outs, owner in ((kept, core), (away, 1 - core)):
                outs[left][slot_of(chip, owner) - (6 if left else 4 * group), j] = blocks[owner, rep ^ d_rep]


def first_grad_kernel(n_high, acts_ref, grad_ref, *refs):
    state_refs, refs = refs[:3], refs[3:]
    away, kept, refs = refs[:2], refs[2:4], refs[4:]
    mine_ref, later_ref, turned_ref, columns, logit_grads, blocks, sems = refs
    _, _, _, rep = position()
    half = blocks.shape[2]
    loads = pltpu.make_async_copy(grad_ref, logit_grads, sems.at[2, 0])
    loads.start()
    first = load_columns(acts_ref, lambda n: columns.at[n], sems.at[0], LOWS[1], n_high, 4 * half)
    others = load_columns(acts_ref, lambda n: later_ref.at[n], sems.at[1], LOWS[0], n_high, 4 * half)
    rows = pl.ds(pl.multiple_of(rep * half, half), half)
    for i, ref in enumerate(state_refs):
        copy = pltpu.make_async_copy(ref.at[rows], mine_ref.at[i], sems.at[2, 1 + i])
        copy.start()
        others.append(copy)
    loads.wait()
    turned = logit_grads[...].T
    turned_ref[...] = turned

    def arrived(n):
        if n % 2 == 0:
            first[n].wait()
            first[n + 1].wait()

    sort_products(n_high, 1, turned, columns, away, kept, blocks, arrived)
    for copy in others:
        copy.wait()


def second_grad_kernel(n_high, columns, turned_ref, away, kept, blocks):
    sort_products(n_high, 0, turned_ref[...], columns, [away], [kept], blocks, lambda n: None)


def columns_kernel(n_high, wide, acts_ref, first_ref, second_ref, sems):
    copies = []
    for i, (lows, out) in enumerate(zip(LOWS, (first_ref, second_ref))):
        slices = lambda n, out=out: out.at[:, pl.ds(n * wide, wide)]
        copies += load_columns(acts_ref, slices, sems.at[i], lows, n_high, wide)
    for copy in copies:
        copy.wait()


def logits_kernel(n_high, group, columns_ref, *refs):
    *pieces, out_ref, weight = refs
    before = None
    if len(pieces[-1].shape) == 2:
        *pieces, before = pieces
    _, _, core, rep = position()
    half, experts = weight.shape[-2:]
    for piece, blocks in zip(pieces, places(group, core, rep)):
        for n, (place, owner, of_rep) in enumerate(blocks):
            for j in range(n_high):
                weight[place, j, owner, of_rep] = piece[n, j]
    total = jnp.dot(
        columns_ref[...],
        weight[...].reshape(8 * n_high * half, experts),
        preferred_element_type=jnp.float32,
    )
    if before is not None:
        total = total + before[...]
    out_ref[...] = total.astype(out_ref.dtype)


def places(group, core, rep):
    pieces = []
    for by in (core, 1 - core):
        blocks = []
        for chip in NEXT[:2] if group == 0 else NEXT[2:]:
            place = LOWS[group].index(chip[0]) ^ by
            blocks += [(place, owner, rep ^ chip[1] ^ by) for owner in range(2)]
        if group == 1:
            blocks.append((1, by, rep ^ 1))
        pieces.append(blocks)
    if group == 1:
        pieces += [[(0, owner, rep)] for owner in (core, 1 - core)]
    return pieces


def solution(mesh):
    n_seq, n_rep = mesh.shape["seq"], mesh.shape["rep"]
    n_high = n_seq // (2 * N_LOW)
    fine = Mesh(mesh.devices.reshape(n_high, N_LOW, 2, n_rep), AXES)

    def swap(x, axis, mask=1):
        return lax.ppermute(x, axis, [(i, i ^ mask) for i in range(fine.shape[axis])])

    def cube_swap(x, change):
        pairs = []
        for low in range(N_LOW):
            for core in range(2):
                d_low, d_rep = change(core)
                for rep in range(n_rep):
                    there = ((low ^ d_low) * 2 + core) * n_rep + (rep ^ d_rep)
                    pairs.append(((low * 2 + core) * n_rep + rep, there))
        return lax.ppermute(x, AXES[1:], pairs)

    def to_slot(x, slot):
        return cube_swap(x, lambda core: CHIPS[slot ^ core if slot < 6 else slot])

    def to_next(x, slot):
        d_low, d_rep = NEXT[slot]
        return cube_swap(x, lambda core: (d_low ^ (3 * core), d_rep ^ core))

    def to_corner(x):
        return cube_swap(x, lambda core: (3, 1))

    def per_device(acts, grad_logits, master, moment_one, moment_two, step_count):
        tokens, experts = grad_logits.shape
        rows = master.shape[0]
        half = rows // n_rep
        high, low, core, rep = position()
        f32, bf16 = jnp.float32, jnp.bfloat16
        in_kernels = half % 16 == 0 and (4 * half) % 128 == 0

        vmem = pl.BlockSpec(memory_space=pltpu.VMEM)
        anywhere = pl.BlockSpec(memory_space=pl.ANY)
        params = pltpu.CompilerParams(vmem_limit_bytes=VMEM_LIMIT)
        state_in = (master, moment_one, moment_two)

        if in_kernels:
            acts = pltpu.with_memory_space_constraint(acts, pltpu.HBM)
            shape = pltpu.VMEM((4, n_high, half, experts), bf16)
            columns_shape = pltpu.VMEM((2 * n_high, tokens, 4 * half), bf16)
            blocks = pltpu.VMEM((2, 2, half, experts), bf16)
            turned = pltpu.VMEM((experts, tokens), bf16)
            pair = pltpu.VMEM((2, n_high, half, experts), bf16)
            *sorted_rows, mine, later, turned = pl.pallas_call(
                functools.partial(first_grad_kernel, n_high),
                out_shape=[pair] * 4 + [pltpu.VMEM((3, half, experts), f32), columns_shape, turned],
                in_specs=[anywhere] * 5,
                out_specs=[vmem] * 7,
                scratch_shapes=[
                    columns_shape,
                    pltpu.VMEM((tokens, experts), bf16),
                    blocks,
                    pltpu.SemaphoreType.DMA((3, max(2 * n_high, 4))),
                ],
                compiler_params=params,
            )(
                acts,
                *(pltpu.with_memory_space_constraint(x, pltpu.HBM) for x in (grad_logits, *state_in)),
            )
            away_first, kept_first = pl.pallas_call(
                functools.partial(second_grad_kernel, n_high),
                out_shape=[shape, shape],
                in_specs=[vmem, vmem],
                out_specs=[vmem] * 2,
                scratch_shapes=[blocks],
                cost_estimate=pl.CostEstimate(
                    flops=4 * n_high * tokens * experts * 4 * half,
                    bytes_accessed=4 * n_high * tokens * 4 * half,
                    transcendentals=0,
                ),
                compiler_params=params,
            )(*(pltpu.with_memory_space_constraint(x, pltpu.VMEM) for x in (later, turned)))
            away, kept = (*sorted_rows[:2], away_first), (*sorted_rows[2:], kept_first)
        else:
            product = lax.dot_general(
                acts, grad_logits, (((0,), (0,)), ((), ())), preferred_element_type=f32
            ).astype(bf16)
            product = product.reshape(n_high, N_LOW, 2, n_rep, half, experts)
            product = product[high ^ jnp.arange(n_high)]

            def sort_rows(owner):
                blocks = []
                for slot in range(8):
                    flip = owner if slot < 6 else 0
                    d_low, d_rep = CHIPS[slot]
                    at = (0, low ^ d_low ^ (3 * flip), owner, rep ^ d_rep ^ flip, 0, 0)
                    part = lax.dynamic_slice(product, at, (n_high, 1, 1, 1, half, experts))
                    blocks.append(part.reshape(n_high, half, experts))
                return jnp.stack(blocks[4:6]), jnp.stack(blocks[6:]), jnp.stack(blocks[:4])

            away, kept = sort_rows(1 - core), sort_rows(core)
            mine = jnp.stack([lax.dynamic_slice_in_dim(x, rep * half, half, 0) for x in state_in])

        arrived = swap(away[1], "core")
        arrived, *rest = lax.optimization_barrier((arrived, away[0], away[2]))
        arrived = [swap(rest[0], "core"), arrived, swap(rest[1], "core")]
        pair, left, first = [own.astype(f32) + x.astype(f32) for own, x in zip(kept, arrived)]
        corner = cube_swap(left[0].astype(bf16), lambda core: (1, 0)).astype(f32)
        parts = [to_slot(x.astype(bf16), 4 + n) for n, x in enumerate(pair)]
        parts += [to_slot(first[n].astype(bf16), n) for n in (2, 3)]
        for n in range(2):
            part = first[n] + jnp.where(core == 1 - n, corner, 0.0)
            parts.append(to_slot(part.astype(bf16), n))
        parts = [left[1], *lax.optimization_barrier(parts)]
        total = sum(x.astype(f32) for x in parts)

        grad = total[0]
        for j in range(1, n_high):
            grad = grad + swap(total[j].astype(bf16), "high", j).astype(f32)
        weight = adamw(grad, *mine, step_count)[0].astype(bf16)

        column = jnp.stack([swap(weight, "high", j) if j else weight for j in range(n_high)])
        other = swap(grad, "rep")
        across = swap(column, "core")
        across, other = lax.optimization_barrier((across, other))
        corner = to_corner(column)
        chip = jnp.where(core == 0, jnp.stack([column, across]), jnp.stack([across, column]))
        got = [to_next(chip, slot) for slot in range(3)]

        whole = jnp.where(
            rep == 0,
            jnp.concatenate([grad, other], 0),
            jnp.concatenate([other, grad], 0),
        )
        state = adamw(whole, *state_in, step_count)

        columns = [None, None]
        if in_kernels:
            state, late_acts = lax.optimization_barrier((state, acts))
            columns = pl.pallas_call(
                functools.partial(columns_kernel, n_high, 4 * half),
                out_shape=(pltpu.VMEM((tokens, 8 * n_high * half), bf16),) * 2,
                in_specs=[anywhere],
                out_specs=(vmem, vmem),
                scratch_shapes=[pltpu.SemaphoreType.DMA((2, 2 * n_high))],
                compiler_params=params,
            )(pltpu.with_memory_space_constraint(late_acts, pltpu.HBM))
        got[0], corner, state, columns = lax.optimization_barrier((got[0], corner, state, columns))
        first, second = jnp.concatenate(got[:2]), jnp.concatenate([got[2], corner[None]])
        first, second = [first, swap(first, "core")], [second, swap(second, "core")]
        second += [column[None], across[None]]
        pieces = (first, second)
        logits = None
        for group, (received, acts_columns) in enumerate(zip(pieces, columns)):
            if in_kernels:
                before = [] if logits is None else [logits]
                operands = [
                    pltpu.with_memory_space_constraint(x, pltpu.VMEM) for x in [acts_columns] + received + before
                ]
                logits = pl.pallas_call(
                    functools.partial(logits_kernel, n_high, group),
                    out_shape=jax.ShapeDtypeStruct((tokens, experts), bf16 if before else f32),
                    in_specs=[vmem] * len(operands),
                    out_specs=vmem,
                    scratch_shapes=[pltpu.VMEM((2, n_high, 2, 2, half, experts), bf16)],
                    compiler_params=params,
                )(*operands)
            else:
                rows_at, values = [], []
                for piece, blocks in zip(received, places(group, core, rep)):
                    for n, (place, owner, of_rep) in enumerate(blocks):
                        d_low = jnp.array(LOWS[group])[place]
                        for j in range(n_high):
                            at = ((high ^ j) * N_LOW + (low ^ d_low)) * 2 + owner
                            rows_at.append(at * n_rep + of_rep)
                            values.append(piece[n, j])
                full = jnp.zeros((2 * n_seq, half, experts), bf16)
                full = full.at[jnp.stack(rows_at)].set(jnp.stack(values))
                full = full.reshape(n_seq * rows, experts)
                part = jnp.dot(acts, full, preferred_element_type=f32)
                logits = part if logits is None else (logits + part).astype(bf16)
        return *state, logits

    rows_of, tokens_of = P(AXES[:3], None), P(AXES, None)
    return jax.shard_map(
        per_device,
        mesh=fine,
        in_specs=(tokens_of, tokens_of, rows_of, rows_of, rows_of, P()),
        out_specs=(rows_of, rows_of, rows_of, tokens_of),
        check_vma=False,
    )
```

```python
import functools

import jax
import jax.numpy as jnp
from jax import lax
from jax.experimental import pallas as pl
from jax.experimental.pallas import tpu as pltpu
from jax.sharding import Mesh
from jax.sharding import PartitionSpec as P

AXES = ("high", "low", "core", "rep")
N_LOW = 4
CHIPS = ((1, 0), (2, 1), (2, 0), (1, 1), (0, 1), (3, 0), (3, 1), (0, 0))
LOWS = ((1, 2), (0, 3))
NEXT = ((1, 0), (2, 0), (0, 1))
VMEM_LIMIT = 8 * 2**20


def slot_of(chip, core):
    slot = CHIPS.index(chip)
    return slot if slot >= 6 else slot ^ core


def position():
    return [lax.axis_index(axis) for axis in AXES]


def adamw(grad, master, moment_one, moment_two, step_count):
    count = step_count[0].astype(jnp.float32)
    beta_one = 0.9
    beta_two = 0.95
    first = beta_one * moment_one + (1.0 - beta_one) * grad
    second = beta_two * moment_two + (1.0 - beta_two) * grad * grad
    first_hat = first / (1.0 - jnp.power(beta_one, count))
    second_hat = second / (1.0 - jnp.power(beta_two, count))
    updated = master - 0.01 * (first_hat / (jnp.sqrt(second_hat) + 1e-08) + 0.1 * master)
    return updated, first, second


def load_columns(acts_ref, slices, sems, lows, n_high, wide):
    high, low, _, _ = position()
    copies = []
    for p, k in enumerate(lows):
        for j in range(n_high):
            column = pl.multiple_of(((high ^ j) * N_LOW + (low ^ k)) * wide, wide)
            n = p * n_high + j
            copy = pltpu.make_async_copy(acts_ref.at[:, pl.ds(column, wide)], slices(n), sems.at[n])
            copy.start()
            copies.append(copy)
    return copies


def sort_products(n_high, group, turned, columns, away, kept, blocks, arrived):
    _, _, core, rep = position()
    for n in range(2 * n_high):
        arrived(n)
        product = jnp.dot(turned, columns[n], preferred_element_type=jnp.float32)
        blocks[...] = product.astype(blocks.dtype).T.reshape(blocks.shape)
        p, j = divmod(n, n_high)
        for d_rep in range(2):
            chip = LOWS[group][p], d_rep
            left = CHIPS.index(chip) >= 6
            for outs, owner in ((kept, core), (away, 1 - core)):
                outs[left][slot_of(chip, owner) - (6 if left else 4 * group), j] = blocks[owner, rep ^ d_rep]


def first_grad_kernel(n_high, acts_ref, grad_ref, *refs):
    state_refs, refs = refs[:3], refs[3:]
    away, kept, refs = refs[:2], refs[2:4], refs[4:]
    mine_ref, later_ref, turned_ref, columns, logit_grads, blocks, sems = refs
    _, _, _, rep = position()
    half = blocks.shape[2]
    loads = pltpu.make_async_copy(grad_ref, logit_grads, sems.at[2, 0])
    loads.start()
    first = load_columns(acts_ref, lambda n: columns.at[n], sems.at[0], LOWS[1], n_high, 4 * half)
    others = load_columns(acts_ref, lambda n: later_ref.at[n], sems.at[1], LOWS[0], n_high, 4 * half)
    rows = pl.ds(pl.multiple_of(rep * half, half), half)
    for i, ref in enumerate(state_refs):
        copy = pltpu.make_async_copy(ref.at[rows], mine_ref.at[i], sems.at[2, 1 + i])
        copy.start()
        others.append(copy)
    loads.wait()
    turned = logit_grads[...].T
    turned_ref[...] = turned

    def arrived(n):
        if n % 2 == 0:
            first[n].wait()
            first[n + 1].wait()

    sort_products(n_high, 1, turned, columns, away, kept, blocks, arrived)
    for copy in others:
        copy.wait()


def second_grad_kernel(n_high, columns, turned_ref, away, kept, blocks):
    sort_products(n_high, 0, turned_ref[...], columns, [away], [kept], blocks, lambda n: None)


def columns_kernel(n_high, wide, acts_ref, first_ref, second_ref, sems):
    copies = []
    for i, (lows, out) in enumerate(zip(LOWS, (first_ref, second_ref))):
        slices = lambda n, out=out: out.at[:, pl.ds(n * wide, wide)]
        copies += load_columns(acts_ref, slices, sems.at[i], lows, n_high, wide)
    for copy in copies:
        copy.wait()


def logits_kernel(n_high, group, columns_ref, *refs):
    *pieces, out_ref, weight = refs
    before = None
    if len(pieces[-1].shape) == 2:
        *pieces, before = pieces
    _, _, core, rep = position()
    half, experts = weight.shape[-2:]
    for piece, blocks in zip(pieces, places(group, core, rep)):
        for n, (place, owner, of_rep) in enumerate(blocks):
            for j in range(n_high):
                weight[place, j, owner, of_rep] = piece[n, j]
    total = jnp.dot(
        columns_ref[...],
        weight[...].reshape(8 * n_high * half, experts),
        preferred_element_type=jnp.float32,
    )
    if before is not None:
        total = total + before[...]
    out_ref[...] = total.astype(out_ref.dtype)


def places(group, core, rep):
    pieces = []
    for by in (core, 1 - core):
        blocks = []
        for chip in NEXT[:2] if group == 0 else NEXT[2:]:
            place = LOWS[group].index(chip[0]) ^ by
            blocks += [(place, owner, rep ^ chip[1] ^ by) for owner in range(2)]
        if group == 1:
            blocks.append((1, by, rep ^ 1))
        pieces.append(blocks)
    if group == 1:
        pieces += [[(0, owner, rep)] for owner in (core, 1 - core)]
    return pieces


def solution(mesh):
    n_seq, n_rep = mesh.shape["seq"], mesh.shape["rep"]
    n_high = n_seq // (2 * N_LOW)
    fine = Mesh(mesh.devices.reshape(n_high, N_LOW, 2, n_rep), AXES)

    def swap(x, axis, mask=1):
        return lax.ppermute(x, axis, [(i, i ^ mask) for i in range(fine.shape[axis])])

    def cube_swap(x, change):
        pairs = []
        for low in range(N_LOW):
            for core in range(2):
                d_low, d_rep = change(core)
                for rep in range(n_rep):
                    there = ((low ^ d_low) * 2 + core) * n_rep + (rep ^ d_rep)
                    pairs.append(((low * 2 + core) * n_rep + rep, there))
        return lax.ppermute(x, AXES[1:], pairs)

    def to_slot(x, slot):
        return cube_swap(x, lambda core: CHIPS[slot ^ core if slot < 6 else slot])

    def to_next(x, slot):
        d_low, d_rep = NEXT[slot]
        return cube_swap(x, lambda core: (d_low ^ (3 * core), d_rep ^ core))

    def to_corner(x):
        return cube_swap(x, lambda core: (3, 1))

    def per_device(acts, grad_logits, master, moment_one, moment_two, step_count):
        tokens, experts = grad_logits.shape
        rows = master.shape[0]
        half = rows // n_rep
        high, low, core, rep = position()
        f32, bf16 = jnp.float32, jnp.bfloat16
        in_kernels = half % 16 == 0 and (4 * half) % 128 == 0

        vmem = pl.BlockSpec(memory_space=pltpu.VMEM)
        anywhere = pl.BlockSpec(memory_space=pl.ANY)
        params = pltpu.CompilerParams(vmem_limit_bytes=VMEM_LIMIT)
        state_in = (master, moment_one, moment_two)

        if in_kernels:
            acts = pltpu.with_memory_space_constraint(acts, pltpu.HBM)
            shape = pltpu.VMEM((4, n_high, half, experts), bf16)
            columns_shape = pltpu.VMEM((2 * n_high, tokens, 4 * half), bf16)
            blocks = pltpu.VMEM((2, 2, half, experts), bf16)
            turned = pltpu.VMEM((experts, tokens), bf16)
            pair = pltpu.VMEM((2, n_high, half, experts), bf16)
            *sorted_rows, mine, later, turned = pl.pallas_call(
                functools.partial(first_grad_kernel, n_high),
                out_shape=[pair] * 4 + [pltpu.VMEM((3, half, experts), f32), columns_shape, turned],
                in_specs=[anywhere] * 5,
                out_specs=[vmem] * 7,
                scratch_shapes=[
                    columns_shape,
                    pltpu.VMEM((tokens, experts), bf16),
                    blocks,
                    pltpu.SemaphoreType.DMA((3, max(2 * n_high, 4))),
                ],
                compiler_params=params,
            )(
                acts,
                *(pltpu.with_memory_space_constraint(x, pltpu.HBM) for x in (grad_logits, *state_in)),
            )
            away_first, kept_first = pl.pallas_call(
                functools.partial(second_grad_kernel, n_high),
                out_shape=[shape, shape],
                in_specs=[vmem, vmem],
                out_specs=[vmem] * 2,
                scratch_shapes=[blocks],
                cost_estimate=pl.CostEstimate(
                    flops=4 * n_high * tokens * experts * 4 * half,
                    bytes_accessed=4 * n_high * tokens * 4 * half,
                    transcendentals=0,
                ),
                compiler_params=params,
            )(*(pltpu.with_memory_space_constraint(x, pltpu.VMEM) for x in (later, turned)))
            away, kept = (*sorted_rows[:2], away_first), (*sorted_rows[2:], kept_first)
        else:
            product = lax.dot_general(
                acts, grad_logits, (((0,), (0,)), ((), ())), preferred_element_type=f32
            ).astype(bf16)
            product = product.reshape(n_high, N_LOW, 2, n_rep, half, experts)
            product = product[high ^ jnp.arange(n_high)]

            def sort_rows(owner):
                blocks = []
                for slot in range(8):
                    flip = owner if slot < 6 else 0
                    d_low, d_rep = CHIPS[slot]
                    at = (0, low ^ d_low ^ (3 * flip), owner, rep ^ d_rep ^ flip, 0, 0)
                    part = lax.dynamic_slice(product, at, (n_high, 1, 1, 1, half, experts))
                    blocks.append(part.reshape(n_high, half, experts))
                return jnp.stack(blocks[4:6]), jnp.stack(blocks[6:]), jnp.stack(blocks[:4])

            away, kept = sort_rows(1 - core), sort_rows(core)
            mine = jnp.stack([lax.dynamic_slice_in_dim(x, rep * half, half, 0) for x in state_in])

        arrived = swap(away[1], "core")
        arrived, *rest = lax.optimization_barrier((arrived, away[0], away[2]))
        arrived = [swap(rest[0], "core"), arrived, swap(rest[1], "core")]
        pair, left, first = [own.astype(f32) + x.astype(f32) for own, x in zip(kept, arrived)]
        corner = cube_swap(left[0].astype(bf16), lambda core: (1 - core, core)).astype(f32)
        sums = [first[0], first[2], first[3], pair[1]]
        parts = [to_slot(x.astype(bf16), slot) for x, slot in zip(sums, (0, 2, 3, 5))]
        for part, slot, of_core in ((pair[0], 4, 1), (first[1], 1, 0)):
            parts.append(to_slot((part + jnp.where(core == of_core, corner, 0.0)).astype(bf16), slot))
        parts = [left[1], *lax.optimization_barrier(parts)]
        total = sum(x.astype(f32) for x in parts)

        grad = total[0]
        for j in range(1, n_high):
            grad = grad + swap(total[j].astype(bf16), "high", j).astype(f32)
        weight = adamw(grad, *mine, step_count)[0].astype(bf16)

        column = jnp.stack([swap(weight, "high", j) if j else weight for j in range(n_high)])
        other = swap(grad, "rep")
        across = swap(column, "core")
        across, other = lax.optimization_barrier((across, other))
        corner = to_corner(column)
        chip = jnp.where(core == 0, jnp.stack([column, across]), jnp.stack([across, column]))
        got = [to_next(chip, slot) for slot in range(3)]

        whole = jnp.where(
            rep == 0,
            jnp.concatenate([grad, other], 0),
            jnp.concatenate([other, grad], 0),
        )
        state = adamw(whole, *state_in, step_count)

        columns = [None, None]
        if in_kernels:
            state, late_acts = lax.optimization_barrier((state, acts))
            columns = pl.pallas_call(
                functools.partial(columns_kernel, n_high, 4 * half),
                out_shape=(pltpu.VMEM((tokens, 8 * n_high * half), bf16),) * 2,
                in_specs=[anywhere],
                out_specs=(vmem, vmem),
                scratch_shapes=[pltpu.SemaphoreType.DMA((2, 2 * n_high))],
                compiler_params=params,
            )(pltpu.with_memory_space_constraint(late_acts, pltpu.HBM))
        got[0], corner, state, columns = lax.optimization_barrier((got[0], corner, state, columns))
        first, second = jnp.concatenate(got[:2]), jnp.concatenate([got[2], corner[None]])
        first, second = [first, swap(first, "core")], [second, swap(second, "core")]
        second += [column[None], across[None]]
        pieces = (first, second)
        logits = None
        for group, (received, acts_columns) in enumerate(zip(pieces, columns)):
            if in_kernels:
                before = [] if logits is None else [logits]
                operands = [
                    pltpu.with_memory_space_constraint(x, pltpu.VMEM) for x in [acts_columns] + received + before
                ]
                logits = pl.pallas_call(
                    functools.partial(logits_kernel, n_high, group),
                    out_shape=jax.ShapeDtypeStruct((tokens, experts), bf16 if before else f32),
                    in_specs=[vmem] * len(operands),
                    out_specs=vmem,
                    scratch_shapes=[pltpu.VMEM((2, n_high, 2, 2, half, experts), bf16)],
                    compiler_params=params,
                )(*operands)
            else:
                rows_at, values = [], []
                for piece, blocks in zip(received, places(group, core, rep)):
                    for n, (place, owner, of_rep) in enumerate(blocks):
                        d_low = jnp.array(LOWS[group])[place]
                        for j in range(n_high):
                            at = ((high ^ j) * N_LOW + (low ^ d_low)) * 2 + owner
                            rows_at.append(at * n_rep + of_rep)
                            values.append(piece[n, j])
                full = jnp.zeros((2 * n_seq, half, experts), bf16)
                full = full.at[jnp.stack(rows_at)].set(jnp.stack(values))
                full = full.reshape(n_seq * rows, experts)
                part = jnp.dot(acts, full, preferred_element_type=f32)
                logits = part if logits is None else (logits + part).astype(bf16)
        return *state, logits

    rows_of, tokens_of = P(AXES[:3], None), P(AXES, None)
    return jax.shard_map(
        per_device,
        mesh=fine,
        in_specs=(tokens_of, tokens_of, rows_of, rows_of, rows_of, P()),
        out_specs=(rows_of, rows_of, rows_of, tokens_of),
        check_vma=False,
    )
```
